512 devices in a mesh: client: 32 (over x, y, core), dp: 16 (over z).
Axes of the slice: x: 4, y: 4, z: 16, core: 2. Of those that a mesh axis runs over, the one named last changes fastest.
Arguments:
- hidden: bfloat16 [32, 2048, 14336], P('client', 'dp'), may hold values from -6 to 6
- frozen_residual: bfloat16 [32, 2048, 64], P('client', 'dp'), may hold values from -6 to 6
- head: bfloat16 [32, 64, 4096], P('client'), may hold values from -0.09375 to 0.09375
- global_input_factor: bfloat16 [16, 14336], replicated, may hold values from -0.046875 to 0.046875
- global_output_factor: bfloat16 [16, 4096], replicated, may hold values from -0.119628906 to 0.119628906
- counts: int32 [32, 16], P('client', 'dp'), may hold values from 32 to 128, as said below
- weights: int32 [32], P('client'), may hold values from 1 to 8
- input_privacy_noise: float32 [16, 14336], P(None, 'dp'), may hold values from -6 to 6
- output_privacy_noise: float32 [16, 4096], P(None, 'dp'), may hold values from -6 to 6
Outputs:
- update_in: float32 [16, 14336], P(None, 'dp')
- update_out: float32 [16, 4096], P(None, 'dp')
The draws below stay inside these ranges and needn't reach their ends.
Inputs may be any that keep to these rules, and one draw needn't show every extreme that they name: `counts`: the live tokens of a device are its first rows; in every client some device has all 128 slots live.
All inputs are finite; a program needn't handle non-finite values.
Results may differ from the reference program's by a relative error of at most 0.0011.
Values sent between devices are 32-bit elements; how exact they have to be, the bound alone decides.
A program may use at most 64 MiB of HBM per device.

```python
import math
import jax
import jax.numpy as jnp
from jax import lax

MODEL_WIDTH = 4096
HIDDEN_UNITS = 14336
ADAPTER_RANK = 16
NOUT = 64
ITERS = 3
TOK_DEV = 128
CLIENTS = 32
SHARDS = 16
CTOK = 2048


def draw_counts(key, part):
    key = jax.random.fold_in(key, 11)
    first, second, third, fourth = jax.random.split(key, 4)
    lowest = max(1, TOK_DEV // 4)
    drawn = jax.random.randint(first, (CLIENTS, SHARDS), lowest, TOK_DEV + 1, dtype=jnp.int32)
    chosen = jax.random.randint(second, (CLIENTS, 1), 0, SHARDS, dtype=jnp.int32)
    offset = jax.random.randint(third, (CLIENTS, 1), 1, SHARDS, dtype=jnp.int32)
    low_client = jax.random.randint(fourth, (), 0, CLIENTS, dtype=jnp.int32)
    column = lax.broadcasted_iota(jnp.int32, (CLIENTS, SHARDS), 1)
    row_index = lax.broadcasted_iota(jnp.int32, (CLIENTS, SHARDS), 0)
    low_column = (chosen + offset) % SHARDS
    filled = jnp.where(column == chosen, jnp.int32(TOK_DEV), drawn)
    return jnp.where((row_index == low_client) & (column == low_column), jnp.int32(lowest), filled)


def place_ends(entries, stream_key, least, top_value):
    dims = entries.shape
    place = [jax.random.randint(jax.random.fold_in(stream_key, axis), (), 0, dims[axis]) for axis in range(len(dims))]
    entries = entries.at[tuple(place)].set(least)
    longest = dims.index(max(dims))
    place[longest] = (place[longest] + 1) % dims[longest]
    return entries.at[tuple(place)].set(top_value)


def block_scale(stream_key, extent, cuts, least, top_value):
    loudness, own = 1.0, jax.random.fold_in(stream_key, 6)
    for axis_at, shards_of in cuts:
        draws = jnp.exp(jax.random.uniform(jax.random.fold_in(own, axis_at), (shards_of,), jnp.float32, least / len(cuts), top_value / len(cuts)))
        loudness = loudness * jnp.repeat(draws, extent[axis_at] // shards_of).reshape([-1 if axis == axis_at else 1 for axis in range(len(extent))])
    return loudness


def normal_values(stream_key, extent, spread, reach, shards=(), kind=jnp.bfloat16):
    values = spread * jax.random.normal(stream_key, extent, jnp.float32)
    if shards:
        values = values * block_scale(stream_key, extent, shards, -0.22, 0.18)
    return jnp.clip(values, -reach, reach).astype(kind)


def setup_inputs(seed: int = 0) -> dict:
    seeds = jax.random.split(jax.random.key(seed), 10)
    hidden = normal_values(seeds[0], (CLIENTS, CTOK, HIDDEN_UNITS), 1.0, 6.0, ((0, 32), (1, 16)))
    frozen_residual = normal_values(seeds[1], (CLIENTS, CTOK, NOUT), 1.0, 6.0, ((0, 32), (1, 16)))
    head = normal_values(seeds[2], (CLIENTS, NOUT, MODEL_WIDTH), MODEL_WIDTH ** -0.5, 0.09375, ((0, 32),))
    global_input_factor = normal_values(seeds[3], (ADAPTER_RANK, HIDDEN_UNITS), HIDDEN_UNITS ** -0.5, 0.046875)
    global_output_factor = normal_values(seeds[4], (ADAPTER_RANK, MODEL_WIDTH), 0.02, 0.119628906)
    counts = draw_counts(jax.random.fold_in(seeds[9], 71), 0)
    weights = place_ends(jax.random.randint(seeds[6], (CLIENTS,), 1, 9), jax.random.fold_in(seeds[6], 1), 1, 8).astype(jnp.int32)
    input_privacy_noise = normal_values(seeds[7], (ADAPTER_RANK, HIDDEN_UNITS), 1.0, 6.0, ((1, 16),), jnp.float32)
    output_privacy_noise = normal_values(seeds[8], (ADAPTER_RANK, MODEL_WIDTH), 1.0, 6.0, ((1, 16),), jnp.float32)
    return dict(hidden=hidden, frozen_residual=frozen_residual, head=head, global_input_factor=global_input_factor, global_output_factor=global_output_factor, counts=counts, weights=weights, input_privacy_noise=input_privacy_noise, output_privacy_noise=output_privacy_noise)


learn_rate = 0.1
clip_bound = 0.001
noise_mult = 0.1

def client_adapter_step(client_rows, baseline_residual, client_head_rows, active_rows, global_input_factor, global_output_factor):
    slots = client_rows.shape[0]
    index = lax.iota(jnp.int32, slots)
    limit = active_rows[index // TOK_DEV]
    mask = (index % TOK_DEV < limit).astype(jnp.float32)[:, None]
    total = jnp.sum(active_rows.astype(jnp.float32))
    resid_zero = baseline_residual.astype(jnp.float32)
    head_wide = client_head_rows.astype(jnp.float32)
    initial_input_factor = global_input_factor.astype(jnp.float32)
    initial_output_factor = global_output_factor.astype(jnp.float32)
    adapt_in, adapt_out = (initial_input_factor, initial_output_factor)
    high = lax.Precision.HIGHEST
    for step in range(ITERS):
        proj = lax.dot_general(client_rows, adapt_in.astype(jnp.bfloat16), (((1,), (1,)), ((), ())), preferred_element_type=jnp.float32)
        mixed = jnp.dot(adapt_out, head_wide.T, precision=high)
        resid = resid_zero + jnp.dot(proj, mixed, precision=high)
        dres = resid * mask / total
        dproj = jnp.dot(dres, mixed.T, precision=high).astype(jnp.bfloat16)
        grad_in = lax.dot_general(dproj, client_rows, (((0,), (0,)), ((), ())), preferred_element_type=jnp.float32)
        grad_out = jnp.dot(jnp.dot(proj.T, dres, precision=high), head_wide, precision=high)
        adapt_in = adapt_in - learn_rate * grad_in
        adapt_out = adapt_out - learn_rate * grad_out
    input_factor_change = adapt_in - initial_input_factor
    output_factor_change = adapt_out - initial_output_factor
    squares = jnp.sum(input_factor_change * input_factor_change) + jnp.sum(output_factor_change * output_factor_change)
    factor_matrix = jnp.minimum(1.0, clip_bound / jnp.sqrt(squares + 1e-06))
    return (input_factor_change, output_factor_change, factor_matrix)

def reference(hidden, frozen_residual, head, global_input_factor, global_output_factor, counts, weights, input_privacy_noise, output_privacy_noise):

    def one_client(items):
        client_rows, baseline_residual, client_head_rows, active_rows, weight = items
        input_factor_change, output_factor_change, factor_matrix = client_adapter_step(client_rows, baseline_residual, client_head_rows, active_rows, global_input_factor, global_output_factor)
        scale = weight.astype(jnp.float32) * factor_matrix
        return (scale * input_factor_change, scale * output_factor_change)
    scaled_in, scaled_out = lax.map(one_client, (hidden, frozen_residual, head, counts, weights))
    agg_in = lax.optimization_barrier(jnp.sum(scaled_in, axis=0))
    agg_out = lax.optimization_barrier(jnp.sum(scaled_out, axis=0))
    wsum = jnp.sum(weights.astype(jnp.float32))
    out_scale = math.sqrt(ADAPTER_RANK * (HIDDEN_UNITS + MODEL_WIDTH)) / clip_bound
    update_in = (agg_in + noise_mult * clip_bound * input_privacy_noise) * out_scale / wsum
    update_out = (agg_out + noise_mult * clip_bound * output_privacy_noise) * out_scale / wsum
    return (update_in, update_out)
```

```python
import functools
import math

import jax
import jax.numpy as jnp
from jax import lax
from jax.experimental import pallas as pl
from jax.experimental.pallas import tpu as pltpu
from jax.sharding import PartitionSpec as P

ITERS = 3
CORES = 2

learn_rate = 0.1
clip_bound = 0.001
noise_mult = 0.1

MESH = pl.DeviceIdType.MESH
HIGH = lax.Precision.HIGHEST
NN = (((1,), (0,)), ((), ()))
NT = (((1,), (1,)), ((), ()))
TN = (((0,), (0,)), ((), ()))


def mm(a, b, dims=NN, precision=None):
    return lax.dot_general(
        a, b, dims, precision=precision, preferred_element_type=jnp.float32
    )


def kernel(
    n,
    clients,
    out_scale,
    hid_ref,
    res_ref,
    head_ref,
    a0_ref,
    b0_ref,
    cnt_ref,
    w_ref,
    nin_ref,
    nout_ref,
    oin_ref,
    oout_ref,
    hv,
    grad,
    slot,
    a_all,
    own,
    part,
    spread,
    row_out,
    row_in,
    pair,
    row_done,
    hid_sem,
    rs_send,
    rs_recv,
    ag_send,
    ag_recv,
    pt_send,
    pt_recv,
    sc_send,
    sc_recv,
    ro_send,
    ro_recv,
    pr_send,
    pr_recv,
    rd_send,
    rd_recv,
):
    half_n = n // 2
    chips = clients // CORES
    rank, width_in = nin_ref.shape
    width_out = nout_ref.shape[1]
    half = rank // 2
    nout = head_ref.shape[0]
    tokens = hv.shape[1]
    width = width_in + width_out

    z = lax.axis_index("dp")
    client = lax.axis_index("client")
    chip = lax.div(client, CORES)
    core = lax.rem(client, CORES)
    twin = chip * CORES + (1 - core)
    ring = (lax.rem(z + n - 1, n), lax.rem(z + 1, n))

    def at_z(k):
        return lax.rem(z + k, n)

    def at_chip(k):
        return lax.rem(chip + k, chips)

    barrier = pltpu.get_barrier_semaphore()
    for k in range(1, n):
        pl.semaphore_signal(barrier, inc=1, device_id={"dp": at_z(k)}, device_id_type=MESH)
    for k in range(1, chips):
        pl.semaphore_signal(
            barrier, inc=1, device_id={"client": at_chip(k) * CORES + core}, device_id_type=MESH
        )
    pl.semaphore_signal(barrier, inc=1, device_id={"client": twin}, device_id_type=MESH)

    def load(j):
        return pltpu.make_async_copy(
            hid_ref.at[0, :, pl.ds(j * width_in, width_in)], hv.at[j], hid_sem.at[j]
        )

    for j in range(n):
        load(j).start()

    head = head_ref[...]
    gram = mm(head, head, NT)
    mixed = mm(b0_ref[...], head, NT)
    mixed_t = mm(head, b0_ref[...], NT)
    base_t = res_ref[...].astype(jnp.float32).T
    lane = lax.broadcasted_iota(jnp.int32, (1, tokens), 1)
    live = cnt_ref[0, 0]
    mask = (lane < live).astype(jnp.float32)

    pl.semaphore_wait(barrier, (n - 1) + (chips - 1) + 1)

    def z_copy(which, k):
        return pltpu.make_async_remote_copy(
            src_ref=spread.at[which, z],
            dst_ref=spread.at[which, z],
            send_sem=sc_send.at[which, k],
            recv_sem=sc_recv.at[which, k],
            device_id={"dp": at_z(k)},
            device_id_type=MESH,
        )

    def z_start(which, row):
        spread[which, z] = row
        for k in range(1, n):
            z_copy(which, k).start()

    def z_finish(which):
        for k in range(1, n):
            z_copy(which, k).wait()
        total = spread[which, 0]
        for j in range(1, n):
            total = total + spread[which, j]
        return total

    z_start(0, jnp.full((1, 128), live.astype(jnp.float32), jnp.float32))

    proj = jnp.zeros((rank, tokens), jnp.float32)
    for j in range(n):
        load(j).wait()
        proj = proj + mm(a0_ref[:, j * width_in : (j + 1) * width_in], hv[j], NT)

    tokens_live = z_finish(0)[:, :1]

    start_cols = pl.ds(pl.multiple_of(z * width_in, 128), width_in)
    own_zero = a0_ref[:, start_cols].astype(jnp.float32)
    for h in range(2):
        own[h] = own_zero[h * half : (h + 1) * half]

    def rs_copy(it, way, h, s, owner):
        return pltpu.make_async_remote_copy(
            src_ref=grad.at[it, owner, h],
            dst_ref=slot.at[it, way, h, s],
            send_sem=rs_send.at[it, way, h, s],
            recv_sem=rs_recv.at[it, way, h, s],
            device_id={"dp": ring[way]},
            device_id_type=MESH,
        )

    def ag_copy(it, way, h, t, owner):
        return pltpu.make_async_remote_copy(
            src_ref=a_all.at[it, owner, h],
            dst_ref=a_all.at[it, owner, h],
            send_sem=ag_send.at[it, way, h, t],
            recv_sem=ag_recv.at[it, way, h, t],
            device_id={"dp": ring[way]},
            device_id_type=MESH,
        )

    def pt_copy(it, way, t, owner):
        return pltpu.make_async_remote_copy(
            src_ref=part.at[it, owner],
            dst_ref=part.at[it, owner],
            send_sem=pt_send.at[it, way, t],
            recv_sem=pt_recv.at[it, way, t],
            device_id={"dp": ring[way]},
            device_id_type=MESH,
        )

    def long(way, h):
        return way == h

    inner_sum = jnp.zeros((rank, nout), jnp.float32)
    for it in range(ITERS):
        last = it == ITERS - 1
        resid = base_t + mm(mixed_t, proj, NN, HIGH)
        dres = resid * mask / tokens_live
        dproj = mm(mixed, dres, NN, HIGH).astype(jnp.bfloat16)

        def local(owner):
            value = mm(dproj, hv[owner])
            for h in range(2):
                grad[it, owner, h] = value[h * half : (h + 1) * half]

        far = at_z(half_n)
        local(far)
        for way in range(2):
            rs_copy(it, way, way, 0, far).start()

        inner = mm(proj, dres, NT, HIGH)
        part[it, z] = jnp.concatenate([inner[:half], inner[half:]], axis=1)
        for way in range(2):
            pt_copy(it, way, 0, z).start()

        for s in range(1, half_n):
            k = half_n - s
            owners = (at_z(n - k), at_z(k))
            for way in range(2):
                local(owners[way])
            for h in range(2):
                for way in range(2):
                    if s > 1 or long(way, h):
                        rs_copy(it, way, h, s - 1, owners[way]).wait_recv()
                        grad[it, owners[way], h] += slot[it, way, h, s - 1]
                    rs_copy(it, way, h, s, owners[way]).start()
            for way in range(2):
                source = at_z(s) if way == 0 else at_z(n - s)
                pt_copy(it, way, s - 1, source).wait_recv()
                if s < half_n - 1 or way == 0:
                    pt_copy(it, way, s, source).start()
        local(z)
        for h in range(2):
            for way in range(2):
                rs_copy(it, way, h, half_n - 1, z).wait_recv()
            total = grad[it, z, h] + (slot[it, 0, h, half_n - 1] + slot[it, 1, h, half_n - 1])
            own[h] = own[h] - learn_rate * total
            if not last:
                a_all[it, z, h] = own[h]
                for way in range(2):
                    ag_copy(it, way, h, 0, z).start()
        pt_copy(it, 0, half_n - 1, far).wait_recv()
        tile = part[it, 0]
        for j in range(1, n):
            tile = tile + part[it, j]
        step_inner = jnp.concatenate([tile[:, :nout], tile[:, nout:]], axis=0)
        inner_sum = inner_sum + step_inner

        if not last:
            mixed = mixed - learn_rate * mm(step_inner, gram, NN, HIGH)
            mixed_t = mixed_t - learn_rate * mm(gram, step_inner, NT, HIGH)

            def project(owner):
                rows = jnp.concatenate([a_all[it, owner, 0], a_all[it, owner, 1]], axis=0)
                return mm(rows.astype(jnp.bfloat16), hv[owner], NT)

            proj = project(z)
            for t in range(1, half_n):
                sources = (at_z(t), at_z(n - t))
                for h in range(2):
                    for way in range(2):
                        ag_copy(it, way, h, t - 1, sources[way]).wait_recv()
                        if t < half_n - 1 or long(way, h):
                            ag_copy(it, way, h, t, sources[way]).start()
                for way in range(2):
                    proj = proj + project(sources[way])
            for way in range(2):
                ag_copy(it, way, way, half_n - 1, far).wait_recv()
            proj = proj + project(far)

    own_three = jnp.concatenate([own[0], own[1]], axis=0)
    delta_in = own_three - own_zero
    out_cols = pl.ds(pl.multiple_of(z * width_out, 128), width_out)
    head_cols = head_ref[:, out_cols].astype(jnp.float32)
    delta_out = -learn_rate * mm(inner_sum, head_cols, NN, HIGH)
    delta = jnp.concatenate([delta_in, delta_out], axis=1)
    sums = jnp.sum(delta * delta, axis=0, keepdims=True)
    lanes = sums[:, :128]
    for j in range(1, width // 128):
        lanes = lanes + sums[:, j * 128 : (j + 1) * 128]
    z_start(1, lanes)
    squares = jnp.sum(z_finish(1), axis=1, keepdims=True)
    factor = jnp.minimum(1.0, clip_bound / jnp.sqrt(squares + 1e-06))
    weight = w_ref[0].astype(jnp.float32)
    scaled = delta * (factor * weight)

    weight_row = jnp.full((1, 128), weight, jnp.float32)
    for r in range(rank):
        row_out[r] = jnp.concatenate([scaled[r : r + 1], weight_row], axis=1)

    def ro_copy(k):
        return pltpu.make_async_remote_copy(
            src_ref=row_out.at[at_chip(k)],
            dst_ref=row_in.at[chip],
            send_sem=ro_send.at[k],
            recv_sem=ro_recv.at[k],
            device_id={"client": at_chip(k) * CORES + core},
            device_id_type=MESH,
        )

    for k in range(1, chips):
        ro_copy(k).start()
    row_in[chip] = row_out[chip]
    for k in range(1, chips):
        ro_copy(k).wait()
    row = row_in[0]
    for j in range(1, chips):
        row = row + row_in[j]
    pair[0] = row
    pr_copy = pltpu.make_async_remote_copy(
        src_ref=pair.at[0],
        dst_ref=pair.at[1],
        send_sem=pr_send,
        recv_sem=pr_recv,
        device_id={"client": twin},
        device_id_type=MESH,
    )
    pr_copy.start()
    noise = jnp.concatenate(
        [nin_ref[pl.ds(chip, 1), :], nout_ref[pl.ds(chip, 1), :]], axis=1
    )
    pr_copy.wait()
    row = pair[0] + pair[1]
    wsum = row[:, width : width + 1]
    row_done[chip] = (row[:, :width] + noise_mult * clip_bound * noise) * out_scale / wsum

    def rd_copy(k):
        return pltpu.make_async_remote_copy(
            src_ref=row_done.at[chip],
            dst_ref=row_done.at[chip],
            send_sem=rd_send.at[k],
            recv_sem=rd_recv.at[k],
            device_id={"client": at_chip(k) * CORES + core},
            device_id_type=MESH,
        )

    for k in range(1, chips):
        rd_copy(k).start()

    for it in range(ITERS):
        for s in range(half_n):
            for way in range(2):
                for h in range(2):
                    if s > 0 or long(way, h):
                        rs_copy(it, way, h, s, z).wait_send()
                    if it < ITERS - 1 and (s < half_n - 1 or long(way, h)):
                        ag_copy(it, way, h, s, z).wait_send()
                if s < half_n - 1 or way == 0:
                    pt_copy(it, way, s, z).wait_send()

    for k in range(1, chips):
        rd_copy(k).wait()
    for r in range(rank):
        row = row_done[r]
        oin_ref[r : r + 1, :] = row[:, :width_in]
        oout_ref[r : r + 1, :] = row[:, width_in:]


def on_device(
    n,
    clients,
    hidden,
    frozen_residual,
    head,
    global_input_factor,
    global_output_factor,
    counts,
    weights,
    input_privacy_noise,
    output_privacy_noise,
):
    tokens, hidden_units = hidden.shape[1:]
    rank, model_width = global_output_factor.shape
    width_in = input_privacy_noise.shape[1]
    width_out = output_privacy_noise.shape[1]
    half = rank // 2
    half_n = n // 2
    chips = clients // CORES
    width = width_in + width_out
    out_scale = math.sqrt(rank * (hidden_units + model_width)) / clip_bound
    f32 = jnp.float32
    dma = pltpu.SemaphoreType.DMA
    vmem = pl.BlockSpec(memory_space=pltpu.VMEM)
    smem = pl.BlockSpec(memory_space=pltpu.SMEM)
    return pl.pallas_call(
        functools.partial(kernel, n, clients, out_scale),
        out_shape=(
            jax.ShapeDtypeStruct((rank, width_in), f32),
            jax.ShapeDtypeStruct((rank, width_out), f32),
        ),
        in_specs=[
            pl.BlockSpec(memory_space=pl.ANY), vmem, vmem, vmem, vmem, smem, smem, vmem, vmem
        ],
        out_specs=(vmem, vmem),
        scratch_shapes=[
            pltpu.VMEM((n, tokens, width_in), jnp.bfloat16),
            pltpu.VMEM((ITERS, n, 2, half, width_in), f32),
            pltpu.VMEM((ITERS, 2, 2, half_n, half, width_in), f32),
            pltpu.VMEM((ITERS - 1, n, 2, half, width_in), f32),
            pltpu.VMEM((2, half, width_in), f32),
            pltpu.VMEM((ITERS, n, half, 128), f32),
            pltpu.VMEM((2, n, 1, 128), f32),
            pltpu.VMEM((rank, 1, width + 128), f32),
            pltpu.VMEM((chips, 1, width + 128), f32),
            pltpu.VMEM((2, 1, width + 128), f32),
            pltpu.VMEM((rank, 1, width), f32),
            dma((n,)),
            dma((ITERS, 2, 2, half_n)),
            dma((ITERS, 2, 2, half_n)),
            dma((ITERS - 1, 2, 2, half_n)),
            dma((ITERS - 1, 2, 2, half_n)),
            dma((ITERS, 2, half_n)),
            dma((ITERS, 2, half_n)),
            dma((2, n)),
            dma((2, n)),
            dma((chips,)),
            dma((chips,)),
            dma,
            dma,
            dma((chips,)),
            dma((chips,)),
        ],
        compiler_params=pltpu.CompilerParams(
            collective_id=0, has_side_effects=True, vmem_limit_bytes=48 * 1024 * 1024
        ),
    )(
        hidden,
        frozen_residual[0],
        head[0],
        global_input_factor,
        global_output_factor,
        counts,
        weights,
        input_privacy_noise,
        output_privacy_noise,
    )


def solution(mesh):
    in_specs = (
        P("client", "dp", None),
        P("client", "dp", None),
        P("client", None, None),
        P(),
        P(),
        P("client", "dp"),
        P("client"),
        P(None, "dp"),
        P(None, "dp"),
    )
    out_specs = (P(None, "dp"), P(None, "dp"))
    body = functools.partial(on_device, mesh.shape["dp"], mesh.shape["client"])
    return jax.shard_map(
        body, mesh=mesh, in_specs=in_specs, out_specs=out_specs, check_vma=False
    )
```

```python
import functools
import math

import jax
import jax.numpy as jnp
from jax import lax
from jax.experimental import pallas as pl
from jax.experimental.pallas import tpu as pltpu
from jax.sharding import PartitionSpec as P

ITERS = 3
CORES = 2

learn_rate = 0.1
clip_bound = 0.001
noise_mult = 0.1

MESH = pl.DeviceIdType.MESH
HIGH = lax.Precision.HIGHEST
NN = (((1,), (0,)), ((), ()))
NT = (((1,), (1,)), ((), ()))
TN = (((0,), (0,)), ((), ()))


def mm(a, b, dims=NN, precision=None):
    return lax.dot_general(
        a, b, dims, precision=precision, preferred_element_type=jnp.float32
    )


def kernel(
    n,
    clients,
    out_scale,
    hid_ref,
    res_hbm,
    head_hbm,
    a0_hbm,
    b0_hbm,
    cnt_ref,
    w_ref,
    nin_hbm,
    nout_hbm,
    oin_ref,
    oout_ref,
    res_ref,
    head_ref,
    a0_ref,
    b0_ref,
    nin_ref,
    nout_ref,
    hv,
    gram,
    mixed,
    mixed_t,
    inner_sum,
    mask,
    tokens_live,
    proj,
    dproj,
    square,
    base_in,
    grad,
    slot,
    a_all,
    own,
    part,
    spread,
    row_out,
    row_in,
    row_done,
    op_sem,
    hid_sem,
    rs_send,
    rs_recv,
    ag_send,
    ag_recv,
    pt_send,
    pt_recv,
    sc_send,
    sc_recv,
    ro_send,
    ro_recv,
    rd_send,
    rd_recv,
):
    half_n = n // 2
    stops = half_n // 2
    chips = clients // CORES
    rank, width_in = nin_ref.shape
    width_out = nout_ref.shape[1]
    half = rank // 2
    nout = head_ref.shape[0]
    tokens = hv.shape[1]
    width = width_in + width_out

    z = lax.axis_index("dp")
    client = lax.axis_index("client")
    chip = lax.div(client, CORES)
    core = lax.rem(client, CORES)
    ring = (
        (lax.rem(z + n - 2, n), lax.rem(z + 2, n)),
        (lax.rem(z + n - 1, n), lax.rem(z + 1, n)),
    )

    def at_z(k):
        return lax.rem(z + k, n)

    def at_chip(k):
        return lax.rem(chip + k, chips)

    def load(j):
        return pltpu.make_async_copy(
            hid_ref.at[0, :, pl.ds(j * width_in, width_in)], hv.at[j], hid_sem.at[j]
        )

    pieces = [
        pltpu.make_async_copy(src, dst, op_sem.at[i])
        for i, (src, dst) in enumerate(
            [
                (head_hbm, head_ref),
                (b0_hbm, b0_ref),
                (res_hbm, res_ref),
                (a0_hbm, a0_ref),
                (nin_hbm, nin_ref),
                (nout_hbm, nout_ref),
            ]
        )
    ]
    for piece in pieces[:4]:
        piece.start()
    for j in range(n):
        load(j).start()
    for piece in pieces[4:]:
        piece.start()

    barrier = pltpu.get_barrier_semaphore()
    for k in range(1, n):
        pl.semaphore_signal(barrier, inc=1, device_id={"dp": at_z(k)}, device_id_type=MESH)
    for k in range(1, clients):
        pl.semaphore_signal(
            barrier, inc=1, device_id={"client": lax.rem(client + k, clients)}, device_id_type=MESH
        )

    for piece in pieces[:3]:
        piece.wait()
    head = head_ref[...]
    gram[...] = mm(head, head, NT)
    mixed[...] = mm(b0_ref[...], head, NT)
    mixed_t[...] = mm(head, b0_ref[...], NT)
    inner_sum[...] = jnp.zeros_like(inner_sum)

    def from_mixed():
        square[...] = mm(mixed[...], mixed[...], NT, HIGH)
        base_in[...] = mm(mixed[...], res_ref[...].astype(jnp.float32), NN, HIGH)

    from_mixed()
    lane = lax.broadcasted_iota(jnp.int32, (1, tokens), 1)
    live = cnt_ref[0, 0]

    pl.semaphore_wait(barrier, (n - 1) + (clients - 1))

    def z_copy(which, k):
        return pltpu.make_async_remote_copy(
            src_ref=spread.at[which, z],
            dst_ref=spread.at[which, z],
            send_sem=sc_send.at[which, k],
            recv_sem=sc_recv.at[which, k],
            device_id={"dp": at_z(k)},
            device_id_type=MESH,
        )

    def z_start(which, row):
        spread[which, z] = row
        for k in range(1, n):
            z_copy(which, k).start()

    def z_finish(which):
        for k in range(1, n):
            z_copy(which, k).wait()
        total = spread[which, 0]
        for j in range(1, n):
            total = total + spread[which, j]
        return total

    z_start(0, jnp.full((1, 128), live.astype(jnp.float32), jnp.float32))

    pieces[3].wait()
    proj[...] = jnp.zeros_like(proj)

    def first(j, _):
        load(j).wait()
        cols = pl.ds(pl.multiple_of(j * width_in, 128), width_in)
        proj[...] += mm(hv[j], a0_ref[:, cols], NT)
        return 0

    lax.fori_loop(0, n, first, 0)

    start_cols = pl.ds(pl.multiple_of(z * width_in, 128), width_in)
    own_zero = a0_ref[:, start_cols].astype(jnp.float32)
    for h in range(2):
        own[h] = own_zero[h * half : (h + 1) * half]
    mask[...] = (lane < live).astype(jnp.float32)
    tokens_live[...] = z_finish(0)

    def rs_copy(it, way, h, odd, e, owner):
        return pltpu.make_async_remote_copy(
            src_ref=grad.at[it, owner, h],
            dst_ref=slot.at[it, way, h, odd, e],
            send_sem=rs_send.at[it, way, h, odd, e],
            recv_sem=rs_recv.at[it, way, h, odd, e],
            device_id={"dp": ring[odd][way]},
            device_id_type=MESH,
        )

    def ag_copy(it, way, h, odd, t, owner):
        return pltpu.make_async_remote_copy(
            src_ref=a_all.at[it, owner, h],
            dst_ref=a_all.at[it, owner, h],
            send_sem=ag_send.at[it, way, h, odd, t],
            recv_sem=ag_recv.at[it, way, h, odd, t],
            device_id={"dp": ring[odd][way]},
            device_id_type=MESH,
        )

    def pt_copy(it, way, odd, t, owner):
        return pltpu.make_async_remote_copy(
            src_ref=part.at[it, owner],
            dst_ref=part.at[it, owner],
            send_sem=pt_send.at[it, way, odd, t],
            recv_sem=pt_recv.at[it, way, odd, t],
            device_id={"dp": ring[odd][way]},
            device_id_type=MESH,
        )

    def long(way, h):
        return way == h

    far = at_z(half_n)

    def local_step(it, _):
        weighted = mask[...] / tokens_live[...]
        through = mm(square[...], proj[...], NT, HIGH)
        dproj[...] = ((base_in[...] + through) * weighted).astype(jnp.bfloat16)

        def local(owner):
            value = mm(dproj[...], hv[owner])
            for h in range(2):
                grad[it, owner, h] = value[h * half : (h + 1) * half]

        def beside(k):
            return at_z(n - k), at_z(k)

        def local_both(k):
            for owner in beside(k):
                local(owner)

        def send_odd(e):
            owners = beside(half_n - 1 - 2 * e)
            for h in range(2):
                for way in range(2):
                    rs_copy(it, way, h, 1, e, owners[way]).start()

        local(far)
        for way in range(2):
            rs_copy(it, way, way, 0, 0, far).start()
        local_both(half_n - 1)
        send_odd(0)
        local_both(half_n - 2)
        local_both(half_n - 3)
        send_odd(1)

        proj_t = proj[...].T
        resid = res_ref[...].astype(jnp.float32) + mm(mixed_t[...], proj_t, NN, HIGH)
        inner = mm(proj_t, resid * weighted, NT, HIGH)
        part[it, z] = jnp.concatenate([inner[:half], inner[half:]], axis=1)
        for odd in range(2):
            for way in range(2):
                pt_copy(it, way, odd, 0, z).start()

        for e in range(1, stops):
            owners = beside(half_n - 2 * e)
            for h in range(2):
                for way in range(2):
                    rs_copy(it, way, h, 1, e - 1, owners[way]).wait_recv()
                    total = grad[it, owners[way], h] + slot[it, way, h, 1, e - 1]
                    if long(way, h) or e > 1:
                        rs_copy(it, way, h, 0, e - 1, owners[way]).wait_recv()
                        total = total + slot[it, way, h, 0, e - 1]
                    grad[it, owners[way], h] = total
                    rs_copy(it, way, h, 0, e, owners[way]).start()
            if e < stops - 1:
                local_both(half_n - 2 * e - 2)
                local_both(half_n - 2 * e - 3)
                send_odd(e + 1)
            else:
                local(z)
            for way in range(2):
                source = at_z(2 * e) if way == 0 else at_z(n - 2 * e)
                pt_copy(it, way, 0, e - 1, source).wait_recv()
                if way == 0 or e < stops - 1:
                    pt_copy(it, way, 0, e, source).start()
                pt_copy(it, way, 1, e, source).start()
                pt_copy(it, way, 1, e - 1, source).wait_recv()
        for h in range(2):
            total = grad[it, z, h]
            for odd in (1, 0):
                for way in range(2):
                    rs_copy(it, way, h, odd, stops - 1, z).wait_recv()
                    total = total + slot[it, way, h, odd, stops - 1]
            own[h] = own[h] - learn_rate * total

            @pl.when(it < ITERS - 1)
            def _():
                a_all[it, z, h] = own[h]
                for way in range(2):
                    ag_copy(it, way, h, 0, 0, z).start()

        @pl.when(it < ITERS - 1)
        def _():
            for h in range(2):
                for way in range(2):
                    ag_copy(it, way, h, 1, 0, z).start()

        pt_copy(it, 0, 0, stops - 1, far).wait_recv()
        for way in range(2):
            pt_copy(it, way, 1, stops - 1, far).wait_recv()
        tile = part[it, 0]
        for j in range(1, n):
            tile = tile + part[it, j]
        step_inner = jnp.concatenate([tile[:, :nout], tile[:, nout:]], axis=0)
        inner_sum[...] += step_inner

        @pl.when(it < ITERS - 1)
        def _():
            mixed[...] = mixed[...] - learn_rate * mm(step_inner, gram[...], NN, HIGH)
            mixed_t[...] = mixed_t[...] - learn_rate * mm(gram[...], step_inner, NT, HIGH)
            from_mixed()

            def project(owner):
                rows = jnp.concatenate([a_all[it, owner, 0], a_all[it, owner, 1]], axis=0)
                return mm(hv[owner], rows.astype(jnp.bfloat16), NT)

            proj[...] = project(z)

            for t in range(1, stops):
                sources = (at_z(2 * t), at_z(n - 2 * t))
                between = (at_z(2 * t - 1), at_z(n - 2 * t + 1))
                for h in range(2):
                    for way in range(2):
                        ag_copy(it, way, h, 0, t - 1, sources[way]).wait_recv()
                        if long(way, h) or t < stops - 1:
                            ag_copy(it, way, h, 0, t, sources[way]).start()
                proj[...] += project(sources[0])
                for h in range(2):
                    for way in range(2):
                        ag_copy(it, way, h, 1, t, sources[way]).start()
                proj[...] += project(sources[1])
                for way in range(2):
                    for h in range(2):
                        ag_copy(it, way, h, 1, t - 1, between[way]).wait_recv()
                    proj[...] += project(between[way])
            between = (at_z(half_n - 1), at_z(n - half_n + 1))
            for way in range(2):
                for h in range(2):
                    ag_copy(it, way, h, 1, stops - 1, between[way]).wait_recv()
                proj[...] += project(between[way])
            for way in range(2):
                ag_copy(it, way, way, 0, stops - 1, far).wait_recv()
            proj[...] += project(far)

        return 0

    lax.fori_loop(0, ITERS, local_step, 0)

    own_three = jnp.concatenate([own[0], own[1]], axis=0)
    delta_in = own_three - own_zero
    out_cols = pl.ds(pl.multiple_of(z * width_out, 128), width_out)
    head_cols = head_ref[:, out_cols].astype(jnp.float32)
    delta_out = -learn_rate * mm(inner_sum[...], head_cols, NN, HIGH)
    delta = jnp.concatenate([delta_in, delta_out], axis=1)
    sums = jnp.sum(delta * delta, axis=0, keepdims=True)
    lanes = sums[:, :128]
    for j in range(1, width // 128):
        lanes = lanes + sums[:, j * 128 : (j + 1) * 128]
    squares = jnp.sum(lanes, axis=1, keepdims=True)
    weight = w_ref[0].astype(jnp.float32)

    mine = lax.broadcasted_iota(jnp.int32, (1, 128), 1) == client
    ends = jnp.concatenate(
        [jnp.where(mine, squares, 0.0), jnp.where(mine, weight, 0.0)], axis=1
    )
    for r in range(rank):
        row_out[r] = jnp.concatenate([delta[r : r + 1], ends], axis=1)

    def ro_copy(k, to_core, from_core):
        return pltpu.make_async_remote_copy(
            src_ref=row_out.at[at_chip(k)],
            dst_ref=row_in.at[client],
            send_sem=ro_send.at[k, to_core],
            recv_sem=ro_recv.at[k, from_core],
            device_id={"client": at_chip(k) * CORES + to_core},
            device_id_type=MESH,
        )

    for k in range(1, chips):
        for to_core in range(CORES):
            ro_copy(k, to_core, core).start()
    ro_copy(0, 1 - core, core).start()
    row_in[client] = row_out[chip]
    for k in range(1, chips):
        for from_core in range(CORES):
            ro_copy(k, from_core, from_core).wait_recv()
    ro_copy(0, 1 - core, 1 - core).wait_recv()
    ends = row_in[0][:, width:]
    for c in range(1, clients):
        ends = ends + row_in[c][:, width:]

    z_start(1, ends[:, :128])
    for piece in pieces[4:]:
        piece.wait()
    noise = jnp.concatenate(
        [nin_ref[pl.ds(chip, 1), :], nout_ref[pl.ds(chip, 1), :]], axis=1
    )
    weights = ends[:, 128:]
    wsum = jnp.sum(weights, axis=1, keepdims=True)
    scales = weights * jnp.minimum(1.0, clip_bound / jnp.sqrt(z_finish(1) + 1e-06))
    row = scales[:, :1] * row_in[0][:, :width]
    for c in range(1, clients):
        row = row + scales[:, c : c + 1] * row_in[c][:, :width]
    row_done[chip] = (row + noise_mult * clip_bound * noise) * out_scale / wsum

    def rd_copy(k):
        return pltpu.make_async_remote_copy(
            src_ref=row_done.at[chip],
            dst_ref=row_done.at[chip],
            send_sem=rd_send.at[k],
            recv_sem=rd_recv.at[k],
            device_id={"client": at_chip(k) * CORES + core},
            device_id_type=MESH,
        )

    for k in range(1, chips):
        rd_copy(k).start()

    def drain_step(it, _):
        for way in range(2):
            for e in range(stops):
                for h in range(2):
                    if long(way, h) or e > 0:
                        rs_copy(it, way, h, 0, e, z).wait_send()
                    rs_copy(it, way, h, 1, e, z).wait_send()
                if way == 0 or e < stops - 1:
                    pt_copy(it, way, 0, e, z).wait_send()
                pt_copy(it, way, 1, e, z).wait_send()

            @pl.when(it < ITERS - 1)
            def _():
                for e in range(stops):
                    for h in range(2):
                        if long(way, h) or e < stops - 1:
                            ag_copy(it, way, h, 0, e, z).wait_send()
                        ag_copy(it, way, h, 1, e, z).wait_send()

        return 0

    lax.fori_loop(0, ITERS, drain_step, 0)

    for k in range(1, chips):
        for to_core in range(CORES):
            ro_copy(k, to_core, core).wait_send()
    ro_copy(0, 1 - core, core).wait_send()
    for k in range(1, chips):
        rd_copy(k).wait()
    for r in range(rank):
        row = row_done[r]
        oin_ref[r : r + 1, :] = row[:, :width_in]
        oout_ref[r : r + 1, :] = row[:, width_in:]


def on_device(
    n,
    clients,
    hidden,
    frozen_residual,
    head,
    global_input_factor,
    global_output_factor,
    counts,
    weights,
    input_privacy_noise,
    output_privacy_noise,
):
    tokens, hidden_units = hidden.shape[1:]
    nout = head.shape[1]
    rank, model_width = global_output_factor.shape
    width_in = input_privacy_noise.shape[1]
    width_out = output_privacy_noise.shape[1]
    half = rank // 2
    stops = n // 4
    chips = clients // CORES
    width = width_in + width_out
    out_scale = math.sqrt(rank * (hidden_units + model_width)) / clip_bound
    f32 = jnp.float32
    dma = pltpu.SemaphoreType.DMA
    hbm = pl.BlockSpec(memory_space=pltpu.HBM)
    vmem = pl.BlockSpec(memory_space=pltpu.VMEM)
    smem = pl.BlockSpec(memory_space=pltpu.SMEM)
    return pl.pallas_call(
        functools.partial(kernel, n, clients, out_scale),
        out_shape=(
            jax.ShapeDtypeStruct((rank, width_in), f32),
            jax.ShapeDtypeStruct((rank, width_out), f32),
        ),
        in_specs=[
            hbm, hbm, hbm, hbm, hbm, smem, smem, hbm, hbm
        ],
        out_specs=(vmem, vmem),
        scratch_shapes=[
            pltpu.VMEM((nout, tokens), jnp.bfloat16),
            pltpu.VMEM((nout, model_width), jnp.bfloat16),
            pltpu.VMEM((rank, hidden_units), jnp.bfloat16),
            pltpu.VMEM((rank, model_width), jnp.bfloat16),
            pltpu.VMEM((rank, width_in), f32),
            pltpu.VMEM((rank, width_out), f32),
            pltpu.VMEM((n, tokens, width_in), jnp.bfloat16),
            pltpu.VMEM((nout, nout), f32),
            pltpu.VMEM((rank, nout), f32),
            pltpu.VMEM((nout, rank), f32),
            pltpu.VMEM((rank, nout), f32),
            pltpu.VMEM((1, tokens), f32),
            pltpu.VMEM((1, tokens), f32),
            pltpu.VMEM((tokens, rank), f32),
            pltpu.VMEM((rank, tokens), jnp.bfloat16),
            pltpu.VMEM((rank, rank), f32),
            pltpu.VMEM((rank, tokens), f32),
            pltpu.VMEM((ITERS, n, 2, half, width_in), f32),
            pltpu.VMEM((ITERS, 2, 2, 2, stops, half, width_in), f32),
            pltpu.VMEM((ITERS - 1, n, 2, half, width_in), f32),
            pltpu.VMEM((2, half, width_in), f32),
            pltpu.VMEM((ITERS, n, half, 128), f32),
            pltpu.VMEM((2, n, 1, 128), f32),
            pltpu.VMEM((rank, 1, width + 256), f32),
            pltpu.VMEM((clients, 1, width + 256), f32),
            pltpu.VMEM((rank, 1, width), f32),
            dma((6,)),
            dma((n,)),
            dma((ITERS, 2, 2, 2, stops)),
            dma((ITERS, 2, 2, 2, stops)),
            dma((ITERS - 1, 2, 2, 2, stops)),
            dma((ITERS - 1, 2, 2, 2, stops)),
            dma((ITERS, 2, 2, stops)),
            dma((ITERS, 2, 2, stops)),
            dma((2, n)),
            dma((2, n)),
            dma((chips, CORES)),
            dma((chips, CORES)),
            dma((chips,)),
            dma((chips,)),
        ],
        compiler_params=pltpu.CompilerParams(
            collective_id=0, has_side_effects=True, vmem_limit_bytes=63 * 1024 * 1024
        ),
    )(
        hidden,
        frozen_residual[0].T,
        head[0],
        global_input_factor,
        global_output_factor,
        counts,
        weights,
        input_privacy_noise,
        output_privacy_noise,
    )


def solution(mesh):
    in_specs = (
        P("client", "dp", None),
        P("client", "dp", None),
        P("client", None, None),
        P(),
        P(),
        P("client", "dp"),
        P("client"),
        P(None, "dp"),
        P(None, "dp"),
    )
    out_specs = (P(None, "dp"), P(None, "dp"))
    body = functools.partial(on_device, mesh.shape["dp"], mesh.shape["client"])
    return jax.shard_map(
        body, mesh=mesh, in_specs=in_specs, out_specs=out_specs, check_vma=False
    )
```

```python
import functools
import math

import jax
import jax.numpy as jnp
from jax import lax
from jax.experimental import pallas as pl
from jax.experimental.pallas import tpu as pltpu
from jax.sharding import PartitionSpec as P

ITERS = 3
CORES = 2

learn_rate = 0.1
clip_bound = 0.001
noise_mult = 0.1

PARENT = {8: 6, 7: 6, 6: 4, 5: 4, 4: 2, 3: 2, 2: 0, 1: 0}
CHILDREN = {p: [k for k in PARENT if PARENT[k] == p] for p in range(9)}

MESH = pl.DeviceIdType.MESH
HIGH = lax.Precision.HIGHEST
NN = (((1,), (0,)), ((), ()))
NT = (((1,), (1,)), ((), ()))
TN = (((0,), (0,)), ((), ()))


def mm(a, b, dims=NN, precision=None):
    return lax.dot_general(
        a, b, dims, precision=precision, preferred_element_type=jnp.float32
    )


def kernel(
    n,
    clients,
    out_scale,
    hid_ref,
    res_hbm,
    head_hbm,
    a0_hbm,
    b0_hbm,
    cnt_ref,
    w_ref,
    nin_hbm,
    nout_hbm,
    oin_ref,
    oout_ref,
    res_ref,
    head_ref,
    a0_ref,
    b0_ref,
    nin_ref,
    nout_ref,
    hv,
    gram,
    mixed,
    mixed_t,
    inner_sum,
    mask,
    tokens_live,
    proj,
    dproj,
    square,
    base_in,
    grad,
    slot,
    a_all,
    own,
    inner_out,
    inner_in,
    inner_all,
    spread,
    row_out,
    row_in,
    row_done,
    op_sem,
    hid_sem,
    rs_send,
    rs_recv,
    ag_send,
    ag_recv,
    ir_send,
    ir_recv,
    is_send,
    is_recv,
    sc_send,
    sc_recv,
    ro_send,
    ro_recv,
    rd_send,
    rd_recv,
):
    half_n = n // 2
    chips = clients // CORES
    rank, width_in = nin_ref.shape
    width_out = nout_ref.shape[1]
    half = rank // 2
    nout = head_ref.shape[0]
    tokens = hv.shape[1]
    width = width_in + width_out

    z = lax.axis_index("dp")
    client = lax.axis_index("client")
    chip = lax.div(client, CORES)
    core = lax.rem(client, CORES)
    def at_z(k):
        return lax.rem(z + k, n)

    def at_chip(k):
        return lax.rem(chip + k, chips)

    barrier = pltpu.get_barrier_semaphore()
    for k in range(1, n):
        pl.semaphore_signal(barrier, inc=1, device_id={"dp": at_z(k)}, device_id_type=MESH)
    for k in range(1, clients):
        pl.semaphore_signal(
            barrier, inc=1, device_id={"client": lax.rem(client + k, clients)}, device_id_type=MESH
        )

    def load(j):
        return pltpu.make_async_copy(
            hid_ref.at[0, :, pl.ds(j * width_in, width_in)], hv.at[j], hid_sem.at[j]
        )

    pieces = [
        pltpu.make_async_copy(src, dst, op_sem.at[i])
        for i, (src, dst) in enumerate(
            [
                (head_hbm, head_ref),
                (b0_hbm, b0_ref),
                (res_hbm, res_ref),
                (a0_hbm, a0_ref),
                (nin_hbm, nin_ref),
                (nout_hbm, nout_ref),
            ]
        )
    ]
    for piece in pieces[:4]:
        piece.start()
    for j in range(n):
        load(j).start()
    for piece in pieces[4:]:
        piece.start()

    lane = lax.broadcasted_iota(jnp.int32, (1, tokens), 1)
    live = cnt_ref[0, 0]

    pl.semaphore_wait(barrier, (n - 1) + (clients - 1))

    def z_copy(which, k):
        return pltpu.make_async_remote_copy(
            src_ref=spread.at[which, z],
            dst_ref=spread.at[which, z],
            send_sem=sc_send.at[which, k],
            recv_sem=sc_recv.at[which, k],
            device_id={"dp": at_z(k)},
            device_id_type=MESH,
        )

    def z_start(which, row):
        spread[which, z] = row
        for k in range(1, n):
            z_copy(which, k).start()

    def z_finish(which):
        for k in range(1, n):
            z_copy(which, k).wait()
        total = spread[which, 0]
        for j in range(1, n):
            total = total + spread[which, j]
        return total

    z_start(0, jnp.full((1, 128), live.astype(jnp.float32), jnp.float32))

    for piece in pieces[:3]:
        piece.wait()
    head = head_ref[...]
    gram[...] = mm(head, head, NT)
    mixed[...] = mm(b0_ref[...], head, NT)
    mixed_t[...] = mm(head, b0_ref[...], NT)
    inner_sum[...] = jnp.zeros_like(inner_sum)

    def from_mixed():
        square[...] = mm(mixed[...], mixed[...], NT, HIGH)
        base_in[...] = mm(mixed[...], res_ref[...].astype(jnp.float32), NN, HIGH)

    from_mixed()
    pieces[3].wait()
    proj[...] = jnp.zeros_like(proj)

    def first(j, _):
        load(j).wait()
        cols = pl.ds(pl.multiple_of(j * width_in, 128), width_in)
        proj[...] += mm(hv[j], a0_ref[:, cols], NT)
        return 0

    lax.fori_loop(0, n, first, 0)

    start_cols = pl.ds(pl.multiple_of(z * width_in, 128), width_in)
    own_zero = a0_ref[:, start_cols].astype(jnp.float32)
    for h in range(2):
        own[h] = own_zero[h * half : (h + 1) * half]
    mask[...] = (lane < live).astype(jnp.float32)
    tokens_live[...] = z_finish(0)

    def toward(way, k):
        return at_z(n - k) if way == 0 else at_z(k)

    def rs_copy(it, way, h, k, owner):
        return pltpu.make_async_remote_copy(
            src_ref=grad.at[it, owner, h],
            dst_ref=slot.at[it, way, h, k - 1],
            send_sem=rs_send.at[it, way, h, k - 1],
            recv_sem=rs_recv.at[it, way, h, k - 1],
            device_id={"dp": toward(way, k - PARENT[k])},
            device_id_type=MESH,
        )

    def ag_copy(it, way, h, k, owner):
        return pltpu.make_async_remote_copy(
            src_ref=a_all.at[it, owner, h],
            dst_ref=a_all.at[it, owner, h],
            send_sem=ag_send.at[it, way, h, k - 1],
            recv_sem=ag_recv.at[it, way, h, k - 1],
            device_id={"dp": toward(way, k - PARENT[k])},
            device_id_type=MESH,
        )

    def row_copy(it, k):
        return pltpu.make_async_remote_copy(
            src_ref=inner_out.at[it, at_z(k)],
            dst_ref=inner_in.at[it, z],
            send_sem=ir_send.at[it, k],
            recv_sem=ir_recv.at[it, k],
            device_id={"dp": at_z(k)},
            device_id_type=MESH,
        )

    def sum_copy(it, k):
        return pltpu.make_async_remote_copy(
            src_ref=inner_all.at[it, z],
            dst_ref=inner_all.at[it, z],
            send_sem=is_send.at[it, k],
            recv_sem=is_recv.at[it, k],
            device_id={"dp": at_z(k)},
            device_id_type=MESH,
        )

    def long(way, h):
        return way == h

    def reaches(way, h, k):
        return k < half_n or long(way, h)

    chains = ((0, 0), (1, 1), (0, 1), (1, 0))
    far = at_z(half_n)

    def local_step(it, _):
        weighted = mask[...] / tokens_live[...]
        through = mm(square[...], proj[...], NT, HIGH)
        dproj[...] = ((base_in[...] + through) * weighted).astype(jnp.bfloat16)

        def local(owner):
            value = mm(dproj[...], hv[owner])
            for h in range(2):
                grad[it, owner, h] = value[h * half : (h + 1) * half]

        def local_both(k):
            for way in range(2):
                local(toward(way, k))

        def send_raw(k, h):
            for way in range(2):
                if reaches(way, h, k):
                    rs_copy(it, way, h, k, toward(way, k)).start()

        def gather_terms(way, h, k, owner):
            total = grad[it, owner, h]
            for child in reversed(CHILDREN[k]):
                if reaches(way, h, child):
                    rs_copy(it, way, h, child, owner).wait_recv()
                    total = total + slot[it, way, h, child - 1]
            return total

        def send_on(way, h, k):
            owner = toward(way, k)
            grad[it, owner, h] = gather_terms(way, h, k, owner)
            rs_copy(it, way, h, k, owner).start()

        local(far)
        send_raw(8, 0)
        local_both(7)
        send_raw(7, 0)
        local_both(6)
        local_both(5)
        send_raw(5, 0)
        proj_t = proj[...].T
        resid = res_ref[...].astype(jnp.float32) + mm(mixed_t[...], proj_t, NN, HIGH)
        inner = mm(proj_t, resid * weighted, NT, HIGH)
        send_raw(8, 1)
        send_raw(7, 1)
        send_raw(5, 1)
        wide = jnp.concatenate([inner, jnp.zeros_like(inner)], axis=1)
        for r in range(rank):
            inner_out[it, r] = wide[r : r + 1]
        inner_in[it, z] = inner_out[it, z]
        for k in range(1, n):
            row_copy(it, k).start()
        for k in (6, 4, 2):
            for way in range(2):
                send_on(way, 0, k)
            if k > 2:
                local_both(k - 2)
                local_both(k - 3)
                send_raw(k - 3, 0)
            else:
                local(z)
            for way in range(2):
                send_on(way, 1, k)
            if k > 2:
                send_raw(k - 3, 1)
            if k == 4:
                for j in range(1, n):
                    row_copy(it, j).wait_recv()
                total = inner_in[it, 0]
                for j in range(1, n):
                    total = total + inner_in[it, j]
                inner_all[it, z] = total
                for j in range(1, n):
                    sum_copy(it, j).start()
        for h in range(2):
            total = grad[it, z, h]
            for way in range(2):
                for child in CHILDREN[0]:
                    rs_copy(it, way, h, child, z).wait_recv()
                    total = total + slot[it, way, h, child - 1]
            own[h] = own[h] - learn_rate * total

            @pl.when(it < ITERS - 1)
            def _():
                a_all[it, z, h] = own[h]
                for way in range(2):
                    ag_copy(it, way, h, 2, z).start()

        def inner_total():
            for k in range(1, n):
                sum_copy(it, k).wait_recv()
            rows = [inner_all[it, r][:, :nout] for r in range(rank)]
            return jnp.concatenate(rows, axis=0)

        @pl.when(it == ITERS - 1)
        def _():
            inner_sum[...] += inner_total()

        @pl.when(it < ITERS - 1)
        def _():
            def project(owner):
                rows = jnp.concatenate([a_all[it, owner, 0], a_all[it, owner, 1]], axis=0)
                return mm(hv[owner], rows.astype(jnp.bfloat16), NT)

            def use(k):
                for way in range(2):
                    proj[...] += project(toward(1 - way, k))

            def arrive(k, h):
                for way in range(2):
                    if reaches(way, h, k):
                        ag_copy(it, way, h, k, toward(1 - way, k)).wait_recv()

            def pass_on(parent, k, h):
                for way in range(2):
                    if reaches(way, h, k):
                        ag_copy(it, way, h, k, toward(1 - way, parent)).start()

            pass_on(0, 1, 0)
            proj[...] = project(z)
            pass_on(0, 1, 1)

            arrive(2, 0)
            pass_on(2, 4, 0)
            step_inner = inner_total()
            inner_sum[...] += step_inner
            pass_on(2, 3, 0)
            arrive(2, 1)
            pass_on(2, 4, 1)
            use(2)
            pass_on(2, 3, 1)
            arrive(1, 0)
            arrive(1, 1)
            use(1)

            arrive(4, 0)
            pass_on(4, 6, 0)
            mixed[...] = mixed[...] - learn_rate * mm(step_inner, gram[...], NN, HIGH)
            mixed_t[...] = mixed_t[...] - learn_rate * mm(gram[...], step_inner, NT, HIGH)
            pass_on(4, 5, 0)
            arrive(4, 1)
            pass_on(4, 6, 1)
            use(4)
            pass_on(4, 5, 1)
            arrive(3, 0)
            arrive(3, 1)
            use(3)

            arrive(6, 0)
            pass_on(6, 8, 0)
            pass_on(6, 7, 0)
            from_mixed()
            arrive(6, 1)
            pass_on(6, 8, 1)
            pass_on(6, 7, 1)
            use(6)
            arrive(5, 0)
            arrive(5, 1)
            use(5)

            arrive(7, 0)
            arrive(7, 1)
            use(7)
            arrive(8, 0)
            arrive(8, 1)
            proj[...] += project(far)

        return 0

    lax.fori_loop(0, ITERS, local_step, 0)

    own_three = jnp.concatenate([own[0], own[1]], axis=0)
    delta_in = own_three - own_zero
    out_cols = pl.ds(pl.multiple_of(z * width_out, 128), width_out)
    head_cols = head_ref[:, out_cols].astype(jnp.float32)
    delta_out = -learn_rate * mm(inner_sum[...], head_cols, NN, HIGH)
    delta = jnp.concatenate([delta_in, delta_out], axis=1)
    sums = jnp.sum(delta * delta, axis=0, keepdims=True)
    lanes = sums[:, :128]
    for j in range(1, width // 128):
        lanes = lanes + sums[:, j * 128 : (j + 1) * 128]
    squares = jnp.sum(lanes, axis=1, keepdims=True)
    weight = w_ref[0].astype(jnp.float32)

    mine = lax.broadcasted_iota(jnp.int32, (1, 128), 1) == client
    ends = jnp.concatenate(
        [jnp.where(mine, squares, 0.0), jnp.where(mine, weight, 0.0)], axis=1
    )
    for r in range(rank):
        row_out[r] = jnp.concatenate([delta[r : r + 1], ends], axis=1)

    def ro_copy(k, to_core, from_core):
        return pltpu.make_async_remote_copy(
            src_ref=row_out.at[at_chip(k)],
            dst_ref=row_in.at[client],
            send_sem=ro_send.at[k, to_core],
            recv_sem=ro_recv.at[k, from_core],
            device_id={"client": at_chip(k) * CORES + to_core},
            device_id_type=MESH,
        )

    for k in range(1, chips):
        for to_core in range(CORES):
            ro_copy(k, to_core, core).start()
    ro_copy(0, 1 - core, core).start()
    row_in[client] = row_out[chip]
    for k in range(1, chips):
        for from_core in range(CORES):
            ro_copy(k, from_core, from_core).wait_recv()
    ro_copy(0, 1 - core, 1 - core).wait_recv()
    ends = row_in[0][:, width:]
    for c in range(1, clients):
        ends = ends + row_in[c][:, width:]

    z_start(1, ends[:, :128])
    for piece in pieces[4:]:
        piece.wait()
    noise = jnp.concatenate(
        [nin_ref[pl.ds(chip, 1), :], nout_ref[pl.ds(chip, 1), :]], axis=1
    )
    weights = ends[:, 128:]
    wsum = jnp.sum(weights, axis=1, keepdims=True)
    scales = weights * jnp.minimum(1.0, clip_bound / jnp.sqrt(z_finish(1) + 1e-06))
    row = scales[:, :1] * row_in[0][:, :width]
    for c in range(1, clients):
        row = row + scales[:, c : c + 1] * row_in[c][:, :width]
    row_done[chip] = (row + noise_mult * clip_bound * noise) * out_scale / wsum

    def rd_copy(k):
        return pltpu.make_async_remote_copy(
            src_ref=row_done.at[chip],
            dst_ref=row_done.at[chip],
            send_sem=rd_send.at[k],
            recv_sem=rd_recv.at[k],
            device_id={"client": at_chip(k) * CORES + core},
            device_id_type=MESH,
        )

    for k in range(1, chips):
        rd_copy(k).start()

    def drain_step(it, _):
        for way, h in chains:
            for k in PARENT:
                if reaches(way, h, k):
                    rs_copy(it, way, h, k, z).wait_send()
        for k in range(1, n):
            row_copy(it, k).wait_send()
            sum_copy(it, k).wait_send()

        @pl.when(it < ITERS - 1)
        def _():
            for way, h in chains:
                for k in PARENT:
                    if reaches(way, h, k):
                        ag_copy(it, way, h, k, z).wait_send()

        return 0

    lax.fori_loop(0, ITERS, drain_step, 0)

    for k in range(1, chips):
        for to_core in range(CORES):
            ro_copy(k, to_core, core).wait_send()
    ro_copy(0, 1 - core, core).wait_send()
    for k in range(1, chips):
        rd_copy(k).wait()
    for r in range(rank):
        row = row_done[r]
        oin_ref[r : r + 1, :] = row[:, :width_in]
        oout_ref[r : r + 1, :] = row[:, width_in:]


def on_device(
    n,
    clients,
    hidden,
    frozen_residual,
    head,
    global_input_factor,
    global_output_factor,
    counts,
    weights,
    input_privacy_noise,
    output_privacy_noise,
):
    tokens, hidden_units = hidden.shape[1:]
    nout = head.shape[1]
    rank, model_width = global_output_factor.shape
    width_in = input_privacy_noise.shape[1]
    width_out = output_privacy_noise.shape[1]
    half = rank // 2
    half_n = n // 2
    chips = clients // CORES
    width = width_in + width_out
    out_scale = math.sqrt(rank * (hidden_units + model_width)) / clip_bound
    f32 = jnp.float32
    dma = pltpu.SemaphoreType.DMA
    hbm = pl.BlockSpec(memory_space=pltpu.HBM)
    vmem = pl.BlockSpec(memory_space=pltpu.VMEM)
    smem = pl.BlockSpec(memory_space=pltpu.SMEM)
    return pl.pallas_call(
        functools.partial(kernel, n, clients, out_scale),
        out_shape=(
            jax.ShapeDtypeStruct((rank, width_in), f32),
            jax.ShapeDtypeStruct((rank, width_out), f32),
        ),
        in_specs=[
            hbm, hbm, hbm, hbm, hbm, smem, smem, hbm, hbm
        ],
        out_specs=(vmem, vmem),
        scratch_shapes=[
            pltpu.VMEM((nout, tokens), jnp.bfloat16),
            pltpu.VMEM((nout, model_width), jnp.bfloat16),
            pltpu.VMEM((rank, hidden_units), jnp.bfloat16),
            pltpu.VMEM((rank, model_width), jnp.bfloat16),
            pltpu.VMEM((rank, width_in), f32),
            pltpu.VMEM((rank, width_out), f32),
            pltpu.VMEM((n, tokens, width_in), jnp.bfloat16),
            pltpu.VMEM((nout, nout), f32),
            pltpu.VMEM((rank, nout), f32),
            pltpu.VMEM((nout, rank), f32),
            pltpu.VMEM((rank, nout), f32),
            pltpu.VMEM((1, tokens), f32),
            pltpu.VMEM((1, tokens), f32),
            pltpu.VMEM((tokens, rank), f32),
            pltpu.VMEM((rank, tokens), jnp.bfloat16),
            pltpu.VMEM((rank, rank), f32),
            pltpu.VMEM((rank, tokens), f32),
            pltpu.VMEM((ITERS, n, 2, half, width_in), f32),
            pltpu.VMEM((ITERS, 2, 2, half_n, half, width_in), f32),
            pltpu.VMEM((ITERS - 1, n, 2, half, width_in), f32),
            pltpu.VMEM((2, half, width_in), f32),
            pltpu.VMEM((ITERS, n, 1, 128), f32),
            pltpu.VMEM((ITERS, n, 1, 128), f32),
            pltpu.VMEM((ITERS, n, 1, 128), f32),
            pltpu.VMEM((2, n, 1, 128), f32),
            pltpu.VMEM((rank, 1, width + 256), f32),
            pltpu.VMEM((clients, 1, width + 256), f32),
            pltpu.VMEM((rank, 1, width), f32),
            dma((6,)),
            dma((n,)),
            dma((ITERS, 2, 2, half_n)),
            dma((ITERS, 2, 2, half_n)),
            dma((ITERS - 1, 2, 2, half_n)),
            dma((ITERS - 1, 2, 2, half_n)),
            dma((ITERS, n)),
            dma((ITERS, n)),
            dma((ITERS, n)),
            dma((ITERS, n)),
            dma((2, n)),
            dma((2, n)),
            dma((chips, CORES)),
            dma((chips, CORES)),
            dma((chips,)),
            dma((chips,)),
        ],
        compiler_params=pltpu.CompilerParams(
            collective_id=0, has_side_effects=True, vmem_limit_bytes=63 * 1024 * 1024
        ),
    )(
        hidden,
        frozen_residual[0].T,
        head[0],
        global_input_factor,
        global_output_factor,
        counts,
        weights,
        input_privacy_noise,
        output_privacy_noise,
    )


def solution(mesh):
    in_specs = (
        P("client", "dp", None),
        P("client", "dp", None),
        P("client", None, None),
        P(),
        P(),
        P("client", "dp"),
        P("client"),
        P(None, "dp"),
        P(None, "dp"),
    )
    out_specs = (P(None, "dp"), P(None, "dp"))
    body = functools.partial(on_device, mesh.shape["dp"], mesh.shape["client"])
    return jax.shard_map(
        body, mesh=mesh, in_specs=in_specs, out_specs=out_specs, check_vma=False
    )
```

```python
import functools
import math

import jax
import jax.numpy as jnp
from jax import lax
from jax.experimental import pallas as pl
from jax.experimental.pallas import tpu as pltpu
from jax.sharding import PartitionSpec as P

ITERS = 3
CORES = 2
BLOCK = 4
VMEM_BYTES = 63 * 1024 * 1024

learn_rate = 0.1
clip_bound = 0.001
noise_mult = 0.1

PARENT = {8: 6, 7: 6, 6: 4, 5: 4, 4: 2, 3: 2, 2: 0, 1: 0}
CHILDREN = {p: [k for k in PARENT if PARENT[k] == p] for p in range(9)}

MESH = pl.DeviceIdType.MESH
HIGH = lax.Precision.HIGHEST
NN = (((1,), (0,)), ((), ()))
NT = (((1,), (1,)), ((), ()))
TN = (((0,), (0,)), ((), ()))


def mm(a, b, dims=NN, precision=None):
    return lax.dot_general(
        a, b, dims, precision=precision, preferred_element_type=jnp.float32
    )


def kernel(
    n,
    clients,
    out_scale,
    hid_ref,
    res_hbm,
    head_hbm,
    a0_hbm,
    b0_hbm,
    cnt_ref,
    w_ref,
    nin_hbm,
    nout_hbm,
    out_ref,
    res_ref,
    head_ref,
    a0_ref,
    b0_ref,
    nin_ref,
    nout_ref,
    hv,
    gram,
    mixed,
    mixed_t,
    inner_sum,
    mask,
    tokens_live,
    proj,
    dproj,
    square,
    base_in,
    grad,
    slot,
    a_all,
    own,
    inner_out,
    inner_in,
    spread,
    row_out,
    row_in,
    row_done,
    op_sem,
    hid_sem,
    rs_send,
    rs_recv,
    ag_send,
    ag_recv,
    in_send,
    in_recv,
    sc_send,
    sc_recv,
    ro_send,
    ro_recv,
    rd_send,
    rd_recv,
):
    half_n = n // 2
    chips = clients // CORES
    rank, width_in = nin_ref.shape
    width_out = nout_ref.shape[1]
    half = rank // 2
    nout = head_ref.shape[0]
    tokens = hv.shape[1]
    width = width_in + width_out

    z = lax.axis_index("dp")
    client = lax.axis_index("client")
    chip = lax.div(client, CORES)
    core = lax.rem(client, CORES)
    corner = lax.div(z, BLOCK) * BLOCK

    def at_z(k):
        return lax.rem(z + k, n)

    def at_chip(k):
        return lax.rem(chip + k, chips)

    def load(j):
        return pltpu.make_async_copy(
            hid_ref.at[0, :, pl.ds(j * width_in, width_in)], hv.at[j], hid_sem.at[j]
        )

    pieces = [
        pltpu.make_async_copy(src, dst, op_sem.at[i])
        for i, (src, dst) in enumerate(
            [
                (head_hbm, head_ref),
                (b0_hbm, b0_ref),
                (res_hbm, res_ref),
                (a0_hbm, a0_ref),
                (nin_hbm, nin_ref),
                (nout_hbm, nout_ref),
            ]
        )
    ]
    for piece in pieces[:4]:
        piece.start()
    for j in range(n):
        load(j).start()
    for piece in pieces[4:]:
        piece.start()

    barrier = pltpu.get_barrier_semaphore()
    for k in range(1, n):
        pl.semaphore_signal(barrier, inc=1, device_id={"dp": at_z(k)}, device_id_type=MESH)
    for k in range(1, clients):
        pl.semaphore_signal(
            barrier, inc=1, device_id={"client": lax.rem(client + k, clients)}, device_id_type=MESH
        )

    for piece in pieces[:3]:
        piece.wait()
    head = head_ref[...]
    gram[...] = mm(head, head, NT)
    mixed[...] = mm(b0_ref[...], head, NT)
    mixed_t[...] = mm(head, b0_ref[...], NT)
    inner_sum[...] = jnp.zeros_like(inner_sum)

    def from_mixed():
        square[...] = mm(mixed[...], mixed[...], NT, HIGH)
        base_in[...] = mm(mixed[...], res_ref[...].astype(jnp.float32), NN, HIGH)

    from_mixed()

    lane = lax.broadcasted_iota(jnp.int32, (1, tokens), 1)
    live = cnt_ref[0, 0]

    pl.semaphore_wait(barrier, (n - 1) + (clients - 1))

    def z_copy(which, k):
        return pltpu.make_async_remote_copy(
            src_ref=spread.at[which, z],
            dst_ref=spread.at[which, z],
            send_sem=sc_send.at[which, k],
            recv_sem=sc_recv.at[which, k],
            device_id={"dp": at_z(k)},
            device_id_type=MESH,
        )

    def z_start(which, row):
        spread[which, z] = row
        for k in range(1, n):
            z_copy(which, k).start()

    def z_finish(which):
        for k in range(1, n):
            z_copy(which, k).wait()
        total = spread[which, 0]
        for j in range(1, n):
            total = total + spread[which, j]
        return total

    z_start(0, jnp.full((1, 128), live.astype(jnp.float32), jnp.float32))

    pieces[3].wait()
    proj[...] = jnp.zeros_like(proj)

    def first(j, _):
        load(j).wait()
        cols = pl.ds(pl.multiple_of(j * width_in, 128), width_in)
        proj[...] += mm(hv[j], a0_ref[:, cols], NT)
        return 0

    lax.fori_loop(0, n, first, 0)

    start_cols = pl.ds(pl.multiple_of(z * width_in, 128), width_in)
    own_zero = a0_ref[:, start_cols].astype(jnp.float32)
    for h in range(2):
        own[h] = own_zero[h * half : (h + 1) * half]
    mask[...] = (lane < live).astype(jnp.float32)
    tokens_live[...] = z_finish(0)

    def toward(way, k):
        return at_z(n - k) if way == 0 else at_z(k)

    def rs_copy(it, way, h, k, owner):
        return pltpu.make_async_remote_copy(
            src_ref=grad.at[it, owner, h],
            dst_ref=slot.at[it, way, h, k - 1],
            send_sem=rs_send.at[it, way, h, k - 1],
            recv_sem=rs_recv.at[it, way, h, k - 1],
            device_id={"dp": toward(way, k - PARENT[k])},
            device_id_type=MESH,
        )

    def ag_copy(it, way, h, k, owner):
        return pltpu.make_async_remote_copy(
            src_ref=a_all.at[it, owner, h],
            dst_ref=a_all.at[it, owner, h],
            send_sem=ag_send.at[it, way, h, k - 1],
            recv_sem=ag_recv.at[it, way, h, k - 1],
            device_id={"dp": toward(way, k - PARENT[k])},
            device_id_type=MESH,
        )

    def inner_copy(it, stage, j):
        peer = at_z(j * BLOCK) if stage == 0 else corner + lax.rem(z - corner + j, BLOCK)
        return pltpu.make_async_remote_copy(
            src_ref=inner_out.at[it, stage],
            dst_ref=inner_in.at[it, stage, j - 1],
            send_sem=in_send.at[it, stage, j - 1],
            recv_sem=in_recv.at[it, stage, j - 1],
            device_id={"dp": peer},
            device_id_type=MESH,
        )

    def inner_start(it, stage, value):
        inner_out[it, stage] = value
        for j in range(1, BLOCK):
            inner_copy(it, stage, j).start()

    def inner_finish(it, stage):
        total = inner_out[it, stage]
        for j in range(1, BLOCK):
            inner_copy(it, stage, j).wait_recv()
            total = total + inner_in[it, stage, j - 1]
        return total

    def long(way, h):
        return way == h

    def reaches(way, h, k):
        return k < half_n or long(way, h)

    chains = ((0, 0), (1, 1), (0, 1), (1, 0))
    far = at_z(half_n)

    def local_step(it, _):
        weighted = mask[...] / tokens_live[...]
        through = mm(square[...], proj[...], NT, HIGH)
        dproj[...] = ((base_in[...] + through) * weighted).astype(jnp.bfloat16)

        def local(owner):
            value = mm(dproj[...], hv[owner])
            for h in range(2):
                grad[it, owner, h] = value[h * half : (h + 1) * half]

        def local_both(k):
            for way in range(2):
                local(toward(way, k))

        def send_raw(k, h):
            for way in range(2):
                if reaches(way, h, k):
                    rs_copy(it, way, h, k, toward(way, k)).start()

        def gather_terms(way, h, k, owner):
            total = grad[it, owner, h]
            for child in reversed(CHILDREN[k]):
                if reaches(way, h, child):
                    rs_copy(it, way, h, child, owner).wait_recv()
                    total = total + slot[it, way, h, child - 1]
            return total

        def send_on(way, h, k):
            owner = toward(way, k)
            grad[it, owner, h] = gather_terms(way, h, k, owner)
            rs_copy(it, way, h, k, owner).start()

        local(far)
        send_raw(8, 0)
        local_both(7)
        send_raw(7, 0)
        local_both(6)
        local_both(5)
        send_raw(5, 0)
        proj_t = proj[...].T
        resid = res_ref[...].astype(jnp.float32) + mm(mixed_t[...], proj_t, NN, HIGH)
        inner = mm(proj_t, resid * weighted, NT, HIGH)
        send_raw(8, 1)
        send_raw(7, 1)
        send_raw(5, 1)
        inner_start(it, 0, jnp.concatenate([inner[:half], inner[half:]], axis=1))
        for k in (6, 4, 2):
            for way in range(2):
                send_on(way, 0, k)
            if k > 2:
                local_both(k - 2)
                local_both(k - 3)
                send_raw(k - 3, 0)
            else:
                local(z)
            for way in range(2):
                send_on(way, 1, k)
            if k > 2:
                send_raw(k - 3, 1)
            if k == 4:
                inner_start(it, 1, inner_finish(it, 0))
        for h in range(2):
            total = grad[it, z, h]
            for way in range(2):
                for child in CHILDREN[0]:
                    rs_copy(it, way, h, child, z).wait_recv()
                    total = total + slot[it, way, h, child - 1]
            own[h] = own[h] - learn_rate * total

            @pl.when(it < ITERS - 1)
            def _():
                a_all[it, z, h] = own[h]
                for way in range(2):
                    ag_copy(it, way, h, 2, z).start()

        def inner_total():
            tile = inner_finish(it, 1)
            return jnp.concatenate([tile[:, :nout], tile[:, nout:]], axis=0)

        @pl.when(it == ITERS - 1)
        def _():
            inner_sum[...] += inner_total()

        @pl.when(it < ITERS - 1)
        def _():
            def project(owner):
                rows = jnp.concatenate([a_all[it, owner, 0], a_all[it, owner, 1]], axis=0)
                return mm(hv[owner], rows.astype(jnp.bfloat16), NT)

            def use(k):
                for way in range(2):
                    proj[...] += project(toward(1 - way, k))

            def arrive(k, h):
                for way in range(2):
                    if reaches(way, h, k):
                        ag_copy(it, way, h, k, toward(1 - way, k)).wait_recv()

            def pass_on(parent, k, h):
                for way in range(2):
                    if reaches(way, h, k):
                        ag_copy(it, way, h, k, toward(1 - way, parent)).start()

            pass_on(0, 1, 0)
            proj[...] = project(z)
            pass_on(0, 1, 1)

            arrive(2, 0)
            pass_on(2, 4, 0)
            step_inner = inner_total()
            inner_sum[...] += step_inner
            pass_on(2, 3, 0)
            arrive(2, 1)
            pass_on(2, 4, 1)
            use(2)
            pass_on(2, 3, 1)
            arrive(1, 0)
            arrive(1, 1)
            use(1)

            arrive(4, 0)
            pass_on(4, 6, 0)
            mixed[...] = mixed[...] - learn_rate * mm(step_inner, gram[...], NN, HIGH)
            mixed_t[...] = mixed_t[...] - learn_rate * mm(gram[...], step_inner, NT, HIGH)
            pass_on(4, 5, 0)
            arrive(4, 1)
            pass_on(4, 6, 1)
            use(4)
            pass_on(4, 5, 1)
            arrive(3, 0)
            arrive(3, 1)
            use(3)

            arrive(6, 0)
            pass_on(6, 8, 0)
            pass_on(6, 7, 0)
            from_mixed()
            arrive(6, 1)
            pass_on(6, 8, 1)
            pass_on(6, 7, 1)
            use(6)
            arrive(5, 0)
            arrive(5, 1)
            use(5)

            arrive(7, 0)
            arrive(7, 1)
            use(7)
            arrive(8, 0)
            arrive(8, 1)
            proj[...] += project(far)

        return 0

    lax.fori_loop(0, ITERS, local_step, 0)

    own_three = jnp.concatenate([own[0], own[1]], axis=0)
    delta_in = own_three - own_zero
    out_cols = pl.ds(pl.multiple_of(z * width_out, 128), width_out)
    head_cols = head_ref[:, out_cols].astype(jnp.float32)
    delta_out = -learn_rate * mm(inner_sum[...], head_cols, NN, HIGH)
    delta = jnp.concatenate([delta_in, delta_out], axis=1)
    sums = jnp.sum(delta * delta, axis=0, keepdims=True)
    lanes = sums[:, :128]
    for j in range(1, width // 128):
        lanes = lanes + sums[:, j * 128 : (j + 1) * 128]
    squares = jnp.sum(lanes, axis=1, keepdims=True)
    weight = w_ref[0].astype(jnp.float32)

    mine = lax.broadcasted_iota(jnp.int32, (1, 128), 1) == client
    ends = jnp.concatenate(
        [jnp.where(mine, squares, 0.0), jnp.where(mine, weight, 0.0)], axis=1
    )
    for r in range(rank):
        row_out[r] = jnp.concatenate([delta[r : r + 1], ends], axis=1)

    def ro_copy(k, to_core, from_core):
        return pltpu.make_async_remote_copy(
            src_ref=row_out.at[at_chip(k)],
            dst_ref=row_in.at[client],
            send_sem=ro_send.at[k, to_core],
            recv_sem=ro_recv.at[k, from_core],
            device_id={"client": at_chip(k) * CORES + to_core},
            device_id_type=MESH,
        )

    for k in range(1, chips):
        for to_core in range(CORES):
            ro_copy(k, to_core, core).start()
    ro_copy(0, 1 - core, core).start()
    row_in[client] = row_out[chip]
    for k in range(1, chips):
        for from_core in range(CORES):
            ro_copy(k, from_core, from_core).wait_recv()
    ro_copy(0, 1 - core, 1 - core).wait_recv()
    ends = row_in[0][:, width:]
    for c in range(1, clients):
        ends = ends + row_in[c][:, width:]

    z_start(1, ends[:, :128])
    for piece in pieces[4:]:
        piece.wait()
    noise = jnp.concatenate(
        [nin_ref[pl.ds(chip, 1), :], nout_ref[pl.ds(chip, 1), :]], axis=1
    )
    weights = ends[:, 128:]
    wsum = jnp.sum(weights, axis=1, keepdims=True)
    scales = weights * jnp.minimum(1.0, clip_bound / jnp.sqrt(z_finish(1) + 1e-06))
    row = scales[:, :1] * row_in[0][:, :width]
    for c in range(1, clients):
        row = row + scales[:, c : c + 1] * row_in[c][:, :width]
    row_done[chip] = (row + noise_mult * clip_bound * noise) * out_scale / wsum

    def rd_copy(k):
        return pltpu.make_async_remote_copy(
            src_ref=row_done.at[chip],
            dst_ref=row_done.at[chip],
            send_sem=rd_send.at[k],
            recv_sem=rd_recv.at[k],
            device_id={"client": at_chip(k) * CORES + core},
            device_id_type=MESH,
        )

    for k in range(1, chips):
        rd_copy(k).start()

    def drain_step(it, _):
        for way, h in chains:
            for k in PARENT:
                if reaches(way, h, k):
                    rs_copy(it, way, h, k, z).wait_send()
        for stage in range(2):
            for j in range(1, BLOCK):
                inner_copy(it, stage, j).wait_send()

        @pl.when(it < ITERS - 1)
        def _():
            for way, h in chains:
                for k in PARENT:
                    if reaches(way, h, k):
                        ag_copy(it, way, h, k, z).wait_send()

        return 0

    lax.fori_loop(0, ITERS, drain_step, 0)

    for k in range(1, chips):
        for to_core in range(CORES):
            ro_copy(k, to_core, core).wait_send()
    ro_copy(0, 1 - core, core).wait_send()
    for k in range(1, chips):
        rd_copy(k).wait()
    for r in range(rank):
        out_ref[r : r + 1, :] = row_done[r]


def split(rows_ref, oin_ref, oout_ref, sem):
    width_in = oin_ref.shape[1]
    width_out = oout_ref.shape[1]
    parts = (
        pltpu.make_async_copy(rows_ref.at[:, pl.ds(0, width_in)], oin_ref, sem.at[0]),
        pltpu.make_async_copy(rows_ref.at[:, pl.ds(width_in, width_out)], oout_ref, sem.at[1]),
    )
    for part in parts:
        part.start()
    for part in parts:
        part.wait()


def on_device(
    n,
    clients,
    hidden,
    frozen_residual,
    head,
    global_input_factor,
    global_output_factor,
    counts,
    weights,
    input_privacy_noise,
    output_privacy_noise,
):
    tokens, hidden_units = hidden.shape[1:]
    nout = head.shape[1]
    rank, model_width = global_output_factor.shape
    width_in = input_privacy_noise.shape[1]
    width_out = output_privacy_noise.shape[1]
    half = rank // 2
    half_n = n // 2
    chips = clients // CORES
    width = width_in + width_out
    out_scale = math.sqrt(rank * (hidden_units + model_width)) / clip_bound
    f32 = jnp.float32
    dma = pltpu.SemaphoreType.DMA
    hbm = pl.BlockSpec(memory_space=pltpu.HBM)
    vmem = pl.BlockSpec(memory_space=pltpu.VMEM)
    smem = pl.BlockSpec(memory_space=pltpu.SMEM)
    rows = pl.pallas_call(
        functools.partial(kernel, n, clients, out_scale),
        out_shape=jax.ShapeDtypeStruct((rank, width), f32),
        in_specs=[
            hbm, hbm, hbm, hbm, hbm, smem, smem, hbm, hbm
        ],
        out_specs=vmem,
        scratch_shapes=[
            pltpu.VMEM((nout, tokens), jnp.bfloat16),
            pltpu.VMEM((nout, model_width), jnp.bfloat16),
            pltpu.VMEM((rank, hidden_units), jnp.bfloat16),
            pltpu.VMEM((rank, model_width), jnp.bfloat16),
            pltpu.VMEM((rank, width_in), f32),
            pltpu.VMEM((rank, width_out), f32),
            pltpu.VMEM((n, tokens, width_in), jnp.bfloat16),
            pltpu.VMEM((nout, nout), f32),
            pltpu.VMEM((rank, nout), f32),
            pltpu.VMEM((nout, rank), f32),
            pltpu.VMEM((rank, nout), f32),
            pltpu.VMEM((1, tokens), f32),
            pltpu.VMEM((1, tokens), f32),
            pltpu.VMEM((tokens, rank), f32),
            pltpu.VMEM((rank, tokens), jnp.bfloat16),
            pltpu.VMEM((rank, rank), f32),
            pltpu.VMEM((rank, tokens), f32),
            pltpu.VMEM((ITERS, n, 2, half, width_in), f32),
            pltpu.VMEM((ITERS, 2, 2, half_n, half, width_in), f32),
            pltpu.VMEM((ITERS - 1, n, 2, half, width_in), f32),
            pltpu.VMEM((2, half, width_in), f32),
            pltpu.VMEM((ITERS, 2, half, 128), f32),
            pltpu.VMEM((ITERS, 2, BLOCK - 1, half, 128), f32),
            pltpu.VMEM((2, n, 1, 128), f32),
            pltpu.VMEM((rank, 1, width + 256), f32),
            pltpu.VMEM((clients, 1, width + 256), f32),
            pltpu.VMEM((rank, 1, width), f32),
            dma((6,)),
            dma((n,)),
            dma((ITERS, 2, 2, half_n)),
            dma((ITERS, 2, 2, half_n)),
            dma((ITERS - 1, 2, 2, half_n)),
            dma((ITERS - 1, 2, 2, half_n)),
            dma((ITERS, 2, BLOCK - 1)),
            dma((ITERS, 2, BLOCK - 1)),
            dma((2, n)),
            dma((2, n)),
            dma((chips, CORES)),
            dma((chips, CORES)),
            dma((chips,)),
            dma((chips,)),
        ],
        compiler_params=pltpu.CompilerParams(
            collective_id=0, has_side_effects=True, vmem_limit_bytes=VMEM_BYTES
        ),
    )(
        hidden,
        frozen_residual[0].T,
        head[0],
        global_input_factor,
        global_output_factor,
        counts,
        weights,
        input_privacy_noise,
        output_privacy_noise,
    )
    return pl.pallas_call(
        split,
        out_shape=(
            jax.ShapeDtypeStruct((rank, width_in), f32),
            jax.ShapeDtypeStruct((rank, width_out), f32),
        ),
        in_specs=[hbm],
        out_specs=(hbm, hbm),
        scratch_shapes=[dma((2,))],
        compiler_params=pltpu.CompilerParams(vmem_limit_bytes=VMEM_BYTES),
    )(rows)


def solution(mesh):
    in_specs = (
        P("client", "dp", None),
        P("client", "dp", None),
        P("client", None, None),
        P(),
        P(),
        P("client", "dp"),
        P("client"),
        P(None, "dp"),
        P(None, "dp"),
    )
    out_specs = (P(None, "dp"), P(None, "dp"))
    body = functools.partial(on_device, mesh.shape["dp"], mesh.shape["client"])
    return jax.shard_map(
        body, mesh=mesh, in_specs=in_specs, out_specs=out_specs, check_vma=False
    )
```

```python
import functools
import math

import jax
import jax.numpy as jnp
from jax import lax
from jax.experimental import pallas as pl
from jax.experimental.pallas import tpu as pltpu
from jax.sharding import PartitionSpec as P

ITERS = 3
CORES = 2
BLOCK = 4
VMEM_BYTES = 63 * 1024 * 1024

learn_rate = 0.1
clip_bound = 0.001
noise_mult = 0.1

PARENT = {8: 6, 7: 6, 6: 3, 5: 3, 4: 3, 3: 0, 2: 0, 1: 0}
CHILDREN = {p: [k for k in PARENT if PARENT[k] == p] for p in range(9)}
LEAVES = {p: [k for k in CHILDREN[p] if not CHILDREN[k]] for p in CHILDREN}
STOPS = [k for k in PARENT if CHILDREN[k]]

MESH = pl.DeviceIdType.MESH
HIGH = lax.Precision.HIGHEST
NN = (((1,), (0,)), ((), ()))
NT = (((1,), (1,)), ((), ()))
TN = (((0,), (0,)), ((), ()))


def mm(a, b, dims=NN, precision=None):
    return lax.dot_general(
        a, b, dims, precision=precision, preferred_element_type=jnp.float32
    )


def kernel(
    n,
    clients,
    out_scale,
    hid_ref,
    res_hbm,
    head_hbm,
    a0_hbm,
    b0_hbm,
    cnt_ref,
    w_ref,
    nin_hbm,
    nout_hbm,
    oin_ref,
    oout_ref,
    res_ref,
    head_ref,
    a0_ref,
    b0_ref,
    nin_ref,
    nout_ref,
    hv,
    gram,
    mixed,
    mixed_t,
    inner_sum,
    mask,
    tokens_live,
    proj,
    dproj,
    square,
    base_in,
    grad,
    slot,
    a_all,
    own,
    inner_out,
    inner_in,
    spread,
    row_out,
    row_in,
    row_done,
    op_sem,
    hid_sem,
    rs_send,
    rs_recv,
    ag_send,
    ag_recv,
    in_send,
    in_recv,
    sc_send,
    sc_recv,
    ro_send,
    ro_recv,
    rd_send,
    rd_recv,
):
    half_n = n // 2
    chips = clients // CORES
    rank, width_in = nin_ref.shape
    width_out = nout_ref.shape[1]
    half = rank // 2
    nout = head_ref.shape[0]
    tokens = hv.shape[1]
    width = width_in + width_out

    z = lax.axis_index("dp")
    client = lax.axis_index("client")
    chip = lax.div(client, CORES)
    core = lax.rem(client, CORES)
    corner = lax.div(z, BLOCK) * BLOCK

    def at_z(k):
        return lax.rem(z + k, n)

    def at_chip(k):
        return lax.rem(chip + k, chips)

    def load(j):
        return pltpu.make_async_copy(
            hid_ref.at[0, :, pl.ds(j * width_in, width_in)], hv.at[j], hid_sem.at[j]
        )

    pieces = [
        pltpu.make_async_copy(src, dst, op_sem.at[i])
        for i, (src, dst) in enumerate(
            [
                (head_hbm, head_ref),
                (b0_hbm, b0_ref),
                (res_hbm, res_ref),
                (a0_hbm, a0_ref),
                (nin_hbm, nin_ref),
                (nout_hbm, nout_ref),
            ]
        )
    ]
    for piece in pieces[:4]:
        piece.start()
    for j in range(n):
        load(j).start()
    for piece in pieces[4:]:
        piece.start()

    barrier = pltpu.get_barrier_semaphore()
    for k in range(1, n):
        pl.semaphore_signal(barrier, inc=1, device_id={"dp": at_z(k)}, device_id_type=MESH)
    for k in range(1, clients):
        pl.semaphore_signal(
            barrier, inc=1, device_id={"client": lax.rem(client + k, clients)}, device_id_type=MESH
        )

    for piece in pieces[:3]:
        piece.wait()
    head = head_ref[...]
    gram[...] = mm(head, head, NT)
    mixed[...] = mm(b0_ref[...], head, NT)
    mixed_t[...] = mm(head, b0_ref[...], NT)
    inner_sum[...] = jnp.zeros_like(inner_sum)

    def from_mixed():
        square[...] = mm(mixed[...], mixed[...], NT, HIGH)
        base_in[...] = mm(mixed[...], res_ref[...].astype(jnp.float32), NN, HIGH)

    from_mixed()

    lane = lax.broadcasted_iota(jnp.int32, (1, tokens), 1)
    live = cnt_ref[0, 0]

    pl.semaphore_wait(barrier, (n - 1) + (clients - 1))

    def z_copy(which, k):
        return pltpu.make_async_remote_copy(
            src_ref=spread.at[which, z],
            dst_ref=spread.at[which, z],
            send_sem=sc_send.at[which, k],
            recv_sem=sc_recv.at[which, k],
            device_id={"dp": at_z(k)},
            device_id_type=MESH,
        )

    def z_start(which, row):
        spread[which, z] = row
        for k in range(1, n):
            z_copy(which, k).start()

    def z_finish(which):
        for k in range(1, n):
            z_copy(which, k).wait()
        total = spread[which, 0]
        for j in range(1, n):
            total = total + spread[which, j]
        return total

    z_start(0, jnp.full((1, 128), live.astype(jnp.float32), jnp.float32))

    pieces[3].wait()
    proj[...] = jnp.zeros_like(proj)

    def first(j, _):
        load(j).wait()
        cols = pl.ds(pl.multiple_of(j * width_in, 128), width_in)
        proj[...] += mm(hv[j], a0_ref[:, cols], NT)
        return 0

    lax.fori_loop(0, n, first, 0)

    start_cols = pl.ds(pl.multiple_of(z * width_in, 128), width_in)
    own_zero = a0_ref[:, start_cols].astype(jnp.float32)
    for h in range(2):
        own[h] = own_zero[h * half : (h + 1) * half]
    mask[...] = (lane < live).astype(jnp.float32)
    tokens_live[...] = z_finish(0)

    def toward(way, k):
        return at_z(n - k) if way == 0 else at_z(k)

    def rs_copy(it, way, h, k, owner):
        return pltpu.make_async_remote_copy(
            src_ref=grad.at[it, owner, h],
            dst_ref=slot.at[it, way, h, k - 1],
            send_sem=rs_send.at[it, way, h, k - 1],
            recv_sem=rs_recv.at[it, way, h, k - 1],
            device_id={"dp": toward(way, k - PARENT[k])},
            device_id_type=MESH,
        )

    def ag_copy(it, way, h, k, owner):
        return pltpu.make_async_remote_copy(
            src_ref=a_all.at[it, owner, h],
            dst_ref=a_all.at[it, owner, h],
            send_sem=ag_send.at[it, way, h, k - 1],
            recv_sem=ag_recv.at[it, way, h, k - 1],
            device_id={"dp": toward(way, k - PARENT[k])},
            device_id_type=MESH,
        )

    def inner_copy(it, stage, j):
        peer = at_z(j * BLOCK) if stage == 0 else corner + lax.rem(z - corner + j, BLOCK)
        return pltpu.make_async_remote_copy(
            src_ref=inner_out.at[it, stage],
            dst_ref=inner_in.at[it, stage, j - 1],
            send_sem=in_send.at[it, stage, j - 1],
            recv_sem=in_recv.at[it, stage, j - 1],
            device_id={"dp": peer},
            device_id_type=MESH,
        )

    def inner_start(it, stage, value):
        inner_out[it, stage] = value
        for j in range(1, BLOCK):
            inner_copy(it, stage, j).start()

    def inner_finish(it, stage):
        total = inner_out[it, stage]
        for j in range(1, BLOCK):
            inner_copy(it, stage, j).wait_recv()
            total = total + inner_in[it, stage, j - 1]
        return total

    def long(way, h):
        return way == h

    def reaches(way, h, k):
        return k < half_n or long(way, h)

    chains = ((0, 0), (1, 1), (0, 1), (1, 0))
    far = at_z(half_n)

    def local_step(it, _):
        weighted = mask[...] / tokens_live[...]
        through = mm(square[...], proj[...], NT, HIGH)
        dproj[...] = ((base_in[...] + through) * weighted).astype(jnp.bfloat16)

        def local(owner):
            value = mm(dproj[...], hv[owner])
            for h in range(2):
                grad[it, owner, h] = value[h * half : (h + 1) * half]

        def local_both(k):
            for way in range(2):
                local(toward(way, k))

        def send_raw(k, h):
            for way in range(2):
                if reaches(way, h, k):
                    rs_copy(it, way, h, k, toward(way, k)).start()

        def gather_terms(way, h, k, owner):
            total = grad[it, owner, h]
            for child in reversed(CHILDREN[k]):
                if reaches(way, h, child):
                    rs_copy(it, way, h, child, owner).wait_recv()
                    total = total + slot[it, way, h, child - 1]
            return total

        def send_on(way, h, k):
            owner = toward(way, k)
            grad[it, owner, h] = gather_terms(way, h, k, owner)
            rs_copy(it, way, h, k, owner).start()

        targets = STOPS + [0]
        early = LEAVES[targets[0]] + LEAVES[targets[1]]
        for k in early:
            if k == half_n:
                local(far)
            else:
                local_both(k)
            send_raw(k, 0)
        local_both(targets[0])
        proj_t = proj[...].T
        resid = res_ref[...].astype(jnp.float32) + mm(mixed_t[...], proj_t, NN, HIGH)
        inner = mm(proj_t, resid * weighted, NT, HIGH)
        for k in early:
            send_raw(k, 1)
        inner_start(it, 0, jnp.concatenate([inner[:half], inner[half:]], axis=1))
        for i, k in enumerate(STOPS):
            later = LEAVES[targets[i + 2]] if i + 2 < len(targets) else []
            for way in range(2):
                send_on(way, 0, k)
            if targets[i + 1]:
                local_both(targets[i + 1])
            else:
                local(z)
            for leaf in later:
                local_both(leaf)
                send_raw(leaf, 0)
            for way in range(2):
                send_on(way, 1, k)
            for leaf in later:
                send_raw(leaf, 1)
            if i == len(STOPS) - 2:
                inner_start(it, 1, inner_finish(it, 0))
        for h in range(2):
            total = grad[it, z, h]
            for way in range(2):
                for child in CHILDREN[0]:
                    rs_copy(it, way, h, child, z).wait_recv()
                    total = total + slot[it, way, h, child - 1]
            own[h] = own[h] - learn_rate * total

            @pl.when(it < ITERS - 1)
            def _():
                a_all[it, z, h] = own[h]
                for way in range(2):
                    ag_copy(it, way, h, STOPS[-1], z).start()

        def inner_total():
            tile = inner_finish(it, 1)
            return jnp.concatenate([tile[:, :nout], tile[:, nout:]], axis=0)

        @pl.when(it == ITERS - 1)
        def _():
            inner_sum[...] += inner_total()

        @pl.when(it < ITERS - 1)
        def _():
            def project(owner):
                rows = jnp.concatenate([a_all[it, owner, 0], a_all[it, owner, 1]], axis=0)
                return mm(hv[owner], rows.astype(jnp.bfloat16), NT)

            def use(k):
                for way in range(2):
                    proj[...] += project(toward(1 - way, k))

            def arrive(k, h):
                for way in range(2):
                    if reaches(way, h, k):
                        ag_copy(it, way, h, k, toward(1 - way, k)).wait_recv()

            def pass_on(parent, k, h):
                for way in range(2):
                    if reaches(way, h, k):
                        ag_copy(it, way, h, k, toward(1 - way, parent)).start()

            def pass_leaves(parent, h):
                for k in LEAVES[parent]:
                    pass_on(parent, k, h)

            def use_leaves(parent):
                for k in LEAVES[parent]:
                    arrive(k, 0)
                    arrive(k, 1)
                    if k == half_n:
                        proj[...] += project(far)
                    else:
                        use(k)

            pass_leaves(0, 0)
            proj[...] = project(z)
            pass_leaves(0, 1)
            before = 0
            for k in reversed(STOPS):
                after = [c for c in CHILDREN[k] if CHILDREN[c]]
                arrive(k, 0)
                for c in after:
                    pass_on(k, c, 0)
                if before == 0:
                    step_inner = inner_total()
                    inner_sum[...] += step_inner
                    mixed[...] = mixed[...] - learn_rate * mm(step_inner, gram[...], NN, HIGH)
                if not after:
                    pass_leaves(k, 0)
                    mixed_t[...] = mixed_t[...] - learn_rate * mm(gram[...], step_inner, NT, HIGH)
                    from_mixed()
                else:
                    pass_leaves(k, 0)
                arrive(k, 1)
                for c in after:
                    pass_on(k, c, 1)
                if not after:
                    pass_leaves(k, 1)
                use(k)
                if after:
                    pass_leaves(k, 1)
                use_leaves(before)
                before = k
            use_leaves(before)

        return 0

    lax.fori_loop(0, ITERS, local_step, 0)

    own_three = jnp.concatenate([own[0], own[1]], axis=0)
    delta_in = own_three - own_zero
    out_cols = pl.ds(pl.multiple_of(z * width_out, 128), width_out)
    head_cols = head_ref[:, out_cols].astype(jnp.float32)
    delta_out = -learn_rate * mm(inner_sum[...], head_cols, NN, HIGH)
    delta = jnp.concatenate([delta_in, delta_out], axis=1)
    sums = jnp.sum(delta * delta, axis=0, keepdims=True)
    lanes = sums[:, :128]
    for j in range(1, width // 128):
        lanes = lanes + sums[:, j * 128 : (j + 1) * 128]
    squares = jnp.sum(lanes, axis=1, keepdims=True)
    weight = w_ref[0].astype(jnp.float32)

    mine = lax.broadcasted_iota(jnp.int32, (1, 128), 1) == client
    ends = jnp.concatenate(
        [jnp.where(mine, squares, 0.0), jnp.where(mine, weight, 0.0)], axis=1
    )
    for r in range(rank):
        row_out[r] = jnp.concatenate([delta[r : r + 1], ends], axis=1)

    def ro_copy(k, to_core, from_core):
        return pltpu.make_async_remote_copy(
            src_ref=row_out.at[at_chip(k)],
            dst_ref=row_in.at[client],
            send_sem=ro_send.at[k, to_core],
            recv_sem=ro_recv.at[k, from_core],
            device_id={"client": at_chip(k) * CORES + to_core},
            device_id_type=MESH,
        )

    for k in range(1, chips):
        for to_core in range(CORES):
            ro_copy(k, to_core, core).start()
    ro_copy(0, 1 - core, core).start()
    row_in[client] = row_out[chip]
    for k in range(1, chips):
        for from_core in range(CORES):
            ro_copy(k, from_core, from_core).wait_recv()
    ro_copy(0, 1 - core, 1 - core).wait_recv()
    ends = row_in[0][:, width:]
    for c in range(1, clients):
        ends = ends + row_in[c][:, width:]

    z_start(1, ends[:, :128])
    for piece in pieces[4:]:
        piece.wait()
    noise = jnp.concatenate(
        [nin_ref[pl.ds(chip, 1), :], nout_ref[pl.ds(chip, 1), :]], axis=1
    )
    weights = ends[:, 128:]
    wsum = jnp.sum(weights, axis=1, keepdims=True)
    scales = weights * jnp.minimum(1.0, clip_bound / jnp.sqrt(z_finish(1) + 1e-06))
    row = scales[:, :1] * row_in[0][:, :width]
    for c in range(1, clients):
        row = row + scales[:, c : c + 1] * row_in[c][:, :width]
    row_done[chip] = (row + noise_mult * clip_bound * noise) * out_scale / wsum

    def rd_copy(k):
        return pltpu.make_async_remote_copy(
            src_ref=row_done.at[chip],
            dst_ref=row_done.at[chip],
            send_sem=rd_send.at[k],
            recv_sem=rd_recv.at[k],
            device_id={"client": at_chip(k) * CORES + core},
            device_id_type=MESH,
        )

    for k in range(1, chips):
        rd_copy(k).start()

    def drain_step(it, _):
        for way, h in chains:
            for k in PARENT:
                if reaches(way, h, k):
                    rs_copy(it, way, h, k, z).wait_send()
        for stage in range(2):
            for j in range(1, BLOCK):
                inner_copy(it, stage, j).wait_send()

        @pl.when(it < ITERS - 1)
        def _():
            for way, h in chains:
                for k in PARENT:
                    if reaches(way, h, k):
                        ag_copy(it, way, h, k, z).wait_send()

        return 0

    lax.fori_loop(0, ITERS, drain_step, 0)

    for k in range(1, chips):
        for to_core in range(CORES):
            ro_copy(k, to_core, core).wait_send()
    ro_copy(0, 1 - core, core).wait_send()
    for k in range(1, chips):
        rd_copy(k).wait()
    for r in range(rank):
        row = row_done[r]
        oin_ref[r : r + 1, :] = row[:, :width_in]
        oout_ref[r : r + 1, :] = row[:, width_in:]


def on_device(
    n,
    clients,
    hidden,
    frozen_residual,
    head,
    global_input_factor,
    global_output_factor,
    counts,
    weights,
    input_privacy_noise,
    output_privacy_noise,
):
    tokens, hidden_units = hidden.shape[1:]
    nout = head.shape[1]
    rank, model_width = global_output_factor.shape
    width_in = input_privacy_noise.shape[1]
    width_out = output_privacy_noise.shape[1]
    half = rank // 2
    half_n = n // 2
    chips = clients // CORES
    width = width_in + width_out
    out_scale = math.sqrt(rank * (hidden_units + model_width)) / clip_bound
    f32 = jnp.float32
    dma = pltpu.SemaphoreType.DMA
    hbm = pl.BlockSpec(memory_space=pltpu.HBM)
    vmem = pl.BlockSpec(memory_space=pltpu.VMEM)
    smem = pl.BlockSpec(memory_space=pltpu.SMEM)
    return pl.pallas_call(
        functools.partial(kernel, n, clients, out_scale),
        out_shape=(
            jax.ShapeDtypeStruct((rank, width_in), f32),
            jax.ShapeDtypeStruct((rank, width_out), f32),
        ),
        in_specs=[
            hbm, hbm, hbm, hbm, hbm, smem, smem, hbm, hbm
        ],
        out_specs=(vmem, vmem),
        scratch_shapes=[
            pltpu.VMEM((nout, tokens), jnp.bfloat16),
            pltpu.VMEM((nout, model_width), jnp.bfloat16),
            pltpu.VMEM((rank, hidden_units), jnp.bfloat16),
            pltpu.VMEM((rank, model_width), jnp.bfloat16),
            pltpu.VMEM((rank, width_in), f32),
            pltpu.VMEM((rank, width_out), f32),
            pltpu.VMEM((n, tokens, width_in), jnp.bfloat16),
            pltpu.VMEM((nout, nout), f32),
            pltpu.VMEM((rank, nout), f32),
            pltpu.VMEM((nout, rank), f32),
            pltpu.VMEM((rank, nout), f32),
            pltpu.VMEM((1, tokens), f32),
            pltpu.VMEM((1, tokens), f32),
            pltpu.VMEM((tokens, rank), f32),
            pltpu.VMEM((rank, tokens), jnp.bfloat16),
            pltpu.VMEM((rank, rank), f32),
            pltpu.VMEM((rank, tokens), f32),
            pltpu.VMEM((ITERS, n, 2, half, width_in), f32),
            pltpu.VMEM((ITERS, 2, 2, half_n, half, width_in), f32),
            pltpu.VMEM((ITERS - 1, n, 2, half, width_in), f32),
            pltpu.VMEM((2, half, width_in), f32),
            pltpu.VMEM((ITERS, 2, half, 128), f32),
            pltpu.VMEM((ITERS, 2, BLOCK - 1, half, 128), f32),
            pltpu.VMEM((2, n, 1, 128), f32),
            pltpu.VMEM((rank, 1, width + 256), f32),
            pltpu.VMEM((clients, 1, width + 256), f32),
            pltpu.VMEM((rank, 1, width), f32),
            dma((6,)),
            dma((n,)),
            dma((ITERS, 2, 2, half_n)),
            dma((ITERS, 2, 2, half_n)),
            dma((ITERS - 1, 2, 2, half_n)),
            dma((ITERS - 1, 2, 2, half_n)),
            dma((ITERS, 2, BLOCK - 1)),
            dma((ITERS, 2, BLOCK - 1)),
            dma((2, n)),
            dma((2, n)),
            dma((chips, CORES)),
            dma((chips, CORES)),
            dma((chips,)),
            dma((chips,)),
        ],
        compiler_params=pltpu.CompilerParams(
            collective_id=0, has_side_effects=True, vmem_limit_bytes=VMEM_BYTES
        ),
    )(
        hidden,
        frozen_residual[0].T,
        head[0],
        global_input_factor,
        global_output_factor,
        counts,
        weights,
        input_privacy_noise,
        output_privacy_noise,
    )


def solution(mesh):
    in_specs = (
        P("client", "dp", None),
        P("client", "dp", None),
        P("client", None, None),
        P(),
        P(),
        P("client", "dp"),
        P("client"),
        P(None, "dp"),
        P(None, "dp"),
    )
    out_specs = (P(None, "dp"), P(None, "dp"))
    body = functools.partial(on_device, mesh.shape["dp"], mesh.shape["client"])
    return jax.shard_map(
        body, mesh=mesh, in_specs=in_specs, out_specs=out_specs, check_vma=False
    )
```

```python
import functools
import math

import jax
import jax.numpy as jnp
from jax import lax
from jax.experimental import pallas as pl
from jax.experimental.pallas import tpu as pltpu
from jax.sharding import PartitionSpec as P

ITERS = 3
CORES = 2
BLOCK = 4
VMEM_BYTES = 63 * 1024 * 1024

learn_rate = 0.1
clip_bound = 0.001
noise_mult = 0.1

PARENT = {8: 6, 7: 6, 6: 4, 5: 4, 4: 2, 3: 2, 2: 0, 1: 0}
CHILDREN = {p: [k for k in PARENT if PARENT[k] == p] for p in range(9)}
LEAVES = {p: [k for k in CHILDREN[p] if not CHILDREN[k]] for p in CHILDREN}
STOPS = [k for k in PARENT if CHILDREN[k]]

MESH = pl.DeviceIdType.MESH
HIGH = lax.Precision.HIGHEST
NN = (((1,), (0,)), ((), ()))
NT = (((1,), (1,)), ((), ()))
TN = (((0,), (0,)), ((), ()))


def mm(a, b, dims=NN, precision=None):
    return lax.dot_general(
        a, b, dims, precision=precision, preferred_element_type=jnp.float32
    )


def kernel(
    n,
    clients,
    out_scale,
    hid_ref,
    res_hbm,
    head_hbm,
    a0_hbm,
    b0_hbm,
    cnt_ref,
    w_ref,
    nin_hbm,
    nout_hbm,
    oin_ref,
    oout_ref,
    res_ref,
    head_ref,
    a0_ref,
    b0_ref,
    nin_ref,
    nout_ref,
    hv,
    gram,
    mixed,
    mixed_t,
    inner_sum,
    mask,
    tokens_live,
    proj,
    dproj,
    square,
    base_in,
    grad,
    slot,
    a_all,
    own,
    inner_out,
    inner_in,
    count_out,
    count_in,
    count_far,
    spread,
    row_out,
    row_in,
    row_done,
    op_sem,
    hid_sem,
    rs_send,
    rs_recv,
    ag_send,
    ag_recv,
    in_send,
    in_recv,
    ct_send,
    ct_recv,
    cf_send,
    cf_recv,
    sc_send,
    sc_recv,
    ro_send,
    ro_recv,
    rd_send,
    rd_recv,
):
    half_n = n // 2
    reach = n // 4
    chips = clients // CORES
    rank, width_in = nin_ref.shape
    width_out = nout_ref.shape[1]
    half = rank // 2
    nout = head_ref.shape[0]
    tokens = hv.shape[1]
    width = width_in + width_out

    z = lax.axis_index("dp")
    client = lax.axis_index("client")
    chip = lax.div(client, CORES)
    core = lax.rem(client, CORES)
    corner = lax.div(z, BLOCK) * BLOCK

    def at_z(k):
        return lax.rem(z + k, n)

    def at_chip(k):
        return lax.rem(chip + k, chips)

    barrier = pltpu.get_barrier_semaphore()
    for k in (reach, n - reach, *range(1, reach), *range(n - reach + 1, n)):
        pl.semaphore_signal(barrier, inc=1, device_id={"dp": at_z(k)}, device_id_type=MESH)
    for k in range(1, clients):
        pl.semaphore_signal(
            barrier, inc=1, device_id={"client": lax.rem(client + k, clients)}, device_id_type=MESH
        )

    def load(j):
        return pltpu.make_async_copy(
            hid_ref.at[0, :, pl.ds(j * width_in, width_in)], hv.at[j], hid_sem.at[j]
        )

    pieces = [
        pltpu.make_async_copy(src, dst, op_sem.at[i])
        for i, (src, dst) in enumerate(
            [
                (head_hbm, head_ref),
                (b0_hbm, b0_ref),
                (res_hbm, res_ref),
                (a0_hbm, a0_ref),
                (nin_hbm, nin_ref),
                (nout_hbm, nout_ref),
            ]
        )
    ]
    for piece in pieces[:4]:
        piece.start()
    for j in range(n):
        load(j).start()
    for piece in pieces[4:]:
        piece.start()

    for piece in pieces[:3]:
        piece.wait()
    head = head_ref[...]
    gram[...] = mm(head, head, NT)
    mixed[...] = mm(b0_ref[...], head, NT)
    mixed_t[...] = mm(head, b0_ref[...], NT)
    inner_sum[...] = jnp.zeros_like(inner_sum)

    def from_mixed():
        square[...] = mm(mixed[...], mixed[...], NT, HIGH)
        base_in[...] = mm(mixed[...], res_ref[...].astype(jnp.float32), NN, HIGH)

    from_mixed()

    lane = lax.broadcasted_iota(jnp.int32, (1, tokens), 1)
    live = cnt_ref[0, 0]

    pl.semaphore_wait(barrier, 2 * reach + (clients - 1))

    near = (*range(1, reach + 1), *range(n - reach, n))

    def count_copy(k):
        return pltpu.make_async_remote_copy(
            src_ref=count_out.at[0],
            dst_ref=count_in.at[n - k],
            send_sem=ct_send.at[k],
            recv_sem=ct_recv.at[n - k],
            device_id={"dp": at_z(k)},
            device_id_type=MESH,
        )

    def far_copy(way):
        return pltpu.make_async_remote_copy(
            src_ref=count_out.at[1 + way],
            dst_ref=count_far.at[way],
            send_sem=cf_send.at[way],
            recv_sem=cf_recv.at[way],
            device_id={"dp": at_z(n - reach) if way == 0 else at_z(reach)},
            device_id_type=MESH,
        )

    count_out[0] = jnp.full((1, 128), live.astype(jnp.float32), jnp.float32)
    for k in reversed(near):
        count_copy(k).start()

    pieces[3].wait()
    proj[...] = jnp.zeros_like(proj)

    def first(j, _):
        load(j).wait()
        cols = pl.ds(pl.multiple_of(j * width_in, 128), width_in)
        proj[...] += mm(hv[j], a0_ref[:, cols], NT)
        return 0

    lax.fori_loop(0, n, first, 0)

    start_cols = pl.ds(pl.multiple_of(z * width_in, 128), width_in)
    own_zero = a0_ref[:, start_cols].astype(jnp.float32)
    for h in range(2):
        own[h] = own_zero[h * half : (h + 1) * half]
    mask[...] = (lane < live).astype(jnp.float32)

    for k in near:
        count_copy(n - k).wait_recv()
    above = count_in[1]
    for k in range(2, reach + 1):
        above = above + count_in[k]
    below = count_in[n - 1]
    for k in range(2, reach):
        below = below + count_in[n - k]
    count_out[1] = above
    count_out[2] = below
    for way in range(2):
        far_copy(way).start()
    nearer = count_out[0] + above + below + count_in[n - reach]
    for way in range(2):
        far_copy(way).wait_recv()
    tokens_live[...] = nearer + count_far[0] + count_far[1]

    def toward(way, k):
        return at_z(n - k) if way == 0 else at_z(k)

    def rs_copy(it, way, h, k, owner):
        return pltpu.make_async_remote_copy(
            src_ref=grad.at[it, owner, h],
            dst_ref=slot.at[it, way, h, k - 1],
            send_sem=rs_send.at[it, way, h, k - 1],
            recv_sem=rs_recv.at[it, way, h, k - 1],
            device_id={"dp": toward(way, k - PARENT[k])},
            device_id_type=MESH,
        )

    def ag_copy(it, way, h, k, owner):
        return pltpu.make_async_remote_copy(
            src_ref=a_all.at[it, owner, h],
            dst_ref=a_all.at[it, owner, h],
            send_sem=ag_send.at[it, way, h, k - 1],
            recv_sem=ag_recv.at[it, way, h, k - 1],
            device_id={"dp": toward(way, k - PARENT[k])},
            device_id_type=MESH,
        )

    def inner_copy(it, stage, j):
        peer = at_z(j * BLOCK) if stage == 0 else corner + lax.rem(z - corner + j, BLOCK)
        return pltpu.make_async_remote_copy(
            src_ref=inner_out.at[it, stage],
            dst_ref=inner_in.at[it, stage, j - 1],
            send_sem=in_send.at[it, stage, j - 1],
            recv_sem=in_recv.at[it, stage, j - 1],
            device_id={"dp": peer},
            device_id_type=MESH,
        )

    def inner_start(it, stage, value):
        inner_out[it, stage] = value
        for j in range(1, BLOCK):
            inner_copy(it, stage, j).start()

    def inner_finish(it, stage):
        total = inner_out[it, stage]
        for j in range(1, BLOCK):
            inner_copy(it, stage, j).wait_recv()
            total = total + inner_in[it, stage, j - 1]
        return total

    def long(way, h):
        return way == h

    def reaches(way, h, k):
        return k < half_n or long(way, h)

    chains = ((0, 0), (1, 1), (0, 1), (1, 0))
    far = at_z(half_n)

    def local_step(it, _):
        weighted = mask[...] / tokens_live[...]
        through = mm(square[...], proj[...], NT, HIGH)
        dproj[...] = ((base_in[...] + through) * weighted).astype(jnp.bfloat16)

        def local(owner):
            value = mm(dproj[...], hv[owner])
            for h in range(2):
                grad[it, owner, h] = value[h * half : (h + 1) * half]

        def local_both(k):
            for way in range(2):
                local(toward(way, k))

        def send_raw(k, h):
            for way in range(2):
                if reaches(way, h, k):
                    rs_copy(it, way, h, k, toward(way, k)).start()

        def gather_terms(way, h, k, owner):
            total = grad[it, owner, h]
            for child in reversed(CHILDREN[k]):
                if reaches(way, h, child):
                    rs_copy(it, way, h, child, owner).wait_recv()
                    total = total + slot[it, way, h, child - 1]
            return total

        def send_on(way, h, k):
            owner = toward(way, k)
            grad[it, owner, h] = gather_terms(way, h, k, owner)
            rs_copy(it, way, h, k, owner).start()

        targets = STOPS + [0]

        def send_leaves(i):
            for k in LEAVES[targets[i]]:
                if k == half_n:
                    local(far)
                else:
                    local_both(k)
                for h in range(2):
                    send_raw(k, h)

        send_leaves(0)
        local_both(targets[0])
        send_leaves(1)
        proj_t = proj[...].T
        resid = res_ref[...].astype(jnp.float32) + mm(mixed_t[...], proj_t, NN, HIGH)
        inner = mm(proj_t, resid * weighted, NT, HIGH)
        inner_start(it, 0, jnp.concatenate([inner[:half], inner[half:]], axis=1))
        for i, k in enumerate(STOPS):
            for way, h in chains:
                send_on(way, h, k)
            if targets[i + 1]:
                local_both(targets[i + 1])
                send_leaves(i + 2)
            else:
                local(z)
            if i == len(STOPS) - 2:
                inner_start(it, 1, inner_finish(it, 0))
        for h in range(2):
            total = grad[it, z, h]
            for way in range(2):
                for child in CHILDREN[0]:
                    rs_copy(it, way, h, child, z).wait_recv()
                    total = total + slot[it, way, h, child - 1]
            own[h] = own[h] - learn_rate * total

            @pl.when(it < ITERS - 1)
            def _():
                a_all[it, z, h] = own[h]
                for way in range(2):
                    ag_copy(it, way, h, STOPS[-1], z).start()

        def inner_total():
            tile = inner_finish(it, 1)
            return jnp.concatenate([tile[:, :nout], tile[:, nout:]], axis=0)

        @pl.when(it == ITERS - 1)
        def _():
            inner_sum[...] += inner_total()

        @pl.when(it < ITERS - 1)
        def _():
            def project(owner):
                rows = jnp.concatenate([a_all[it, owner, 0], a_all[it, owner, 1]], axis=0)
                return mm(hv[owner], rows.astype(jnp.bfloat16), NT)

            def use(k):
                for way in range(2):
                    proj[...] += project(toward(1 - way, k))

            def arrive(way, h, k):
                if reaches(way, h, k):
                    ag_copy(it, way, h, k, toward(1 - way, k)).wait_recv()

            def pass_on(way, h, parent, k):
                if reaches(way, h, k):
                    ag_copy(it, way, h, k, toward(1 - way, parent)).start()

            def pass_leaves(parent):
                for k in LEAVES[parent]:
                    for way, h in chains:
                        pass_on(way, h, parent, k)

            def use_leaves(parent):
                for k in LEAVES[parent]:
                    for way, h in chains:
                        arrive(way, h, k)
                    if k == half_n:
                        proj[...] += project(far)
                    else:
                        use(k)

            pass_leaves(0)
            proj[...] = project(z)
            step_inner = inner_total()
            inner_sum[...] += step_inner
            mixed[...] = mixed[...] - learn_rate * mm(step_inner, gram[...], NN, HIGH)
            mixed_t[...] = mixed_t[...] - learn_rate * mm(gram[...], step_inner, NT, HIGH)
            from_mixed()
            before = 0
            for k in reversed(STOPS):
                for way, h in chains:
                    arrive(way, h, k)
                    for c in CHILDREN[k]:
                        if CHILDREN[c]:
                            pass_on(way, h, k, c)
                if k < STOPS[0]:
                    proj[...] += project(toward(1, k))
                pass_leaves(k)
                if k < STOPS[0]:
                    proj[...] += project(toward(0, k))
                else:
                    use(k)
                use_leaves(before)
                before = k
            use_leaves(before)

        return 0

    lax.fori_loop(0, ITERS, local_step, 0)

    def z_copy(k):
        return pltpu.make_async_remote_copy(
            src_ref=spread.at[z],
            dst_ref=spread.at[z],
            send_sem=sc_send.at[k],
            recv_sem=sc_recv.at[k],
            device_id={"dp": at_z(k)},
            device_id_type=MESH,
        )

    def z_start(row):
        spread[z] = row
        for k in sorted(range(1, n), key=lambda k: -min(k, n - k)):
            z_copy(k).start()

    def z_finish():
        for k in range(1, n):
            z_copy(k).wait()
        total = spread[0]
        for j in range(1, n):
            total = total + spread[j]
        return total

    own_three = jnp.concatenate([own[0], own[1]], axis=0)
    delta_in = own_three - own_zero
    out_cols = pl.ds(pl.multiple_of(z * width_out, 128), width_out)
    head_cols = head_ref[:, out_cols].astype(jnp.float32)
    delta_out = -learn_rate * mm(inner_sum[...], head_cols, NN, HIGH)
    delta = jnp.concatenate([delta_in, delta_out], axis=1)
    sums = jnp.sum(delta * delta, axis=0, keepdims=True)
    lanes = sums[:, :128]
    for j in range(1, width // 128):
        lanes = lanes + sums[:, j * 128 : (j + 1) * 128]
    squares = jnp.sum(lanes, axis=1, keepdims=True)
    weight = w_ref[0].astype(jnp.float32)

    mine = lax.broadcasted_iota(jnp.int32, (1, 128), 1) == client
    ends = jnp.concatenate(
        [jnp.where(mine, squares, 0.0), jnp.where(mine, weight, 0.0)], axis=1
    )
    for r in range(rank):
        row_out[r] = jnp.concatenate([delta[r : r + 1], ends], axis=1)

    def ro_copy(k, to_core, from_core):
        return pltpu.make_async_remote_copy(
            src_ref=row_out.at[at_chip(k)],
            dst_ref=row_in.at[client],
            send_sem=ro_send.at[k, to_core],
            recv_sem=ro_recv.at[k, from_core],
            device_id={"client": at_chip(k) * CORES + to_core},
            device_id_type=MESH,
        )

    for k in range(1, chips):
        for to_core in range(CORES):
            ro_copy(k, to_core, core).start()
    ro_copy(0, 1 - core, core).start()
    row_in[client] = row_out[chip]
    for k in range(1, chips):
        for from_core in range(CORES):
            ro_copy(k, from_core, from_core).wait_recv()
    ro_copy(0, 1 - core, 1 - core).wait_recv()
    ends = row_in[0][:, width:]
    for c in range(1, clients):
        ends = ends + row_in[c][:, width:]

    z_start(ends[:, :128])
    for piece in pieces[4:]:
        piece.wait()
    noise = jnp.concatenate(
        [nin_ref[pl.ds(chip, 1), :], nout_ref[pl.ds(chip, 1), :]], axis=1
    )
    weights = ends[:, 128:]
    wsum = jnp.sum(weights, axis=1, keepdims=True)
    scales = weights * jnp.minimum(1.0, clip_bound / jnp.sqrt(z_finish() + 1e-06))
    row = scales[:, :1] * row_in[0][:, :width]
    for c in range(1, clients):
        row = row + scales[:, c : c + 1] * row_in[c][:, :width]
    row_done[chip] = (row + noise_mult * clip_bound * noise) * out_scale / wsum

    def rd_copy(k):
        return pltpu.make_async_remote_copy(
            src_ref=row_done.at[chip],
            dst_ref=row_done.at[chip],
            send_sem=rd_send.at[k],
            recv_sem=rd_recv.at[k],
            device_id={"client": at_chip(k) * CORES + core},
            device_id_type=MESH,
        )

    for k in range(1, chips):
        rd_copy(k).start()

    def drain_step(it, _):
        for way, h in chains:
            for k in PARENT:
                if reaches(way, h, k):
                    rs_copy(it, way, h, k, z).wait_send()
        for stage in range(2):
            for j in range(1, BLOCK):
                inner_copy(it, stage, j).wait_send()

        @pl.when(it < ITERS - 1)
        def _():
            for way, h in chains:
                for k in PARENT:
                    if reaches(way, h, k):
                        ag_copy(it, way, h, k, z).wait_send()

        return 0

    lax.fori_loop(0, ITERS, drain_step, 0)
    for k in near:
        count_copy(k).wait_send()
    for way in range(2):
        far_copy(way).wait_send()

    for k in range(1, chips):
        for to_core in range(CORES):
            ro_copy(k, to_core, core).wait_send()
    ro_copy(0, 1 - core, core).wait_send()
    for k in range(1, chips):
        rd_copy(k).wait()
    for r in range(rank):
        row = row_done[r]
        oin_ref[r : r + 1, :] = row[:, :width_in]
        oout_ref[r : r + 1, :] = row[:, width_in:]


def on_device(
    n,
    clients,
    hidden,
    frozen_residual,
    head,
    global_input_factor,
    global_output_factor,
    counts,
    weights,
    input_privacy_noise,
    output_privacy_noise,
):
    tokens, hidden_units = hidden.shape[1:]
    nout = head.shape[1]
    rank, model_width = global_output_factor.shape
    width_in = input_privacy_noise.shape[1]
    width_out = output_privacy_noise.shape[1]
    half = rank // 2
    half_n = n // 2
    chips = clients // CORES
    width = width_in + width_out
    out_scale = math.sqrt(rank * (hidden_units + model_width)) / clip_bound
    f32 = jnp.float32
    dma = pltpu.SemaphoreType.DMA
    hbm = pl.BlockSpec(memory_space=pltpu.HBM)
    vmem = pl.BlockSpec(memory_space=pltpu.VMEM)
    smem = pl.BlockSpec(memory_space=pltpu.SMEM)
    return pl.pallas_call(
        functools.partial(kernel, n, clients, out_scale),
        out_shape=(
            jax.ShapeDtypeStruct((rank, width_in), f32),
            jax.ShapeDtypeStruct((rank, width_out), f32),
        ),
        in_specs=[
            hbm, hbm, hbm, hbm, hbm, smem, smem, hbm, hbm
        ],
        out_specs=(vmem, vmem),
        scratch_shapes=[
            pltpu.VMEM((nout, tokens), jnp.bfloat16),
            pltpu.VMEM((nout, model_width), jnp.bfloat16),
            pltpu.VMEM((rank, hidden_units), jnp.bfloat16),
            pltpu.VMEM((rank, model_width), jnp.bfloat16),
            pltpu.VMEM((rank, width_in), f32),
            pltpu.VMEM((rank, width_out), f32),
            pltpu.VMEM((n, tokens, width_in), jnp.bfloat16),
            pltpu.VMEM((nout, nout), f32),
            pltpu.VMEM((rank, nout), f32),
            pltpu.VMEM((nout, rank), f32),
            pltpu.VMEM((rank, nout), f32),
            pltpu.VMEM((1, tokens), f32),
            pltpu.VMEM((1, tokens), f32),
            pltpu.VMEM((tokens, rank), f32),
            pltpu.VMEM((rank, tokens), jnp.bfloat16),
            pltpu.VMEM((rank, rank), f32),
            pltpu.VMEM((rank, tokens), f32),
            pltpu.VMEM((ITERS, n, 2, half, width_in), f32),
            pltpu.VMEM((ITERS, 2, 2, half_n, half, width_in), f32),
            pltpu.VMEM((ITERS - 1, n, 2, half, width_in), f32),
            pltpu.VMEM((2, half, width_in), f32),
            pltpu.VMEM((ITERS, 2, half, 128), f32),
            pltpu.VMEM((ITERS, 2, BLOCK - 1, half, 128), f32),
            pltpu.VMEM((3, 1, 128), f32),
            pltpu.VMEM((n, 1, 128), f32),
            pltpu.VMEM((2, 1, 128), f32),
            pltpu.VMEM((n, 1, 128), f32),
            pltpu.VMEM((rank, 1, width + 256), f32),
            pltpu.VMEM((clients, 1, width + 256), f32),
            pltpu.VMEM((rank, 1, width), f32),
            dma((6,)),
            dma((n,)),
            dma((ITERS, 2, 2, half_n)),
            dma((ITERS, 2, 2, half_n)),
            dma((ITERS - 1, 2, 2, half_n)),
            dma((ITERS - 1, 2, 2, half_n)),
            dma((ITERS, 2, BLOCK - 1)),
            dma((ITERS, 2, BLOCK - 1)),
            dma((n,)),
            dma((n,)),
            dma((2,)),
            dma((2,)),
            dma((n,)),
            dma((n,)),
            dma((chips, CORES)),
            dma((chips, CORES)),
            dma((chips,)),
            dma((chips,)),
        ],
        compiler_params=pltpu.CompilerParams(
            collective_id=0, has_side_effects=True, vmem_limit_bytes=VMEM_BYTES
        ),
    )(
        hidden,
        frozen_residual[0].T,
        head[0],
        global_input_factor,
        global_output_factor,
        counts,
        weights,
        input_privacy_noise,
        output_privacy_noise,
    )


def solution(mesh):
    in_specs = (
        P("client", "dp", None),
        P("client", "dp", None),
        P("client", None, None),
        P(),
        P(),
        P("client", "dp"),
        P("client"),
        P(None, "dp"),
        P(None, "dp"),
    )
    out_specs = (P(None, "dp"), P(None, "dp"))
    body = functools.partial(on_device, mesh.shape["dp"], mesh.shape["client"])
    return jax.shard_map(
        body, mesh=mesh, in_specs=in_specs, out_specs=out_specs, check_vma=False
    )
```

```python
import functools
import math

import jax
import jax.numpy as jnp
from jax import lax
from jax.experimental import pallas as pl
from jax.experimental.pallas import tpu as pltpu
from jax.sharding import PartitionSpec as P

ITERS = 3
CORES = 2
BLOCK = 4
VMEM_BYTES = 63 * 1024 * 1024

learn_rate = 0.1
clip_bound = 0.001
noise_mult = 0.1

PARENT = {8: 6, 7: 6, 6: 4, 5: 4, 4: 2, 3: 2, 2: 0, 1: 0}
CHILDREN = {p: [k for k in PARENT if PARENT[k] == p] for p in range(9)}
LEAVES = {p: [k for k in CHILDREN[p] if not CHILDREN[k]] for p in CHILDREN}
STOPS = [k for k in PARENT if CHILDREN[k]]

MESH = pl.DeviceIdType.MESH
HIGH = lax.Precision.HIGHEST
NN = (((1,), (0,)), ((), ()))
NT = (((1,), (1,)), ((), ()))
TN = (((0,), (0,)), ((), ()))


def mm(a, b, dims=NN, precision=None):
    return lax.dot_general(
        a, b, dims, precision=precision, preferred_element_type=jnp.float32
    )


def kernel(
    n,
    clients,
    out_scale,
    hid_ref,
    res_hbm,
    head_hbm,
    a0_hbm,
    b0_hbm,
    cnt_ref,
    w_ref,
    nin_hbm,
    nout_hbm,
    oin_ref,
    oout_ref,
    res_ref,
    head_ref,
    a0_ref,
    b0_ref,
    nin_ref,
    nout_ref,
    hv,
    gram,
    mixed,
    mixed_t,
    inner_sum,
    mask,
    tokens_live,
    proj,
    dproj,
    square,
    base_in,
    grad,
    slot,
    a_all,
    own,
    inner_out,
    inner_in,
    spread,
    row_out,
    row_in,
    row_done,
    op_sem,
    hid_sem,
    rs_send,
    rs_recv,
    ag_send,
    ag_recv,
    in_send,
    in_recv,
    sc_send,
    sc_recv,
    ro_send,
    ro_recv,
    rd_send,
    rd_recv,
):
    half_n = n // 2
    chips = clients // CORES
    rank, width_in = nin_ref.shape
    width_out = nout_ref.shape[1]
    half = rank // 2
    nout = head_ref.shape[0]
    tokens = hv.shape[1]
    width = width_in + width_out

    z = lax.axis_index("dp")
    client = lax.axis_index("client")
    chip = lax.div(client, CORES)
    core = lax.rem(client, CORES)
    corner = lax.div(z, BLOCK) * BLOCK

    def at_z(k):
        return lax.rem(z + k, n)

    def at_chip(k):
        return lax.rem(chip + k, chips)

    def load(j):
        return pltpu.make_async_copy(
            hid_ref.at[0, :, pl.ds(j * width_in, width_in)], hv.at[j], hid_sem.at[j]
        )

    pieces = [
        pltpu.make_async_copy(src, dst, op_sem.at[i])
        for i, (src, dst) in enumerate(
            [
                (head_hbm, head_ref),
                (b0_hbm, b0_ref),
                (res_hbm, res_ref),
                (a0_hbm, a0_ref),
                (nin_hbm, nin_ref),
                (nout_hbm, nout_ref),
            ]
        )
    ]
    for piece in pieces[:4]:
        piece.start()
    for j in range(n):
        load(j).start()
    for piece in pieces[4:]:
        piece.start()

    barrier = pltpu.get_barrier_semaphore()
    for k in range(1, n):
        pl.semaphore_signal(barrier, inc=1, device_id={"dp": at_z(k)}, device_id_type=MESH)
    for k in range(1, clients):
        pl.semaphore_signal(
            barrier, inc=1, device_id={"client": lax.rem(client + k, clients)}, device_id_type=MESH
        )

    for piece in pieces[:3]:
        piece.wait()
    head = head_ref[...]
    gram[...] = mm(head, head, NT)
    mixed[...] = mm(b0_ref[...], head, NT)
    mixed_t[...] = mm(head, b0_ref[...], NT)
    inner_sum[...] = jnp.zeros_like(inner_sum)

    def from_mixed():
        square[...] = mm(mixed[...], mixed[...], NT, HIGH)
        base_in[...] = mm(mixed[...], res_ref[...].astype(jnp.float32), NN, HIGH)

    from_mixed()

    lane = lax.broadcasted_iota(jnp.int32, (1, tokens), 1)
    live = cnt_ref[0, 0]

    pl.semaphore_wait(barrier, (n - 1) + (clients - 1))

    def z_copy(which, k):
        return pltpu.make_async_remote_copy(
            src_ref=spread.at[which, z],
            dst_ref=spread.at[which, z],
            send_sem=sc_send.at[which, k],
            recv_sem=sc_recv.at[which, k],
            device_id={"dp": at_z(k)},
            device_id_type=MESH,
        )

    def z_start(which, row):
        spread[which, z] = row
        for k in range(1, n):
            z_copy(which, k).start()

    def z_finish(which):
        for k in range(1, n):
            z_copy(which, k).wait()
        total = spread[which, 0]
        for j in range(1, n):
            total = total + spread[which, j]
        return total

    z_start(0, jnp.full((1, 128), live.astype(jnp.float32), jnp.float32))

    pieces[3].wait()
    proj[...] = jnp.zeros_like(proj)

    def first(j, _):
        load(j).wait()
        cols = pl.ds(pl.multiple_of(j * width_in, 128), width_in)
        proj[...] += mm(hv[j], a0_ref[:, cols], NT)
        return 0

    lax.fori_loop(0, n, first, 0)

    start_cols = pl.ds(pl.multiple_of(z * width_in, 128), width_in)
    own_zero = a0_ref[:, start_cols].astype(jnp.float32)
    for h in range(2):
        own[h] = own_zero[h * half : (h + 1) * half]
    mask[...] = (lane < live).astype(jnp.float32)
    tokens_live[...] = z_finish(0)

    def toward(way, k):
        return at_z(n - k) if way == 0 else at_z(k)

    def rs_copy(it, way, h, k, owner):
        return pltpu.make_async_remote_copy(
            src_ref=grad.at[it, owner, h],
            dst_ref=slot.at[it, way, h, k - 1],
            send_sem=rs_send.at[it, way, h, k - 1],
            recv_sem=rs_recv.at[it, way, h, k - 1],
            device_id={"dp": toward(way, k - PARENT[k])},
            device_id_type=MESH,
        )

    def ag_copy(it, way, h, k, owner):
        return pltpu.make_async_remote_copy(
            src_ref=a_all.at[it, owner, h],
            dst_ref=a_all.at[it, owner, h],
            send_sem=ag_send.at[it, way, h, k - 1],
            recv_sem=ag_recv.at[it, way, h, k - 1],
            device_id={"dp": toward(way, k - PARENT[k])},
            device_id_type=MESH,
        )

    def inner_copy(it, stage, j):
        peer = at_z(j * BLOCK) if stage == 0 else corner + lax.rem(z - corner + j, BLOCK)
        return pltpu.make_async_remote_copy(
            src_ref=inner_out.at[it, stage],
            dst_ref=inner_in.at[it, stage, j - 1],
            send_sem=in_send.at[it, stage, j - 1],
            recv_sem=in_recv.at[it, stage, j - 1],
            device_id={"dp": peer},
            device_id_type=MESH,
        )

    def inner_start(it, stage, value):
        inner_out[it, stage] = value
        for j in range(1, BLOCK):
            inner_copy(it, stage, j).start()

    def inner_finish(it, stage):
        total = inner_out[it, stage]
        for j in range(1, BLOCK):
            inner_copy(it, stage, j).wait_recv()
            total = total + inner_in[it, stage, j - 1]
        return total

    def long(way, h):
        return way == h

    def reaches(way, h, k):
        return k < half_n or long(way, h)

    chains = ((0, 0), (1, 1), (0, 1), (1, 0))
    far = at_z(half_n)

    def local_step(it, _):
        weighted = mask[...] / tokens_live[...]
        through = mm(square[...], proj[...], NT, HIGH)
        dproj[...] = ((base_in[...] + through) * weighted).astype(jnp.bfloat16)

        def local(owner):
            value = mm(dproj[...], hv[owner])
            for h in range(2):
                grad[it, owner, h] = value[h * half : (h + 1) * half]

        def local_both(k):
            for way in range(2):
                local(toward(way, k))

        def send_raw(k, h):
            for way in range(2):
                if reaches(way, h, k):
                    rs_copy(it, way, h, k, toward(way, k)).start()

        def gather_terms(way, h, k, owner):
            total = grad[it, owner, h]
            for child in reversed(CHILDREN[k]):
                if reaches(way, h, child):
                    rs_copy(it, way, h, child, owner).wait_recv()
                    total = total + slot[it, way, h, child - 1]
            return total

        def send_on(way, h, k):
            owner = toward(way, k)
            grad[it, owner, h] = gather_terms(way, h, k, owner)
            rs_copy(it, way, h, k, owner).start()

        def left(h, *places):
            for k in places:
                for way in range(2):
                    if reaches(way, h, k):
                        rs_copy(it, way, h, k, z).wait_send()

        local(far)
        send_raw(8, 0)
        local_both(7)
        send_raw(7, 0)
        local_both(6)
        left(0, 8, 7)
        send_raw(8, 1)
        send_raw(7, 1)
        local_both(5)
        proj_t = proj[...].T
        resid = res_ref[...].astype(jnp.float32) + mm(mixed_t[...], proj_t, NN, HIGH)
        inner = mm(proj_t, resid * weighted, NT, HIGH)
        left(1, 8, 7)
        send_raw(5, 0)
        send_raw(5, 1)
        inner_start(it, 0, jnp.concatenate([inner[:half], inner[half:]], axis=1))
        for k in STOPS:
            for way in range(2):
                send_on(way, 0, k)
            if k > 2:
                local_both(k - 2)
            else:
                local(z)
            left(0, k)
            for way in range(2):
                send_on(way, 1, k)
            if k > 2:
                local_both(k - 3)
                left(1, k)
                for h in range(2):
                    send_raw(k - 3, h)
            if k == 4:
                inner_start(it, 1, inner_finish(it, 0))
        for h in range(2):
            total = grad[it, z, h]
            for way in range(2):
                for child in CHILDREN[0]:
                    rs_copy(it, way, h, child, z).wait_recv()
                    total = total + slot[it, way, h, child - 1]
            own[h] = own[h] - learn_rate * total

            @pl.when(it < ITERS - 1)
            def _():
                a_all[it, z, h] = own[h]
                for way in range(2):
                    ag_copy(it, way, h, STOPS[-1], z).start()

        def inner_total():
            tile = inner_finish(it, 1)
            return jnp.concatenate([tile[:, :nout], tile[:, nout:]], axis=0)

        @pl.when(it == ITERS - 1)
        def _():
            inner_sum[...] += inner_total()

        @pl.when(it < ITERS - 1)
        def _():
            def project(owner):
                rows = jnp.concatenate([a_all[it, owner, 0], a_all[it, owner, 1]], axis=0)
                return mm(hv[owner], rows.astype(jnp.bfloat16), NT)

            def use(k):
                for way in range(2):
                    proj[...] += project(toward(1 - way, k))

            def arrive(k, h):
                for way in range(2):
                    if reaches(way, h, k):
                        ag_copy(it, way, h, k, toward(1 - way, k)).wait_recv()

            def pass_on(parent, k, h):
                for way in range(2):
                    if reaches(way, h, k):
                        ag_copy(it, way, h, k, toward(1 - way, parent)).start()

            def pass_leaves(parent, h):
                for k in LEAVES[parent]:
                    pass_on(parent, k, h)

            def use_leaves(parent):
                for k in LEAVES[parent]:
                    arrive(k, 0)
                    arrive(k, 1)
                    if k == half_n:
                        proj[...] += project(far)
                    else:
                        use(k)

            def gone(h, k):
                for way in range(2):
                    ag_copy(it, way, h, k, z).wait_send()

            proj[...] = project(z)
            step_inner = inner_total()
            inner_sum[...] += step_inner
            gone(0, STOPS[-1])
            gone(1, STOPS[-1])
            pass_leaves(0, 0)
            pass_leaves(0, 1)
            mixed[...] = mixed[...] - learn_rate * mm(step_inner, gram[...], NN, HIGH)
            mixed_t[...] = mixed_t[...] - learn_rate * mm(gram[...], step_inner, NT, HIGH)
            passed = [0]
            for k in reversed(STOPS):
                onward = [c for c in CHILDREN[k] if CHILDREN[c]]
                arrive(k, 0)
                for c in onward or LEAVES[k]:
                    pass_on(k, c, 0)
                if k == STOPS[-1]:
                    from_mixed()
                else:
                    use_leaves(passed[-2])
                for c in onward:
                    gone(0, c)
                arrive(k, 1)
                for c in onward or LEAVES[k]:
                    pass_on(k, c, 1)
                use(k)
                if onward:
                    for c in onward:
                        gone(1, c)
                    pass_leaves(k, 0)
                    pass_leaves(k, 1)
                passed.append(k)
            use_leaves(passed[-2])
            use_leaves(passed[-1])

        return 0

    lax.fori_loop(0, ITERS, local_step, 0)

    own_three = jnp.concatenate([own[0], own[1]], axis=0)
    delta_in = own_three - own_zero
    out_cols = pl.ds(pl.multiple_of(z * width_out, 128), width_out)
    head_cols = head_ref[:, out_cols].astype(jnp.float32)
    delta_out = -learn_rate * mm(inner_sum[...], head_cols, NN, HIGH)
    delta = jnp.concatenate([delta_in, delta_out], axis=1)
    sums = jnp.sum(delta * delta, axis=0, keepdims=True)
    lanes = sums[:, :128]
    for j in range(1, width // 128):
        lanes = lanes + sums[:, j * 128 : (j + 1) * 128]
    squares = jnp.sum(lanes, axis=1, keepdims=True)
    weight = w_ref[0].astype(jnp.float32)

    mine = lax.broadcasted_iota(jnp.int32, (1, 128), 1) == client
    ends = jnp.concatenate(
        [jnp.where(mine, squares, 0.0), jnp.where(mine, weight, 0.0)], axis=1
    )
    for r in range(rank):
        row_out[r] = jnp.concatenate([delta[r : r + 1], ends], axis=1)

    def ro_copy(k, to_core, from_core):
        return pltpu.make_async_remote_copy(
            src_ref=row_out.at[at_chip(k)],
            dst_ref=row_in.at[client],
            send_sem=ro_send.at[k, to_core],
            recv_sem=ro_recv.at[k, from_core],
            device_id={"client": at_chip(k) * CORES + to_core},
            device_id_type=MESH,
        )

    for k in range(1, chips):
        for to_core in range(CORES):
            ro_copy(k, to_core, core).start()
    ro_copy(0, 1 - core, core).start()
    row_in[client] = row_out[chip]
    for k in range(1, chips):
        for from_core in range(CORES):
            ro_copy(k, from_core, from_core).wait_recv()
    ro_copy(0, 1 - core, 1 - core).wait_recv()
    ends = row_in[0][:, width:]
    for c in range(1, clients):
        ends = ends + row_in[c][:, width:]

    z_start(1, ends[:, :128])
    for piece in pieces[4:]:
        piece.wait()
    noise = jnp.concatenate(
        [nin_ref[pl.ds(chip, 1), :], nout_ref[pl.ds(chip, 1), :]], axis=1
    )
    weights = ends[:, 128:]
    wsum = jnp.sum(weights, axis=1, keepdims=True)
    scales = weights * jnp.minimum(1.0, clip_bound / jnp.sqrt(z_finish(1) + 1e-06))
    row = scales[:, :1] * row_in[0][:, :width]
    for c in range(1, clients):
        row = row + scales[:, c : c + 1] * row_in[c][:, :width]
    row_done[chip] = (row + noise_mult * clip_bound * noise) * out_scale / wsum

    def rd_copy(k):
        return pltpu.make_async_remote_copy(
            src_ref=row_done.at[chip],
            dst_ref=row_done.at[chip],
            send_sem=rd_send.at[k],
            recv_sem=rd_recv.at[k],
            device_id={"client": at_chip(k) * CORES + core},
            device_id_type=MESH,
        )

    for k in range(1, chips):
        rd_copy(k).start()

    def drain_step(it, _):
        for way, h in chains:
            for k in (5, 3, 1):
                rs_copy(it, way, h, k, z).wait_send()
            if h == 1:
                rs_copy(it, way, h, STOPS[-1], z).wait_send()
        for stage in range(2):
            for j in range(1, BLOCK):
                inner_copy(it, stage, j).wait_send()

        @pl.when(it < ITERS - 1)
        def _():
            for way, h in chains:
                for k in (8, 7, 5, 3, 1):
                    if reaches(way, h, k):
                        ag_copy(it, way, h, k, z).wait_send()

        return 0

    lax.fori_loop(0, ITERS, drain_step, 0)

    for k in range(1, chips):
        for to_core in range(CORES):
            ro_copy(k, to_core, core).wait_send()
    ro_copy(0, 1 - core, core).wait_send()
    for k in range(1, chips):
        rd_copy(k).wait()
    for r in range(rank):
        row = row_done[r]
        oin_ref[r : r + 1, :] = row[:, :width_in]
        oout_ref[r : r + 1, :] = row[:, width_in:]


def on_device(
    n,
    clients,
    hidden,
    frozen_residual,
    head,
    global_input_factor,
    global_output_factor,
    counts,
    weights,
    input_privacy_noise,
    output_privacy_noise,
):
    tokens, hidden_units = hidden.shape[1:]
    nout = head.shape[1]
    rank, model_width = global_output_factor.shape
    width_in = input_privacy_noise.shape[1]
    width_out = output_privacy_noise.shape[1]
    half = rank // 2
    half_n = n // 2
    chips = clients // CORES
    width = width_in + width_out
    out_scale = math.sqrt(rank * (hidden_units + model_width)) / clip_bound
    f32 = jnp.float32
    dma = pltpu.SemaphoreType.DMA
    hbm = pl.BlockSpec(memory_space=pltpu.HBM)
    vmem = pl.BlockSpec(memory_space=pltpu.VMEM)
    smem = pl.BlockSpec(memory_space=pltpu.SMEM)
    return pl.pallas_call(
        functools.partial(kernel, n, clients, out_scale),
        out_shape=(
            jax.ShapeDtypeStruct((rank, width_in), f32),
            jax.ShapeDtypeStruct((rank, width_out), f32),
        ),
        in_specs=[
            hbm, hbm, hbm, hbm, hbm, smem, smem, hbm, hbm
        ],
        out_specs=(vmem, vmem),
        scratch_shapes=[
            pltpu.VMEM((nout, tokens), jnp.bfloat16),
            pltpu.VMEM((nout, model_width), jnp.bfloat16),
            pltpu.VMEM((rank, hidden_units), jnp.bfloat16),
            pltpu.VMEM((rank, model_width), jnp.bfloat16),
            pltpu.VMEM((rank, width_in), f32),
            pltpu.VMEM((rank, width_out), f32),
            pltpu.VMEM((n, tokens, width_in), jnp.bfloat16),
            pltpu.VMEM((nout, nout), f32),
            pltpu.VMEM((rank, nout), f32),
            pltpu.VMEM((nout, rank), f32),
            pltpu.VMEM((rank, nout), f32),
            pltpu.VMEM((1, tokens), f32),
            pltpu.VMEM((1, tokens), f32),
            pltpu.VMEM((tokens, rank), f32),
            pltpu.VMEM((rank, tokens), jnp.bfloat16),
            pltpu.VMEM((rank, rank), f32),
            pltpu.VMEM((rank, tokens), f32),
            pltpu.VMEM((ITERS, n, 2, half, width_in), f32),
            pltpu.VMEM((ITERS, 2, 2, half_n, half, width_in), f32),
            pltpu.VMEM((ITERS - 1, n, 2, half, width_in), f32),
            pltpu.VMEM((2, half, width_in), f32),
            pltpu.VMEM((ITERS, 2, half, 128), f32),
            pltpu.VMEM((ITERS, 2, BLOCK - 1, half, 128), f32),
            pltpu.VMEM((2, n, 1, 128), f32),
            pltpu.VMEM((rank, 1, width + 256), f32),
            pltpu.VMEM((clients, 1, width + 256), f32),
            pltpu.VMEM((rank, 1, width), f32),
            dma((6,)),
            dma((n,)),
            dma((ITERS, 2, 2, half_n)),
            dma((ITERS, 2, 2, half_n)),
            dma((ITERS - 1, 2, 2, half_n)),
            dma((ITERS - 1, 2, 2, half_n)),
            dma((ITERS, 2, BLOCK - 1)),
            dma((ITERS, 2, BLOCK - 1)),
            dma((2, n)),
            dma((2, n)),
            dma((chips, CORES)),
            dma((chips, CORES)),
            dma((chips,)),
            dma((chips,)),
        ],
        compiler_params=pltpu.CompilerParams(
            collective_id=0, has_side_effects=True, vmem_limit_bytes=VMEM_BYTES
        ),
    )(
        hidden,
        frozen_residual[0].T,
        head[0],
        global_input_factor,
        global_output_factor,
        counts,
        weights,
        input_privacy_noise,
        output_privacy_noise,
    )


def solution(mesh):
    in_specs = (
        P("client", "dp", None),
        P("client", "dp", None),
        P("client", None, None),
        P(),
        P(),
        P("client", "dp"),
        P("client"),
        P(None, "dp"),
        P(None, "dp"),
    )
    out_specs = (P(None, "dp"), P(None, "dp"))
    body = functools.partial(on_device, mesh.shape["dp"], mesh.shape["client"])
    return jax.shard_map(
        body, mesh=mesh, in_specs=in_specs, out_specs=out_specs, check_vma=False
    )
```

```python
import functools
import math

import jax
import jax.numpy as jnp
from jax import lax
from jax.experimental import pallas as pl
from jax.experimental.pallas import tpu as pltpu
from jax.sharding import PartitionSpec as P

ITERS = 3
CORES = 2
BLOCK = 4
VMEM_BYTES = 63 * 1024 * 1024

learn_rate = 0.1
clip_bound = 0.001
noise_mult = 0.1

PARENT = {8: 7, 7: 6, 6: 5, 5: 4, 4: 2, 3: 2, 2: 0, 1: 0}
CHILDREN = {p: [k for k in PARENT if PARENT[k] == p] for p in range(9)}
CHAIN = (8, 7, 6, 5, 4, 2)

MESH = pl.DeviceIdType.MESH
HIGH = lax.Precision.HIGHEST
NN = (((1,), (0,)), ((), ()))
NT = (((1,), (1,)), ((), ()))
TN = (((0,), (0,)), ((), ()))


def mm(a, b, dims=NN, precision=None):
    return lax.dot_general(
        a, b, dims, precision=precision, preferred_element_type=jnp.float32
    )


def kernel(
    n,
    clients,
    out_scale,
    hid_ref,
    res_hbm,
    head_hbm,
    a0_hbm,
    b0_hbm,
    cnt_ref,
    w_ref,
    nin_hbm,
    nout_hbm,
    oin_ref,
    oout_ref,
    res_ref,
    head_ref,
    a0_ref,
    b0_ref,
    nin_ref,
    nout_ref,
    hv,
    gram,
    mixed,
    mixed_t,
    inner_sum,
    mask,
    tokens_live,
    proj,
    dproj,
    square,
    base_in,
    grad,
    slot,
    a_all,
    own,
    inner_out,
    inner_in,
    spread,
    row_out,
    row_in,
    row_done,
    op_sem,
    hid_sem,
    rs_send,
    rs_recv,
    ag_send,
    ag_recv,
    in_send,
    in_recv,
    sc_send,
    sc_recv,
    ro_send,
    ro_recv,
    rd_send,
    rd_recv,
):
    half_n = n // 2
    chips = clients // CORES
    rank, width_in = nin_ref.shape
    width_out = nout_ref.shape[1]
    half = rank // 2
    nout = head_ref.shape[0]
    tokens = hv.shape[1]
    width = width_in + width_out

    z = lax.axis_index("dp")
    client = lax.axis_index("client")
    chip = lax.div(client, CORES)
    core = lax.rem(client, CORES)
    corner = lax.div(z, BLOCK) * BLOCK

    def at_z(k):
        return lax.rem(z + k, n)

    def at_chip(k):
        return lax.rem(chip + k, chips)

    def load(j):
        return pltpu.make_async_copy(
            hid_ref.at[0, :, pl.ds(j * width_in, width_in)], hv.at[j], hid_sem.at[j]
        )

    pieces = [
        pltpu.make_async_copy(src, dst, op_sem.at[i])
        for i, (src, dst) in enumerate(
            [
                (head_hbm, head_ref),
                (b0_hbm, b0_ref),
                (res_hbm, res_ref),
                (a0_hbm, a0_ref),
                (nin_hbm, nin_ref),
                (nout_hbm, nout_ref),
            ]
        )
    ]
    for piece in pieces[:4]:
        piece.start()
    for j in range(n):
        load(j).start()
    for piece in pieces[4:]:
        piece.start()

    barrier = pltpu.get_barrier_semaphore()
    for k in range(1, n):
        pl.semaphore_signal(barrier, inc=1, device_id={"dp": at_z(k)}, device_id_type=MESH)
    for k in range(1, clients):
        pl.semaphore_signal(
            barrier, inc=1, device_id={"client": lax.rem(client + k, clients)}, device_id_type=MESH
        )

    for piece in pieces[:3]:
        piece.wait()
    head = head_ref[...]
    gram[...] = mm(head, head, NT)
    mixed[...] = mm(b0_ref[...], head, NT)
    mixed_t[...] = mm(head, b0_ref[...], NT)
    inner_sum[...] = jnp.zeros_like(inner_sum)

    def from_mixed():
        square[...] = mm(mixed[...], mixed[...], NT, HIGH)
        base_in[...] = mm(mixed[...], res_ref[...].astype(jnp.float32), NN, HIGH)

    from_mixed()

    lane = lax.broadcasted_iota(jnp.int32, (1, tokens), 1)
    live = cnt_ref[0, 0]

    pl.semaphore_wait(barrier, (n - 1) + (clients - 1))

    def z_copy(which, k):
        return pltpu.make_async_remote_copy(
            src_ref=spread.at[which, z],
            dst_ref=spread.at[which, z],
            send_sem=sc_send.at[which, k],
            recv_sem=sc_recv.at[which, k],
            device_id={"dp": at_z(k)},
            device_id_type=MESH,
        )

    def z_start(which, row):
        spread[which, z] = row
        for k in range(1, n):
            z_copy(which, k).start()

    def z_finish(which):
        for k in range(1, n):
            z_copy(which, k).wait()
        total = spread[which, 0]
        for j in range(1, n):
            total = total + spread[which, j]
        return total

    z_start(0, jnp.full((1, 128), live.astype(jnp.float32), jnp.float32))

    pieces[3].wait()
    proj[...] = jnp.zeros_like(proj)

    def first(j, _):
        load(j).wait()
        cols = pl.ds(pl.multiple_of(j * width_in, 128), width_in)
        proj[...] += mm(hv[j], a0_ref[:, cols], NT)
        return 0

    lax.fori_loop(0, n, first, 0)

    start_cols = pl.ds(pl.multiple_of(z * width_in, 128), width_in)
    own_zero = a0_ref[:, start_cols].astype(jnp.float32)
    for h in range(2):
        own[h] = own_zero[h * half : (h + 1) * half]
    mask[...] = (lane < live).astype(jnp.float32)
    tokens_live[...] = z_finish(0)

    def toward(way, k):
        return at_z(n - k) if way == 0 else at_z(k)

    def rs_copy(it, way, h, k, owner):
        return pltpu.make_async_remote_copy(
            src_ref=grad.at[it, owner, h],
            dst_ref=slot.at[it, way, h, k - 1],
            send_sem=rs_send.at[it, way, h, k - 1],
            recv_sem=rs_recv.at[it, way, h, k - 1],
            device_id={"dp": toward(way, k - PARENT[k])},
            device_id_type=MESH,
        )

    def ag_copy(it, way, h, k, owner):
        return pltpu.make_async_remote_copy(
            src_ref=a_all.at[it, owner, h],
            dst_ref=a_all.at[it, owner, h],
            send_sem=ag_send.at[it, way, h, k - 1],
            recv_sem=ag_recv.at[it, way, h, k - 1],
            device_id={"dp": toward(way, k - PARENT[k])},
            device_id_type=MESH,
        )

    def inner_copy(it, stage, j):
        peer = at_z(j * BLOCK) if stage == 0 else corner + lax.rem(z - corner + j, BLOCK)
        return pltpu.make_async_remote_copy(
            src_ref=inner_out.at[it, stage],
            dst_ref=inner_in.at[it, stage, j - 1],
            send_sem=in_send.at[it, stage, j - 1],
            recv_sem=in_recv.at[it, stage, j - 1],
            device_id={"dp": peer},
            device_id_type=MESH,
        )

    def inner_start(it, stage, value):
        inner_out[it, stage] = value
        for j in range(1, BLOCK):
            inner_copy(it, stage, j).start()

    def inner_finish(it, stage):
        total = inner_out[it, stage]
        for j in range(1, BLOCK):
            inner_copy(it, stage, j).wait_recv()
            total = total + inner_in[it, stage, j - 1]
        return total

    def long(way, h):
        return way == h

    def reaches(way, h, k):
        return k < half_n or long(way, h)

    chains = ((0, 0), (1, 1), (0, 1), (1, 0))
    far = at_z(half_n)

    def local_step(it, _):
        weighted = mask[...] / tokens_live[...]
        through = mm(square[...], proj[...], NT, HIGH)
        dproj[...] = ((base_in[...] + through) * weighted).astype(jnp.bfloat16)

        def local(owner):
            value = mm(dproj[...], hv[owner])
            for h in range(2):
                grad[it, owner, h] = value[h * half : (h + 1) * half]

        def local_both(k):
            for way in range(2):
                local(toward(way, k))

        def send_raw(k, h):
            for way in range(2):
                if reaches(way, h, k):
                    rs_copy(it, way, h, k, toward(way, k)).start()

        def gather_terms(way, h, k, owner):
            total = grad[it, owner, h]
            for child in reversed(CHILDREN[k]):
                if reaches(way, h, child):
                    rs_copy(it, way, h, child, owner).wait_recv()
                    total = total + slot[it, way, h, child - 1]
            return total

        def send_on(way, h, k):
            owner = toward(way, k)
            grad[it, owner, h] = gather_terms(way, h, k, owner)
            rs_copy(it, way, h, k, owner).start()

        def step(h, i):
            send_on(h, h, CHAIN[i])
            if i + 1 < len(CHAIN):
                send_on(1 - h, h, CHAIN[i + 1])

        local(far)
        send_raw(8, 0)
        local_both(7)
        rs_copy(it, 1, 0, 7, toward(1, 7)).start()
        local_both(6)
        proj_t = proj[...].T
        resid = res_ref[...].astype(jnp.float32) + mm(mixed_t[...], proj_t, NN, HIGH)
        inner = mm(proj_t, resid * weighted, NT, HIGH)
        send_raw(8, 1)
        rs_copy(it, 0, 1, 7, toward(0, 7)).start()
        inner_start(it, 0, jnp.concatenate([inner[:half], inner[half:]], axis=1))
        local_both(5)
        step(0, 1)
        local_both(4)
        local_both(3)
        send_raw(3, 0)
        step(1, 1)
        send_raw(3, 1)
        step(0, 2)
        local_both(2)
        local_both(1)
        send_raw(1, 0)
        step(1, 2)
        send_raw(1, 1)
        step(0, 3)
        local(z)
        step(1, 3)
        step(0, 4)
        inner_start(it, 1, inner_finish(it, 0))
        step(1, 4)
        step(0, 5)
        step(1, 5)
        for h in range(2):
            total = grad[it, z, h]
            for way in range(2):
                for child in CHILDREN[0]:
                    rs_copy(it, way, h, child, z).wait_recv()
                    total = total + slot[it, way, h, child - 1]
            own[h] = own[h] - learn_rate * total

            @pl.when(it < ITERS - 1)
            def _():
                a_all[it, z, h] = own[h]
                for way in range(2):
                    ag_copy(it, way, h, CHAIN[-1], z).start()

        def inner_total():
            tile = inner_finish(it, 1)
            return jnp.concatenate([tile[:, :nout], tile[:, nout:]], axis=0)

        @pl.when(it == ITERS - 1)
        def _():
            inner_sum[...] += inner_total()

        @pl.when(it < ITERS - 1)
        def _():
            def project(owner):
                rows = jnp.concatenate([a_all[it, owner, 0], a_all[it, owner, 1]], axis=0)
                return mm(hv[owner], rows.astype(jnp.bfloat16), NT)

            def use(k):
                for way in range(2):
                    proj[...] += project(toward(1 - way, k))

            def arrive(way, h, k):
                if reaches(way, h, k):
                    ag_copy(it, way, h, k, toward(1 - way, k)).wait_recv()

            def pass_on(way, h, parent, k):
                if reaches(way, h, k):
                    ag_copy(it, way, h, k, toward(1 - way, parent)).start()

            def relay(h, k, onward):
                for way in (h, 1 - h):
                    arrive(way, h, k)
                    pass_on(way, h, k, onward)

            def use_leaf(k):
                for way, h in chains:
                    arrive(way, h, k)
                use(k)

            for way, h in chains:
                pass_on(way, h, 0, 1)
            proj[...] = project(z)
            step_inner = inner_total()
            inner_sum[...] += step_inner
            mixed[...] = mixed[...] - learn_rate * mm(step_inner, gram[...], NN, HIGH)
            relay(0, 2, 4)
            mixed_t[...] = mixed_t[...] - learn_rate * mm(gram[...], step_inner, NT, HIGH)
            relay(1, 2, 4)
            for way, h in chains:
                pass_on(way, h, 2, 3)
            use(2)
            from_mixed()
            relay(0, 4, 5)
            use_leaf(1)
            relay(1, 4, 5)
            use(4)
            relay(0, 5, 6)
            use_leaf(3)
            relay(1, 5, 6)
            use(5)
            relay(0, 6, 7)
            relay(1, 6, 7)
            use(6)
            relay(0, 7, 8)
            relay(1, 7, 8)
            use(7)
            arrive(0, 0, 8)
            arrive(1, 1, 8)
            proj[...] += project(far)

        return 0

    lax.fori_loop(0, ITERS, local_step, 0)

    own_three = jnp.concatenate([own[0], own[1]], axis=0)
    delta_in = own_three - own_zero
    out_cols = pl.ds(pl.multiple_of(z * width_out, 128), width_out)
    head_cols = head_ref[:, out_cols].astype(jnp.float32)
    delta_out = -learn_rate * mm(inner_sum[...], head_cols, NN, HIGH)
    delta = jnp.concatenate([delta_in, delta_out], axis=1)
    sums = jnp.sum(delta * delta, axis=0, keepdims=True)
    lanes = sums[:, :128]
    for j in range(1, width // 128):
        lanes = lanes + sums[:, j * 128 : (j + 1) * 128]
    squares = jnp.sum(lanes, axis=1, keepdims=True)
    weight = w_ref[0].astype(jnp.float32)

    mine = lax.broadcasted_iota(jnp.int32, (1, 128), 1) == client
    ends = jnp.concatenate(
        [jnp.where(mine, squares, 0.0), jnp.where(mine, weight, 0.0)], axis=1
    )
    for r in range(rank):
        row_out[r] = jnp.concatenate([delta[r : r + 1], ends], axis=1)

    def ro_copy(k, to_core, from_core):
        return pltpu.make_async_remote_copy(
            src_ref=row_out.at[at_chip(k)],
            dst_ref=row_in.at[client],
            send_sem=ro_send.at[k, to_core],
            recv_sem=ro_recv.at[k, from_core],
            device_id={"client": at_chip(k) * CORES + to_core},
            device_id_type=MESH,
        )

    for k in range(1, chips):
        for to_core in range(CORES):
            ro_copy(k, to_core, core).start()
    ro_copy(0, 1 - core, core).start()
    row_in[client] = row_out[chip]
    for k in range(1, chips):
        for from_core in range(CORES):
            ro_copy(k, from_core, from_core).wait_recv()
    ro_copy(0, 1 - core, 1 - core).wait_recv()
    ends = row_in[0][:, width:]
    for c in range(1, clients):
        ends = ends + row_in[c][:, width:]

    z_start(1, ends[:, :128])
    for piece in pieces[4:]:
        piece.wait()
    noise = jnp.concatenate(
        [nin_ref[pl.ds(chip, 1), :], nout_ref[pl.ds(chip, 1), :]], axis=1
    )
    weights = ends[:, 128:]
    wsum = jnp.sum(weights, axis=1, keepdims=True)
    scales = weights * jnp.minimum(1.0, clip_bound / jnp.sqrt(z_finish(1) + 1e-06))
    row = scales[:, :1] * row_in[0][:, :width]
    for c in range(1, clients):
        row = row + scales[:, c : c + 1] * row_in[c][:, :width]
    row_done[chip] = (row + noise_mult * clip_bound * noise) * out_scale / wsum

    def rd_copy(k):
        return pltpu.make_async_remote_copy(
            src_ref=row_done.at[chip],
            dst_ref=row_done.at[chip],
            send_sem=rd_send.at[k],
            recv_sem=rd_recv.at[k],
            device_id={"client": at_chip(k) * CORES + core},
            device_id_type=MESH,
        )

    for k in range(1, chips):
        rd_copy(k).start()

    def drain_step(it, _):
        for way, h in chains:
            for k in PARENT:
                if reaches(way, h, k):
                    rs_copy(it, way, h, k, z).wait_send()
        for stage in range(2):
            for j in range(1, BLOCK):
                inner_copy(it, stage, j).wait_send()

        @pl.when(it < ITERS - 1)
        def _():
            for way, h in chains:
                for k in PARENT:
                    if reaches(way, h, k):
                        ag_copy(it, way, h, k, z).wait_send()

        return 0

    lax.fori_loop(0, ITERS, drain_step, 0)

    for k in range(1, chips):
        for to_core in range(CORES):
            ro_copy(k, to_core, core).wait_send()
    ro_copy(0, 1 - core, core).wait_send()
    for k in range(1, chips):
        rd_copy(k).wait()
    for r in range(rank):
        row = row_done[r]
        oin_ref[r : r + 1, :] = row[:, :width_in]
        oout_ref[r : r + 1, :] = row[:, width_in:]


def on_device(
    n,
    clients,
    hidden,
    frozen_residual,
    head,
    global_input_factor,
    global_output_factor,
    counts,
    weights,
    input_privacy_noise,
    output_privacy_noise,
):
    tokens, hidden_units = hidden.shape[1:]
    nout = head.shape[1]
    rank, model_width = global_output_factor.shape
    width_in = input_privacy_noise.shape[1]
    width_out = output_privacy_noise.shape[1]
    half = rank // 2
    half_n = n // 2
    chips = clients // CORES
    width = width_in + width_out
    out_scale = math.sqrt(rank * (hidden_units + model_width)) / clip_bound
    f32 = jnp.float32
    dma = pltpu.SemaphoreType.DMA
    hbm = pl.BlockSpec(memory_space=pltpu.HBM)
    vmem = pl.BlockSpec(memory_space=pltpu.VMEM)
    smem = pl.BlockSpec(memory_space=pltpu.SMEM)
    return pl.pallas_call(
        functools.partial(kernel, n, clients, out_scale),
        out_shape=(
            jax.ShapeDtypeStruct((rank, width_in), f32),
            jax.ShapeDtypeStruct((rank, width_out), f32),
        ),
        in_specs=[
            hbm, hbm, hbm, hbm, hbm, smem, smem, hbm, hbm
        ],
        out_specs=(vmem, vmem),
        scratch_shapes=[
            pltpu.VMEM((nout, tokens), jnp.bfloat16),
            pltpu.VMEM((nout, model_width), jnp.bfloat16),
            pltpu.VMEM((rank, hidden_units), jnp.bfloat16),
            pltpu.VMEM((rank, model_width), jnp.bfloat16),
            pltpu.VMEM((rank, width_in), f32),
            pltpu.VMEM((rank, width_out), f32),
            pltpu.VMEM((n, tokens, width_in), jnp.bfloat16),
            pltpu.VMEM((nout, nout), f32),
            pltpu.VMEM((rank, nout), f32),
            pltpu.VMEM((nout, rank), f32),
            pltpu.VMEM((rank, nout), f32),
            pltpu.VMEM((1, tokens), f32),
            pltpu.VMEM((1, tokens), f32),
            pltpu.VMEM((tokens, rank), f32),
            pltpu.VMEM((rank, tokens), jnp.bfloat16),
            pltpu.VMEM((rank, rank), f32),
            pltpu.VMEM((rank, tokens), f32),
            pltpu.VMEM((ITERS, n, 2, half, width_in), f32),
            pltpu.VMEM((ITERS, 2, 2, half_n, half, width_in), f32),
            pltpu.VMEM((ITERS - 1, n, 2, half, width_in), f32),
            pltpu.VMEM((2, half, width_in), f32),
            pltpu.VMEM((ITERS, 2, half, 128), f32),
            pltpu.VMEM((ITERS, 2, BLOCK - 1, half, 128), f32),
            pltpu.VMEM((2, n, 1, 128), f32),
            pltpu.VMEM((rank, 1, width + 256), f32),
            pltpu.VMEM((clients, 1, width + 256), f32),
            pltpu.VMEM((rank, 1, width), f32),
            dma((6,)),
            dma((n,)),
            dma((ITERS, 2, 2, half_n)),
            dma((ITERS, 2, 2, half_n)),
            dma((ITERS - 1, 2, 2, half_n)),
            dma((ITERS - 1, 2, 2, half_n)),
            dma((ITERS, 2, BLOCK - 1)),
            dma((ITERS, 2, BLOCK - 1)),
            dma((2, n)),
            dma((2, n)),
            dma((chips, CORES)),
            dma((chips, CORES)),
            dma((chips,)),
            dma((chips,)),
        ],
        compiler_params=pltpu.CompilerParams(
            collective_id=0, has_side_effects=True, vmem_limit_bytes=VMEM_BYTES
        ),
    )(
        hidden,
        frozen_residual[0].T,
        head[0],
        global_input_factor,
        global_output_factor,
        counts,
        weights,
        input_privacy_noise,
        output_privacy_noise,
    )


def solution(mesh):
    in_specs = (
        P("client", "dp", None),
        P("client", "dp", None),
        P("client", None, None),
        P(),
        P(),
        P("client", "dp"),
        P("client"),
        P(None, "dp"),
        P(None, "dp"),
    )
    out_specs = (P(None, "dp"), P(None, "dp"))
    body = functools.partial(on_device, mesh.shape["dp"], mesh.shape["client"])
    return jax.shard_map(
        body, mesh=mesh, in_specs=in_specs, out_specs=out_specs, check_vma=False
    )
```

```python
import functools
import math

import jax
import jax.numpy as jnp
from jax import lax
from jax.experimental import pallas as pl
from jax.experimental.pallas import tpu as pltpu
from jax.sharding import PartitionSpec as P

ITERS = 3
CORES = 2
BLOCK = 4
VMEM_BYTES = 63 * 1024 * 1024

learn_rate = 0.1
clip_bound = 0.001
noise_mult = 0.1

PARENT = {8: 6, 7: 6, 6: 4, 5: 4, 4: 2, 3: 2, 2: 0, 1: 0}
CHILDREN = {p: [k for k in PARENT if PARENT[k] == p] for p in range(9)}
LEAVES = {p: [k for k in CHILDREN[p] if not CHILDREN[k]] for p in CHILDREN}
STOPS = [k for k in PARENT if CHILDREN[k]]

MESH = pl.DeviceIdType.MESH
HIGH = lax.Precision.HIGHEST
NN = (((1,), (0,)), ((), ()))
NT = (((1,), (1,)), ((), ()))
TN = (((0,), (0,)), ((), ()))


def mm(a, b, dims=NN, precision=None):
    return lax.dot_general(
        a, b, dims, precision=precision, preferred_element_type=jnp.float32
    )


def kernel(
    n,
    clients,
    out_scale,
    hid_ref,
    res_hbm,
    head_hbm,
    a0_hbm,
    b0_hbm,
    cnt_ref,
    w_ref,
    nin_hbm,
    nout_hbm,
    oin_ref,
    oout_ref,
    res_ref,
    head_ref,
    a0_ref,
    b0_ref,
    nin_ref,
    nout_ref,
    hv,
    gram,
    mixed,
    mixed_t,
    inner_sum,
    mask,
    tokens_live,
    proj,
    dproj,
    square,
    base_in,
    grad,
    slot,
    a_all,
    own,
    inner_out,
    inner_in,
    spread,
    row_out,
    row_in,
    row_done,
    op_sem,
    hid_sem,
    rs_send,
    rs_recv,
    ag_send,
    ag_recv,
    in_send,
    in_recv,
    sc_send,
    sc_recv,
    ro_send,
    ro_recv,
    rd_send,
    rd_recv,
):
    half_n = n // 2
    chips = clients // CORES
    rank, width_in = nin_ref.shape
    width_out = nout_ref.shape[1]
    half = rank // 2
    nout = head_ref.shape[0]
    tokens = hv.shape[1]
    width = width_in + width_out

    z = lax.axis_index("dp")
    client = lax.axis_index("client")
    chip = lax.div(client, CORES)
    core = lax.rem(client, CORES)
    corner = lax.div(z, BLOCK) * BLOCK

    def at_z(k):
        return lax.rem(z + k, n)

    def at_chip(k):
        return lax.rem(chip + k, chips)

    def load(j):
        return pltpu.make_async_copy(
            hid_ref.at[0, :, pl.ds(j * width_in, width_in)], hv.at[j], hid_sem.at[j]
        )

    pieces = [
        pltpu.make_async_copy(src, dst, op_sem.at[i])
        for i, (src, dst) in enumerate(
            [
                (head_hbm, head_ref),
                (b0_hbm, b0_ref),
                (res_hbm, res_ref),
                (a0_hbm, a0_ref),
                (nin_hbm, nin_ref),
                (nout_hbm, nout_ref),
            ]
        )
    ]
    for piece in pieces[:4]:
        piece.start()
    for j in range(n):
        load(j).start()
    for piece in pieces[4:]:
        piece.start()

    barrier = pltpu.get_barrier_semaphore()
    for k in range(1, n):
        pl.semaphore_signal(barrier, inc=1, device_id={"dp": at_z(k)}, device_id_type=MESH)
    for k in range(1, clients):
        pl.semaphore_signal(
            barrier, inc=1, device_id={"client": lax.rem(client + k, clients)}, device_id_type=MESH
        )

    for piece in pieces[:3]:
        piece.wait()
    head = head_ref[...]
    gram[...] = mm(head, head, NT)
    mixed[...] = mm(b0_ref[...], head, NT)
    mixed_t[...] = mm(head, b0_ref[...], NT)
    inner_sum[...] = jnp.zeros_like(inner_sum)

    def from_mixed():
        square[...] = mm(mixed[...], mixed[...], NT, HIGH)
        base_in[...] = mm(mixed[...], res_ref[...].astype(jnp.float32), NN, HIGH)

    from_mixed()

    lane = lax.broadcasted_iota(jnp.int32, (1, tokens), 1)
    live = cnt_ref[0, 0]

    pl.semaphore_wait(barrier, (n - 1) + (clients - 1))

    def z_copy(which, k):
        return pltpu.make_async_remote_copy(
            src_ref=spread.at[which, z],
            dst_ref=spread.at[which, z],
            send_sem=sc_send.at[which, k],
            recv_sem=sc_recv.at[which, k],
            device_id={"dp": at_z(k)},
            device_id_type=MESH,
        )

    def z_start(which, row):
        spread[which, z] = row
        for k in range(1, n):
            z_copy(which, k).start()

    def z_finish(which):
        for k in range(1, n):
            z_copy(which, k).wait()
        total = spread[which, 0]
        for j in range(1, n):
            total = total + spread[which, j]
        return total

    z_start(0, jnp.full((1, 128), live.astype(jnp.float32), jnp.float32))

    pieces[3].wait()
    proj[...] = jnp.zeros_like(proj)

    def first(j, _):
        load(j).wait()
        cols = pl.ds(pl.multiple_of(j * width_in, 128), width_in)
        proj[...] += mm(hv[j], a0_ref[:, cols], NT)
        return 0

    lax.fori_loop(0, n, first, 0)

    start_cols = pl.ds(pl.multiple_of(z * width_in, 128), width_in)
    own_zero = a0_ref[:, start_cols].astype(jnp.float32)
    for h in range(2):
        own[h] = own_zero[h * half : (h + 1) * half]
    mask[...] = (lane < live).astype(jnp.float32)
    tokens_live[...] = z_finish(0)

    def toward(way, k):
        return at_z(n - k) if way == 0 else at_z(k)

    def chunk(ref, way, k):
        return ref.at[way] if k == half_n else ref

    def rs_copy(it, way, k, owner):
        return pltpu.make_async_remote_copy(
            src_ref=chunk(grad.at[it, owner], way, k),
            dst_ref=chunk(slot.at[it, way, k - 1], way, k),
            send_sem=rs_send.at[it, way, k - 1],
            recv_sem=rs_recv.at[it, way, k - 1],
            device_id={"dp": toward(way, k - PARENT[k])},
            device_id_type=MESH,
        )

    def ag_copy(it, way, k, owner):
        return pltpu.make_async_remote_copy(
            src_ref=chunk(a_all.at[it, owner], way, k),
            dst_ref=chunk(a_all.at[it, owner], way, k),
            send_sem=ag_send.at[it, way, k - 1],
            recv_sem=ag_recv.at[it, way, k - 1],
            device_id={"dp": toward(way, k - PARENT[k])},
            device_id_type=MESH,
        )

    def inner_copy(it, stage, j):
        peer = at_z(j * BLOCK) if stage == 0 else corner + lax.rem(z - corner + j, BLOCK)
        return pltpu.make_async_remote_copy(
            src_ref=inner_out.at[it, stage],
            dst_ref=inner_in.at[it, stage, j - 1],
            send_sem=in_send.at[it, stage, j - 1],
            recv_sem=in_recv.at[it, stage, j - 1],
            device_id={"dp": peer},
            device_id_type=MESH,
        )

    def inner_start(it, stage, value):
        inner_out[it, stage] = value
        for j in range(1, BLOCK):
            inner_copy(it, stage, j).start()

    def inner_finish(it, stage):
        total = inner_out[it, stage]
        for j in range(1, BLOCK):
            inner_copy(it, stage, j).wait_recv()
            total = total + inner_in[it, stage, j - 1]
        return total

    far = at_z(half_n)

    def local_step(it, _):
        weighted = mask[...] / tokens_live[...]
        through = mm(square[...], proj[...], NT, HIGH)
        dproj[...] = ((base_in[...] + through) * weighted).astype(jnp.bfloat16)

        def local(owner):
            value = mm(dproj[...], hv[owner])
            for h in range(2):
                grad[it, owner, h] = value[h * half : (h + 1) * half]

        def local_both(k):
            for way in range(2):
                local(toward(way, k))

        def add_terms(way, k, owner, total):
            for child in reversed(CHILDREN[k]):
                rs_copy(it, way, child, owner).wait_recv()
                for h in range(2):
                    if child < half_n or h == way:
                        total[h] = total[h] + slot[it, way, child - 1, h]
            return total

        def send_on(way, k):
            owner = toward(way, k)
            total = add_terms(way, k, owner, [grad[it, owner, h] for h in range(2)])
            for h in range(2):
                grad[it, owner, h] = total[h]
            rs_copy(it, way, k, owner).start()

        targets = STOPS + [0]

        def send_leaves(i):
            for k in LEAVES[targets[i]]:
                if k == half_n:
                    local(far)
                else:
                    local_both(k)
                for way in range(2):
                    rs_copy(it, way, k, toward(way, k)).start()

        send_leaves(0)
        local_both(targets[0])
        send_leaves(1)
        proj_t = proj[...].T
        resid = res_ref[...].astype(jnp.float32) + mm(mixed_t[...], proj_t, NN, HIGH)
        inner = mm(proj_t, resid * weighted, NT, HIGH)
        inner_start(it, 0, jnp.concatenate([inner[:half], inner[half:]], axis=1))
        for i, k in enumerate(STOPS):
            for way in range(2):
                send_on(way, k)
            if targets[i + 1]:
                local_both(targets[i + 1])
                send_leaves(i + 2)
            else:
                local(z)
            if i == len(STOPS) - 2:
                inner_start(it, 1, inner_finish(it, 0))
        total = [grad[it, z, h] for h in range(2)]
        for way in range(2):
            total = add_terms(way, 0, z, total)
        for h in range(2):
            own[h] = own[h] - learn_rate * total[h]

        @pl.when(it < ITERS - 1)
        def _():
            for h in range(2):
                a_all[it, z, h] = own[h]
            for way in range(2):
                ag_copy(it, way, STOPS[-1], z).start()

        def inner_total():
            tile = inner_finish(it, 1)
            return jnp.concatenate([tile[:, :nout], tile[:, nout:]], axis=0)

        @pl.when(it == ITERS - 1)
        def _():
            inner_sum[...] += inner_total()

        @pl.when(it < ITERS - 1)
        def _():
            def project(owner):
                rows = jnp.concatenate([a_all[it, owner, 0], a_all[it, owner, 1]], axis=0)
                return mm(hv[owner], rows.astype(jnp.bfloat16), NT)

            def use(k):
                for way in range(2):
                    proj[...] += project(toward(1 - way, k))

            def arrive(way, k):
                ag_copy(it, way, k, toward(1 - way, k)).wait_recv()

            def pass_on(way, parent, k):
                ag_copy(it, way, k, toward(1 - way, parent)).start()

            def pass_leaves(parent):
                for k in LEAVES[parent]:
                    for way in range(2):
                        pass_on(way, parent, k)

            def use_leaves(parent):
                for k in LEAVES[parent]:
                    for way in range(2):
                        arrive(way, k)
                    if k == half_n:
                        proj[...] += project(far)
                    else:
                        use(k)

            pass_leaves(0)
            proj[...] = project(z)
            step_inner = inner_total()
            inner_sum[...] += step_inner
            mixed[...] = mixed[...] - learn_rate * mm(step_inner, gram[...], NN, HIGH)
            mixed_t[...] = mixed_t[...] - learn_rate * mm(gram[...], step_inner, NT, HIGH)
            from_mixed()
            before = 0
            for k in reversed(STOPS):
                for way in range(2):
                    arrive(way, k)
                    for c in CHILDREN[k]:
                        if CHILDREN[c]:
                            pass_on(way, k, c)
                if k < STOPS[0]:
                    proj[...] += project(toward(1, k))
                pass_leaves(k)
                if k < STOPS[0]:
                    proj[...] += project(toward(0, k))
                else:
                    use(k)
                use_leaves(before)
                before = k
            use_leaves(before)

        return 0

    lax.fori_loop(0, ITERS, local_step, 0)

    own_three = jnp.concatenate([own[0], own[1]], axis=0)
    delta_in = own_three - own_zero
    out_cols = pl.ds(pl.multiple_of(z * width_out, 128), width_out)
    head_cols = head_ref[:, out_cols].astype(jnp.float32)
    delta_out = -learn_rate * mm(inner_sum[...], head_cols, NN, HIGH)
    delta = jnp.concatenate([delta_in, delta_out], axis=1)
    sums = jnp.sum(delta * delta, axis=0, keepdims=True)
    lanes = sums[:, :128]
    for j in range(1, width // 128):
        lanes = lanes + sums[:, j * 128 : (j + 1) * 128]
    squares = jnp.sum(lanes, axis=1, keepdims=True)
    weight = w_ref[0].astype(jnp.float32)

    mine = lax.broadcasted_iota(jnp.int32, (1, 128), 1) == client
    ends = jnp.concatenate(
        [jnp.where(mine, squares, 0.0), jnp.where(mine, weight, 0.0)], axis=1
    )
    for r in range(rank):
        row_out[r] = jnp.concatenate([delta[r : r + 1], ends], axis=1)

    def ro_copy(k, to_core, from_core):
        return pltpu.make_async_remote_copy(
            src_ref=row_out.at[at_chip(k)],
            dst_ref=row_in.at[client],
            send_sem=ro_send.at[k, to_core],
            recv_sem=ro_recv.at[k, from_core],
            device_id={"client": at_chip(k) * CORES + to_core},
            device_id_type=MESH,
        )

    for k in range(1, chips):
        for to_core in range(CORES):
            ro_copy(k, to_core, core).start()
    ro_copy(0, 1 - core, core).start()
    row_in[client] = row_out[chip]
    for k in range(1, chips):
        for from_core in range(CORES):
            ro_copy(k, from_core, from_core).wait_recv()
    ro_copy(0, 1 - core, 1 - core).wait_recv()
    ends = row_in[0][:, width:]
    for c in range(1, clients):
        ends = ends + row_in[c][:, width:]

    z_start(1, ends[:, :128])
    for piece in pieces[4:]:
        piece.wait()
    noise = jnp.concatenate(
        [nin_ref[pl.ds(chip, 1), :], nout_ref[pl.ds(chip, 1), :]], axis=1
    )
    weights = ends[:, 128:]
    wsum = jnp.sum(weights, axis=1, keepdims=True)
    scales = weights * jnp.minimum(1.0, clip_bound / jnp.sqrt(z_finish(1) + 1e-06))
    row = scales[:, :1] * row_in[0][:, :width]
    for c in range(1, clients):
        row = row + scales[:, c : c + 1] * row_in[c][:, :width]
    row_done[chip] = (row + noise_mult * clip_bound * noise) * out_scale / wsum

    def rd_copy(k):
        return pltpu.make_async_remote_copy(
            src_ref=row_done.at[chip],
            dst_ref=row_done.at[chip],
            send_sem=rd_send.at[k],
            recv_sem=rd_recv.at[k],
            device_id={"client": at_chip(k) * CORES + core},
            device_id_type=MESH,
        )

    for k in range(1, chips):
        rd_copy(k).start()

    def drain_step(it, _):
        for way in range(2):
            for k in PARENT:
                rs_copy(it, way, k, z).wait_send()
        for stage in range(2):
            for j in range(1, BLOCK):
                inner_copy(it, stage, j).wait_send()

        @pl.when(it < ITERS - 1)
        def _():
            for way in range(2):
                for k in PARENT:
                    ag_copy(it, way, k, z).wait_send()

        return 0

    lax.fori_loop(0, ITERS, drain_step, 0)

    for k in range(1, chips):
        for to_core in range(CORES):
            ro_copy(k, to_core, core).wait_send()
    ro_copy(0, 1 - core, core).wait_send()
    for k in range(1, chips):
        rd_copy(k).wait()
    for r in range(rank):
        row = row_done[r]
        oin_ref[r : r + 1, :] = row[:, :width_in]
        oout_ref[r : r + 1, :] = row[:, width_in:]


def on_device(
    n,
    clients,
    hidden,
    frozen_residual,
    head,
    global_input_factor,
    global_output_factor,
    counts,
    weights,
    input_privacy_noise,
    output_privacy_noise,
):
    tokens, hidden_units = hidden.shape[1:]
    nout = head.shape[1]
    rank, model_width = global_output_factor.shape
    width_in = input_privacy_noise.shape[1]
    width_out = output_privacy_noise.shape[1]
    half = rank // 2
    half_n = n // 2
    chips = clients // CORES
    width = width_in + width_out
    out_scale = math.sqrt(rank * (hidden_units + model_width)) / clip_bound
    f32 = jnp.float32
    dma = pltpu.SemaphoreType.DMA
    hbm = pl.BlockSpec(memory_space=pltpu.HBM)
    vmem = pl.BlockSpec(memory_space=pltpu.VMEM)
    smem = pl.BlockSpec(memory_space=pltpu.SMEM)
    return pl.pallas_call(
        functools.partial(kernel, n, clients, out_scale),
        out_shape=(
            jax.ShapeDtypeStruct((rank, width_in), f32),
            jax.ShapeDtypeStruct((rank, width_out), f32),
        ),
        in_specs=[
            hbm, hbm, hbm, hbm, hbm, smem, smem, hbm, hbm
        ],
        out_specs=(vmem, vmem),
        scratch_shapes=[
            pltpu.VMEM((nout, tokens), jnp.bfloat16),
            pltpu.VMEM((nout, model_width), jnp.bfloat16),
            pltpu.VMEM((rank, hidden_units), jnp.bfloat16),
            pltpu.VMEM((rank, model_width), jnp.bfloat16),
            pltpu.VMEM((rank, width_in), f32),
            pltpu.VMEM((rank, width_out), f32),
            pltpu.VMEM((n, tokens, width_in), jnp.bfloat16),
            pltpu.VMEM((nout, nout), f32),
            pltpu.VMEM((rank, nout), f32),
            pltpu.VMEM((nout, rank), f32),
            pltpu.VMEM((rank, nout), f32),
            pltpu.VMEM((1, tokens), f32),
            pltpu.VMEM((1, tokens), f32),
            pltpu.VMEM((tokens, rank), f32),
            pltpu.VMEM((rank, tokens), jnp.bfloat16),
            pltpu.VMEM((rank, rank), f32),
            pltpu.VMEM((rank, tokens), f32),
            pltpu.VMEM((ITERS, n, 2, half, width_in), f32),
            pltpu.VMEM((ITERS, 2, half_n, 2, half, width_in), f32),
            pltpu.VMEM((ITERS - 1, n, 2, half, width_in), f32),
            pltpu.VMEM((2, half, width_in), f32),
            pltpu.VMEM((ITERS, 2, half, 128), f32),
            pltpu.VMEM((ITERS, 2, BLOCK - 1, half, 128), f32),
            pltpu.VMEM((2, n, 1, 128), f32),
            pltpu.VMEM((rank, 1, width + 256), f32),
            pltpu.VMEM((clients, 1, width + 256), f32),
            pltpu.VMEM((rank, 1, width), f32),
            dma((6,)),
            dma((n,)),
            dma((ITERS, 2, half_n)),
            dma((ITERS, 2, half_n)),
            dma((ITERS - 1, 2, half_n)),
            dma((ITERS - 1, 2, half_n)),
            dma((ITERS, 2, BLOCK - 1)),
            dma((ITERS, 2, BLOCK - 1)),
            dma((2, n)),
            dma((2, n)),
            dma((chips, CORES)),
            dma((chips, CORES)),
            dma((chips,)),
            dma((chips,)),
        ],
        compiler_params=pltpu.CompilerParams(
            collective_id=0, has_side_effects=True, vmem_limit_bytes=VMEM_BYTES
        ),
    )(
        hidden,
        frozen_residual[0].T,
        head[0],
        global_input_factor,
        global_output_factor,
        counts,
        weights,
        input_privacy_noise,
        output_privacy_noise,
    )


def solution(mesh):
    in_specs = (
        P("client", "dp", None),
        P("client", "dp", None),
        P("client", None, None),
        P(),
        P(),
        P("client", "dp"),
        P("client"),
        P(None, "dp"),
        P(None, "dp"),
    )
    out_specs = (P(None, "dp"), P(None, "dp"))
    body = functools.partial(on_device, mesh.shape["dp"], mesh.shape["client"])
    return jax.shard_map(
        body, mesh=mesh, in_specs=in_specs, out_specs=out_specs, check_vma=False
    )
```

```python
import functools
import math

import jax
import jax.numpy as jnp
from jax import lax
from jax.experimental import pallas as pl
from jax.experimental.pallas import tpu as pltpu
from jax.sharding import PartitionSpec as P

ITERS = 3
CORES = 2

learn_rate = 0.1
clip_bound = 0.001
noise_mult = 0.1

MESH = pl.DeviceIdType.MESH
HIGH = lax.Precision.HIGHEST
NN = (((1,), (0,)), ((), ()))
NT = (((1,), (1,)), ((), ()))
TN = (((0,), (0,)), ((), ()))


def mm(a, b, dims=NN, precision=None):
    return lax.dot_general(
        a, b, dims, precision=precision, preferred_element_type=jnp.float32
    )


def kernel(
    n,
    clients,
    out_scale,
    hid_ref,
    res_hbm,
    head_hbm,
    a0_hbm,
    b0_hbm,
    cnt_ref,
    w_ref,
    nin_hbm,
    nout_hbm,
    oin_ref,
    oout_ref,
    res_ref,
    head_ref,
    a0_ref,
    b0_ref,
    nin_ref,
    nout_ref,
    hv,
    gram,
    mixed,
    mixed_t,
    inner_sum,
    mask,
    tokens_live,
    proj,
    dproj,
    square,
    base_in,
    grad,
    slot,
    a_all,
    own,
    part,
    spread,
    row_out,
    row_in,
    row_done,
    op_sem,
    hid_sem,
    rs_send,
    rs_recv,
    ag_send,
    ag_recv,
    pt_send,
    pt_recv,
    sc_send,
    sc_recv,
    ro_send,
    ro_recv,
    rd_send,
    rd_recv,
):
    half_n = n // 2
    stops = half_n // 2
    chips = clients // CORES
    rank, width_in = nin_ref.shape
    width_out = nout_ref.shape[1]
    half = rank // 2
    nout = head_ref.shape[0]
    tokens = hv.shape[1]
    width = width_in + width_out

    z = lax.axis_index("dp")
    client = lax.axis_index("client")
    chip = lax.div(client, CORES)
    core = lax.rem(client, CORES)
    ring = (
        (lax.rem(z + n - 2, n), lax.rem(z + 2, n)),
        (lax.rem(z + n - 1, n), lax.rem(z + 1, n)),
    )

    def at_z(k):
        return lax.rem(z + k, n)

    def at_chip(k):
        return lax.rem(chip + k, chips)

    def load(j):
        return pltpu.make_async_copy(
            hid_ref.at[0, :, pl.ds(j * width_in, width_in)], hv.at[j], hid_sem.at[j]
        )

    pieces = [
        pltpu.make_async_copy(src, dst, op_sem.at[i])
        for i, (src, dst) in enumerate(
            [
                (head_hbm, head_ref),
                (b0_hbm, b0_ref),
                (res_hbm, res_ref),
                (a0_hbm, a0_ref),
                (nin_hbm, nin_ref),
                (nout_hbm, nout_ref),
            ]
        )
    ]
    for piece in pieces[:4]:
        piece.start()
    for j in range(n):
        load(j).start()
    for piece in pieces[4:]:
        piece.start()

    barrier = pltpu.get_barrier_semaphore()
    for k in range(1, n):
        pl.semaphore_signal(barrier, inc=1, device_id={"dp": at_z(k)}, device_id_type=MESH)
    for k in range(1, clients):
        pl.semaphore_signal(
            barrier, inc=1, device_id={"client": lax.rem(client + k, clients)}, device_id_type=MESH
        )

    for piece in pieces[:3]:
        piece.wait()
    head = head_ref[...]
    gram[...] = mm(head, head, NT)
    mixed[...] = mm(b0_ref[...], head, NT)
    mixed_t[...] = mm(head, b0_ref[...], NT)
    inner_sum[...] = jnp.zeros_like(inner_sum)

    def from_mixed():
        square[...] = mm(mixed[...], mixed[...], NT, HIGH)
        base_in[...] = mm(mixed[...], res_ref[...].astype(jnp.float32), NN, HIGH)

    from_mixed()
    lane = lax.broadcasted_iota(jnp.int32, (1, tokens), 1)
    live = cnt_ref[0, 0]

    pl.semaphore_wait(barrier, (n - 1) + (clients - 1))

    def z_copy(which, k):
        return pltpu.make_async_remote_copy(
            src_ref=spread.at[which, z],
            dst_ref=spread.at[which, z],
            send_sem=sc_send.at[which, k],
            recv_sem=sc_recv.at[which, k],
            device_id={"dp": at_z(k)},
            device_id_type=MESH,
        )

    def z_start(which, row):
        spread[which, z] = row
        for k in range(1, n):
            z_copy(which, k).start()

    def z_finish(which):
        for k in range(1, n):
            z_copy(which, k).wait()
        total = spread[which, 0]
        for j in range(1, n):
            total = total + spread[which, j]
        return total

    z_start(0, jnp.full((1, 128), live.astype(jnp.float32), jnp.float32))

    pieces[3].wait()
    proj[...] = jnp.zeros_like(proj)

    def first(j, _):
        load(j).wait()
        cols = pl.ds(pl.multiple_of(j * width_in, 128), width_in)
        proj[...] += mm(hv[j], a0_ref[:, cols], NT)
        return 0

    lax.fori_loop(0, n, first, 0)

    start_cols = pl.ds(pl.multiple_of(z * width_in, 128), width_in)
    own_zero = a0_ref[:, start_cols].astype(jnp.float32)
    for h in range(2):
        own[h] = own_zero[h * half : (h + 1) * half]
    mask[...] = (lane < live).astype(jnp.float32)
    tokens_live[...] = z_finish(0)

    cut = width_in // 256 * 128 + 128
    pieces_of = [(h, pl.ds(at, size)) for h in range(2) for at, size in ((0, cut), (cut, width_in - cut))]

    def piece_of(ref, p):
        h, cols = pieces_of[p]
        return ref.at[h, :, cols]

    def rs_copy(it, way, p, odd, e, owner):
        return pltpu.make_async_remote_copy(
            src_ref=piece_of(grad.at[it, owner], p),
            dst_ref=piece_of(slot.at[it, way, odd, e], p),
            send_sem=rs_send.at[it, way, p, odd, e],
            recv_sem=rs_recv.at[it, way, p, odd, e],
            device_id={"dp": ring[odd][way]},
            device_id_type=MESH,
        )

    def ag_copy(it, way, p, odd, t, owner):
        return pltpu.make_async_remote_copy(
            src_ref=piece_of(a_all.at[it, owner], p),
            dst_ref=piece_of(a_all.at[it, owner], p),
            send_sem=ag_send.at[it, way, p, odd, t],
            recv_sem=ag_recv.at[it, way, p, odd, t],
            device_id={"dp": ring[odd][way]},
            device_id_type=MESH,
        )

    def pt_copy(it, way, odd, t, owner):
        return pltpu.make_async_remote_copy(
            src_ref=part.at[it, owner],
            dst_ref=part.at[it, owner],
            send_sem=pt_send.at[it, way, odd, t],
            recv_sem=pt_recv.at[it, way, odd, t],
            device_id={"dp": ring[odd][way]},
            device_id_type=MESH,
        )

    def long(way, p):
        return way == pieces_of[p][0]

    def own_pieces(way):
        return [p for p in range(4) if long(way, p)]

    far = at_z(half_n)

    def local_step(it, _):
        weighted = mask[...] / tokens_live[...]
        through = mm(square[...], proj[...], NT, HIGH)
        dproj[...] = ((base_in[...] + through) * weighted).astype(jnp.bfloat16)

        def local(owner):
            value = mm(dproj[...], hv[owner])
            for h in range(2):
                grad[it, owner, h] = value[h * half : (h + 1) * half]

        def beside(k):
            return at_z(n - k), at_z(k)

        def local_both(k):
            for owner in beside(k):
                local(owner)

        def send_odd(e):
            owners = beside(half_n - 1 - 2 * e)
            for p in range(4):
                for way in range(2):
                    rs_copy(it, way, p, 1, e, owners[way]).start()

        local(far)
        for way in range(2):
            for p in own_pieces(way):
                rs_copy(it, way, p, 0, 0, far).start()
        local_both(half_n - 1)
        send_odd(0)
        local_both(half_n - 2)
        local_both(half_n - 3)
        send_odd(1)

        proj_t = proj[...].T
        resid = res_ref[...].astype(jnp.float32) + mm(mixed_t[...], proj_t, NN, HIGH)
        inner = mm(proj_t, resid * weighted, NT, HIGH)
        part[it, z] = jnp.concatenate([inner[:half], inner[half:]], axis=1)
        for odd in range(2):
            for way in range(2):
                pt_copy(it, way, odd, 0, z).start()

        for e in range(1, stops):
            owners = beside(half_n - 2 * e)
            for p, (h, cols) in enumerate(pieces_of):
                for way in range(2):
                    rs_copy(it, way, p, 1, e - 1, owners[way]).wait_recv()
                    total = grad[it, owners[way], h, :, cols] + slot[it, way, 1, e - 1, h, :, cols]
                    if long(way, p) or e > 1:
                        rs_copy(it, way, p, 0, e - 1, owners[way]).wait_recv()
                        total = total + slot[it, way, 0, e - 1, h, :, cols]
                    grad[it, owners[way], h, :, cols] = total
                    rs_copy(it, way, p, 0, e, owners[way]).start()
            if e < stops - 1:
                local_both(half_n - 2 * e - 2)
                local_both(half_n - 2 * e - 3)
                send_odd(e + 1)
            else:
                local(z)
            for way in range(2):
                source = at_z(2 * e) if way == 0 else at_z(n - 2 * e)
                pt_copy(it, way, 0, e - 1, source).wait_recv()
                if way == 0 or e < stops - 1:
                    pt_copy(it, way, 0, e, source).start()
                pt_copy(it, way, 1, e, source).start()
                pt_copy(it, way, 1, e - 1, source).wait_recv()
        for p, (h, cols) in enumerate(pieces_of):
            total = grad[it, z, h, :, cols]
            for odd in (1, 0):
                for way in range(2):
                    rs_copy(it, way, p, odd, stops - 1, z).wait_recv()
                    total = total + slot[it, way, odd, stops - 1, h, :, cols]
            own[h, :, cols] = own[h, :, cols] - learn_rate * total

            @pl.when(it < ITERS - 1)
            def _():
                a_all[it, z, h, :, cols] = own[h, :, cols]
                for way in range(2):
                    ag_copy(it, way, p, 0, 0, z).start()

        def inner_total():
            pt_copy(it, 0, 0, stops - 1, far).wait_recv()
            for way in range(2):
                pt_copy(it, way, 1, stops - 1, far).wait_recv()
            tile = part[it, 0]
            for j in range(1, n):
                tile = tile + part[it, j]
            return jnp.concatenate([tile[:, :nout], tile[:, nout:]], axis=0)

        @pl.when(it == ITERS - 1)
        def _():
            inner_sum[...] += inner_total()

        @pl.when(it < ITERS - 1)
        def _():
            def project(owner):
                rows = jnp.concatenate([a_all[it, owner, 0], a_all[it, owner, 1]], axis=0)
                return mm(hv[owner], rows.astype(jnp.bfloat16), NT)

            def send_between(t, sources):
                for p in range(4):
                    for way in range(2):
                        ag_copy(it, way, p, 1, t, sources[way]).start()

            def use_between(t):
                owners = (at_z(2 * t + 1), at_z(n - 2 * t - 1))
                for way in range(2):
                    for p in range(4):
                        ag_copy(it, way, p, 1, t, owners[way]).wait_recv()
                    proj[...] += project(owners[way])

            send_between(0, (z, z))
            proj[...] = project(z)

            for t in range(1, stops):
                sources = (at_z(2 * t), at_z(n - 2 * t))
                for p in range(4):
                    for way in range(2):
                        ag_copy(it, way, p, 0, t - 1, sources[way]).wait_recv()
                        if long(way, p) or t < stops - 1:
                            ag_copy(it, way, p, 0, t, sources[way]).start()
                if t == stops - 1:
                    send_between(t, sources)
                proj[...] += project(sources[0])
                if t < stops - 1:
                    send_between(t, sources)
                proj[...] += project(sources[1])
                use_between(t - 1)
                if t == 1:
                    step_inner = inner_total()
                    inner_sum[...] += step_inner
                if t == 2:
                    mixed[...] = mixed[...] - learn_rate * mm(step_inner, gram[...], NN, HIGH)
                    mixed_t[...] = mixed_t[...] - learn_rate * mm(gram[...], step_inner, NT, HIGH)
                if t == stops - 1:
                    from_mixed()
            for way in range(2):
                for p in own_pieces(way):
                    ag_copy(it, way, p, 0, stops - 1, far).wait_recv()
            proj[...] += project(far)
            use_between(stops - 1)

        return 0

    lax.fori_loop(0, ITERS, local_step, 0)

    own_three = jnp.concatenate([own[0], own[1]], axis=0)
    delta_in = own_three - own_zero
    out_cols = pl.ds(pl.multiple_of(z * width_out, 128), width_out)
    head_cols = head_ref[:, out_cols].astype(jnp.float32)
    delta_out = -learn_rate * mm(inner_sum[...], head_cols, NN, HIGH)
    delta = jnp.concatenate([delta_in, delta_out], axis=1)
    sums = jnp.sum(delta * delta, axis=0, keepdims=True)
    lanes = sums[:, :128]
    for j in range(1, width // 128):
        lanes = lanes + sums[:, j * 128 : (j + 1) * 128]
    squares = jnp.sum(lanes, axis=1, keepdims=True)
    weight = w_ref[0].astype(jnp.float32)

    mine = lax.broadcasted_iota(jnp.int32, (1, 128), 1) == client
    ends = jnp.concatenate(
        [jnp.where(mine, squares, 0.0), jnp.where(mine, weight, 0.0)], axis=1
    )
    for r in range(rank):
        row_out[r] = jnp.concatenate([delta[r : r + 1], ends], axis=1)

    def ro_copy(k, to_core, from_core):
        return pltpu.make_async_remote_copy(
            src_ref=row_out.at[at_chip(k)],
            dst_ref=row_in.at[client],
            send_sem=ro_send.at[k, to_core],
            recv_sem=ro_recv.at[k, from_core],
            device_id={"client": at_chip(k) * CORES + to_core},
            device_id_type=MESH,
        )

    for k in range(1, chips):
        for to_core in range(CORES):
            ro_copy(k, to_core, core).start()
    ro_copy(0, 1 - core, core).start()
    row_in[client] = row_out[chip]
    for k in range(1, chips):
        for from_core in range(CORES):
            ro_copy(k, from_core, from_core).wait_recv()
    ro_copy(0, 1 - core, 1 - core).wait_recv()
    ends = row_in[0][:, width:]
    for c in range(1, clients):
        ends = ends + row_in[c][:, width:]

    z_start(1, ends[:, :128])
    for piece in pieces[4:]:
        piece.wait()
    noise = jnp.concatenate(
        [nin_ref[pl.ds(chip, 1), :], nout_ref[pl.ds(chip, 1), :]], axis=1
    )
    weights = ends[:, 128:]
    wsum = jnp.sum(weights, axis=1, keepdims=True)
    scales = weights * jnp.minimum(1.0, clip_bound / jnp.sqrt(z_finish(1) + 1e-06))
    row = scales[:, :1] * row_in[0][:, :width]
    for c in range(1, clients):
        row = row + scales[:, c : c + 1] * row_in[c][:, :width]
    row_done[chip] = (row + noise_mult * clip_bound * noise) * out_scale / wsum

    def rd_copy(k):
        return pltpu.make_async_remote_copy(
            src_ref=row_done.at[chip],
            dst_ref=row_done.at[chip],
            send_sem=rd_send.at[k],
            recv_sem=rd_recv.at[k],
            device_id={"client": at_chip(k) * CORES + core},
            device_id_type=MESH,
        )

    for k in range(1, chips):
        rd_copy(k).start()

    def drain_step(it, _):
        for way in range(2):
            for e in range(stops):
                for p in range(4):
                    if long(way, p) or e > 0:
                        rs_copy(it, way, p, 0, e, z).wait_send()
                    rs_copy(it, way, p, 1, e, z).wait_send()
                if way == 0 or e < stops - 1:
                    pt_copy(it, way, 0, e, z).wait_send()
                pt_copy(it, way, 1, e, z).wait_send()

            @pl.when(it < ITERS - 1)
            def _():
                for e in range(stops):
                    for p in range(4):
                        if long(way, p) or e < stops - 1:
                            ag_copy(it, way, p, 0, e, z).wait_send()
                        ag_copy(it, way, p, 1, e, z).wait_send()

        return 0

    lax.fori_loop(0, ITERS, drain_step, 0)

    for k in range(1, chips):
        for to_core in range(CORES):
            ro_copy(k, to_core, core).wait_send()
    ro_copy(0, 1 - core, core).wait_send()
    for k in range(1, chips):
        rd_copy(k).wait()
    for r in range(rank):
        row = row_done[r]
        oin_ref[r : r + 1, :] = row[:, :width_in]
        oout_ref[r : r + 1, :] = row[:, width_in:]


def on_device(
    n,
    clients,
    hidden,
    frozen_residual,
    head,
    global_input_factor,
    global_output_factor,
    counts,
    weights,
    input_privacy_noise,
    output_privacy_noise,
):
    tokens, hidden_units = hidden.shape[1:]
    nout = head.shape[1]
    rank, model_width = global_output_factor.shape
    width_in = input_privacy_noise.shape[1]
    width_out = output_privacy_noise.shape[1]
    half = rank // 2
    stops = n // 4
    chips = clients // CORES
    width = width_in + width_out
    out_scale = math.sqrt(rank * (hidden_units + model_width)) / clip_bound
    f32 = jnp.float32
    dma = pltpu.SemaphoreType.DMA
    hbm = pl.BlockSpec(memory_space=pltpu.HBM)
    vmem = pl.BlockSpec(memory_space=pltpu.VMEM)
    smem = pl.BlockSpec(memory_space=pltpu.SMEM)
    return pl.pallas_call(
        functools.partial(kernel, n, clients, out_scale),
        out_shape=(
            jax.ShapeDtypeStruct((rank, width_in), f32),
            jax.ShapeDtypeStruct((rank, width_out), f32),
        ),
        in_specs=[
            hbm, hbm, hbm, hbm, hbm, smem, smem, hbm, hbm
        ],
        out_specs=(vmem, vmem),
        scratch_shapes=[
            pltpu.VMEM((nout, tokens), jnp.bfloat16),
            pltpu.VMEM((nout, model_width), jnp.bfloat16),
            pltpu.VMEM((rank, hidden_units), jnp.bfloat16),
            pltpu.VMEM((rank, model_width), jnp.bfloat16),
            pltpu.VMEM((rank, width_in), f32),
            pltpu.VMEM((rank, width_out), f32),
            pltpu.VMEM((n, tokens, width_in), jnp.bfloat16),
            pltpu.VMEM((nout, nout), f32),
            pltpu.VMEM((rank, nout), f32),
            pltpu.VMEM((nout, rank), f32),
            pltpu.VMEM((rank, nout), f32),
            pltpu.VMEM((1, tokens), f32),
            pltpu.VMEM((1, tokens), f32),
            pltpu.VMEM((tokens, rank), f32),
            pltpu.VMEM((rank, tokens), jnp.bfloat16),
            pltpu.VMEM((rank, rank), f32),
            pltpu.VMEM((rank, tokens), f32),
            pltpu.VMEM((ITERS, n, 2, half, width_in), f32),
            pltpu.VMEM((ITERS, 2, 2, stops, 2, half, width_in), f32),
            pltpu.VMEM((ITERS - 1, n, 2, half, width_in), f32),
            pltpu.VMEM((2, half, width_in), f32),
            pltpu.VMEM((ITERS, n, half, 128), f32),
            pltpu.VMEM((2, n, 1, 128), f32),
            pltpu.VMEM((rank, 1, width + 256), f32),
            pltpu.VMEM((clients, 1, width + 256), f32),
            pltpu.VMEM((rank, 1, width), f32),
            dma((6,)),
            dma((n,)),
            dma((ITERS, 2, 4, 2, stops)),
            dma((ITERS, 2, 4, 2, stops)),
            dma((ITERS - 1, 2, 4, 2, stops)),
            dma((ITERS - 1, 2, 4, 2, stops)),
            dma((ITERS, 2, 2, stops)),
            dma((ITERS, 2, 2, stops)),
            dma((2, n)),
            dma((2, n)),
            dma((chips, CORES)),
            dma((chips, CORES)),
            dma((chips,)),
            dma((chips,)),
        ],
        compiler_params=pltpu.CompilerParams(
            collective_id=0, has_side_effects=True, vmem_limit_bytes=63 * 1024 * 1024
        ),
    )(
        hidden,
        frozen_residual[0].T,
        head[0],
        global_input_factor,
        global_output_factor,
        counts,
        weights,
        input_privacy_noise,
        output_privacy_noise,
    )


def solution(mesh):
    in_specs = (
        P("client", "dp", None),
        P("client", "dp", None),
        P("client", None, None),
        P(),
        P(),
        P("client", "dp"),
        P("client"),
        P(None, "dp"),
        P(None, "dp"),
    )
    out_specs = (P(None, "dp"), P(None, "dp"))
    body = functools.partial(on_device, mesh.shape["dp"], mesh.shape["client"])
    return jax.shard_map(
        body, mesh=mesh, in_specs=in_specs, out_specs=out_specs, check_vma=False
    )
```

```python
import functools
import math

import jax
import jax.numpy as jnp
from jax import lax
from jax.experimental import pallas as pl
from jax.experimental.pallas import tpu as pltpu
from jax.sharding import PartitionSpec as P

ITERS = 3
CORES = 2

learn_rate = 0.1
clip_bound = 0.001
noise_mult = 0.1

MESH = pl.DeviceIdType.MESH
HIGH = lax.Precision.HIGHEST
NN = (((1,), (0,)), ((), ()))
NT = (((1,), (1,)), ((), ()))
TN = (((0,), (0,)), ((), ()))


def mm(a, b, dims=NN, precision=None):
    return lax.dot_general(
        a, b, dims, precision=precision, preferred_element_type=jnp.float32
    )


def kernel(
    n,
    clients,
    out_scale,
    hid_ref,
    res_hbm,
    head_hbm,
    a0_hbm,
    b0_hbm,
    cnt_ref,
    w_ref,
    nin_hbm,
    nout_hbm,
    oin_ref,
    oout_ref,
    res_ref,
    head_ref,
    a0_ref,
    b0_ref,
    nin_ref,
    nout_ref,
    hv,
    gram,
    mixed,
    mixed_t,
    inner_sum,
    mask,
    tokens_live,
    proj,
    dproj,
    square,
    base_in,
    grad,
    slot,
    a_all,
    own,
    part,
    spread,
    row_out,
    row_in,
    row_done,
    op_sem,
    hid_sem,
    rs_send,
    rs_recv,
    ag_send,
    ag_recv,
    pt_send,
    pt_recv,
    sc_send,
    sc_recv,
    ro_send,
    ro_recv,
    rd_send,
    rd_recv,
):
    half_n = n // 2
    stops = half_n // 2
    chips = clients // CORES
    rank, width_in = nin_ref.shape
    width_out = nout_ref.shape[1]
    half = rank // 2
    nout = head_ref.shape[0]
    tokens = hv.shape[1]
    width = width_in + width_out

    z = lax.axis_index("dp")
    client = lax.axis_index("client")
    chip = lax.div(client, CORES)
    core = lax.rem(client, CORES)
    ring = (
        (lax.rem(z + n - 2, n), lax.rem(z + 2, n)),
        (lax.rem(z + n - 1, n), lax.rem(z + 1, n)),
    )

    def at_z(k):
        return lax.rem(z + k, n)

    def at_chip(k):
        return lax.rem(chip + k, chips)

    def load(j):
        return pltpu.make_async_copy(
            hid_ref.at[0, :, pl.ds(j * width_in, width_in)], hv.at[j], hid_sem.at[j]
        )

    pieces = [
        pltpu.make_async_copy(src, dst, op_sem.at[i])
        for i, (src, dst) in enumerate(
            [
                (head_hbm, head_ref),
                (b0_hbm, b0_ref),
                (res_hbm, res_ref),
                (a0_hbm, a0_ref),
                (nin_hbm, nin_ref),
                (nout_hbm, nout_ref),
            ]
        )
    ]
    for piece in pieces[:4]:
        piece.start()
    for j in range(n):
        load(j).start()
    for piece in pieces[4:]:
        piece.start()

    barrier = pltpu.get_barrier_semaphore()
    for k in range(1, n):
        pl.semaphore_signal(barrier, inc=1, device_id={"dp": at_z(k)}, device_id_type=MESH)
    for k in range(1, clients):
        pl.semaphore_signal(
            barrier, inc=1, device_id={"client": lax.rem(client + k, clients)}, device_id_type=MESH
        )

    for piece in pieces[:3]:
        piece.wait()
    head = head_ref[...]
    gram[...] = mm(head, head, NT)
    mixed[...] = mm(b0_ref[...], head, NT)
    mixed_t[...] = mm(head, b0_ref[...], NT)
    inner_sum[...] = jnp.zeros_like(inner_sum)

    def from_mixed():
        square[...] = mm(mixed[...], mixed[...], NT, HIGH)
        base_in[...] = mm(mixed[...], res_ref[...].astype(jnp.float32), NN, HIGH)

    from_mixed()
    lane = lax.broadcasted_iota(jnp.int32, (1, tokens), 1)
    live = cnt_ref[0, 0]

    pl.semaphore_wait(barrier, (n - 1) + (clients - 1))

    def z_copy(which, k):
        return pltpu.make_async_remote_copy(
            src_ref=spread.at[which, z],
            dst_ref=spread.at[which, z],
            send_sem=sc_send.at[which, k],
            recv_sem=sc_recv.at[which, k],
            device_id={"dp": at_z(k)},
            device_id_type=MESH,
        )

    def z_start(which, row):
        spread[which, z] = row
        for k in range(1, n):
            z_copy(which, k).start()

    def z_finish(which):
        for k in range(1, n):
            z_copy(which, k).wait()
        total = spread[which, 0]
        for j in range(1, n):
            total = total + spread[which, j]
        return total

    z_start(0, jnp.full((1, 128), live.astype(jnp.float32), jnp.float32))

    pieces[3].wait()
    proj[...] = jnp.zeros_like(proj)

    def first(j, _):
        load(j).wait()
        cols = pl.ds(pl.multiple_of(j * width_in, 128), width_in)
        proj[...] += mm(hv[j], a0_ref[:, cols], NT)
        return 0

    lax.fori_loop(0, n, first, 0)

    start_cols = pl.ds(pl.multiple_of(z * width_in, 128), width_in)
    own_zero = a0_ref[:, start_cols].astype(jnp.float32)
    for h in range(2):
        own[h] = own_zero[h * half : (h + 1) * half]
    mask[...] = (lane < live).astype(jnp.float32)
    tokens_live[...] = z_finish(0)

    cut = width_in // 256 * 128 + 128
    pieces_of = [(h, pl.ds(at, size)) for h in range(2) for at, size in ((0, cut), (cut, width_in - cut))]

    def piece_of(ref, odd, p):
        if odd:
            return ref.at[p]
        h, cols = pieces_of[p]
        return ref.at[h, :, cols]

    def rs_copy(it, way, p, odd, e, owner):
        return pltpu.make_async_remote_copy(
            src_ref=piece_of(grad.at[it, owner], odd, p),
            dst_ref=piece_of(slot.at[it, way, odd, e], odd, p),
            send_sem=rs_send.at[it, way, p, odd, e],
            recv_sem=rs_recv.at[it, way, p, odd, e],
            device_id={"dp": ring[odd][way]},
            device_id_type=MESH,
        )

    def ag_copy(it, way, p, odd, t, owner):
        return pltpu.make_async_remote_copy(
            src_ref=piece_of(a_all.at[it, owner], odd, p),
            dst_ref=piece_of(a_all.at[it, owner], odd, p),
            send_sem=ag_send.at[it, way, p, odd, t],
            recv_sem=ag_recv.at[it, way, p, odd, t],
            device_id={"dp": ring[odd][way]},
            device_id_type=MESH,
        )

    def pt_copy(it, way, odd, t, owner):
        return pltpu.make_async_remote_copy(
            src_ref=part.at[it, owner],
            dst_ref=part.at[it, owner],
            send_sem=pt_send.at[it, way, odd, t],
            recv_sem=pt_recv.at[it, way, odd, t],
            device_id={"dp": ring[odd][way]},
            device_id_type=MESH,
        )

    def long(way, p):
        return way == pieces_of[p][0]

    def own_pieces(way):
        return [p for p in range(4) if long(way, p)]

    far = at_z(half_n)

    def local_step(it, _):
        weighted = mask[...] / tokens_live[...]
        through = mm(square[...], proj[...], NT, HIGH)
        dproj[...] = ((base_in[...] + through) * weighted).astype(jnp.bfloat16)

        def local(owner):
            value = mm(dproj[...], hv[owner])
            for h in range(2):
                grad[it, owner, h] = value[h * half : (h + 1) * half]

        def beside(k):
            return at_z(n - k), at_z(k)

        def local_both(k):
            for owner in beside(k):
                local(owner)

        def send_odd(e):
            owners = beside(half_n - 1 - 2 * e)
            for h in range(2):
                for way in range(2):
                    rs_copy(it, way, h, 1, e, owners[way]).start()

        local(far)
        for way in range(2):
            for p in own_pieces(way):
                rs_copy(it, way, p, 0, 0, far).start()
        local_both(half_n - 1)
        send_odd(0)
        local_both(half_n - 2)
        local_both(half_n - 3)
        send_odd(1)

        proj_t = proj[...].T
        resid = res_ref[...].astype(jnp.float32) + mm(mixed_t[...], proj_t, NN, HIGH)
        inner = mm(proj_t, resid * weighted, NT, HIGH)
        part[it, z] = jnp.concatenate([inner[:half], inner[half:]], axis=1)
        for odd in range(2):
            for way in range(2):
                pt_copy(it, way, odd, 0, z).start()

        for e in range(1, stops):
            owners = beside(half_n - 2 * e)
            for p, (h, cols) in enumerate(pieces_of):
                for way in range(2):
                    if p % 2 == 0:
                        rs_copy(it, way, h, 1, e - 1, owners[way]).wait_recv()
                    total = grad[it, owners[way], h, :, cols] + slot[it, way, 1, e - 1, h, :, cols]
                    if long(way, p) or e > 1:
                        rs_copy(it, way, p, 0, e - 1, owners[way]).wait_recv()
                        total = total + slot[it, way, 0, e - 1, h, :, cols]
                    grad[it, owners[way], h, :, cols] = total
                    rs_copy(it, way, p, 0, e, owners[way]).start()
            if e < stops - 1:
                local_both(half_n - 2 * e - 2)
                local_both(half_n - 2 * e - 3)
                send_odd(e + 1)
            else:
                local(z)
            for way in range(2):
                source = at_z(2 * e) if way == 0 else at_z(n - 2 * e)
                pt_copy(it, way, 0, e - 1, source).wait_recv()
                if way == 0 or e < stops - 1:
                    pt_copy(it, way, 0, e, source).start()
                pt_copy(it, way, 1, e, source).start()
                pt_copy(it, way, 1, e - 1, source).wait_recv()
        for p, (h, cols) in enumerate(pieces_of):
            total = grad[it, z, h, :, cols]
            for odd in (1, 0):
                for way in range(2):
                    if not odd:
                        rs_copy(it, way, p, 0, stops - 1, z).wait_recv()
                    elif p % 2 == 0:
                        rs_copy(it, way, h, 1, stops - 1, z).wait_recv()
                    total = total + slot[it, way, odd, stops - 1, h, :, cols]
            own[h, :, cols] = own[h, :, cols] - learn_rate * total

            @pl.when(it < ITERS - 1)
            def _():
                a_all[it, z, h, :, cols] = own[h, :, cols]
                for way in range(2):
                    ag_copy(it, way, p, 0, 0, z).start()

        def inner_total():
            pt_copy(it, 0, 0, stops - 1, far).wait_recv()
            for way in range(2):
                pt_copy(it, way, 1, stops - 1, far).wait_recv()
            tile = part[it, 0]
            for j in range(1, n):
                tile = tile + part[it, j]
            return jnp.concatenate([tile[:, :nout], tile[:, nout:]], axis=0)

        @pl.when(it == ITERS - 1)
        def _():
            inner_sum[...] += inner_total()

        @pl.when(it < ITERS - 1)
        def _():
            def project(owner):
                rows = jnp.concatenate([a_all[it, owner, 0], a_all[it, owner, 1]], axis=0)
                return mm(hv[owner], rows.astype(jnp.bfloat16), NT)

            def send_between(t, sources):
                for h in range(2):
                    for way in range(2):
                        ag_copy(it, way, h, 1, t, sources[way]).start()

            def use_between(t):
                owners = (at_z(2 * t + 1), at_z(n - 2 * t - 1))
                for way in range(2):
                    for h in range(2):
                        ag_copy(it, way, h, 1, t, owners[way]).wait_recv()
                    proj[...] += project(owners[way])

            send_between(0, (z, z))
            proj[...] = project(z)

            for t in range(1, stops):
                sources = (at_z(2 * t), at_z(n - 2 * t))
                for p in range(4):
                    for way in range(2):
                        ag_copy(it, way, p, 0, t - 1, sources[way]).wait_recv()
                        if long(way, p) or t < stops - 1:
                            ag_copy(it, way, p, 0, t, sources[way]).start()
                if t == stops - 1:
                    send_between(t, sources)
                proj[...] += project(sources[0])
                if t < stops - 1:
                    send_between(t, sources)
                proj[...] += project(sources[1])
                use_between(t - 1)
                if t == 1:
                    step_inner = inner_total()
                    inner_sum[...] += step_inner
                if t == 2:
                    mixed[...] = mixed[...] - learn_rate * mm(step_inner, gram[...], NN, HIGH)
                    mixed_t[...] = mixed_t[...] - learn_rate * mm(gram[...], step_inner, NT, HIGH)
                if t == stops - 1:
                    from_mixed()
            for way in range(2):
                for p in own_pieces(way):
                    ag_copy(it, way, p, 0, stops - 1, far).wait_recv()
            proj[...] += project(far)
            use_between(stops - 1)

        return 0

    lax.fori_loop(0, ITERS, local_step, 0)

    own_three = jnp.concatenate([own[0], own[1]], axis=0)
    delta_in = own_three - own_zero
    out_cols = pl.ds(pl.multiple_of(z * width_out, 128), width_out)
    head_cols = head_ref[:, out_cols].astype(jnp.float32)
    delta_out = -learn_rate * mm(inner_sum[...], head_cols, NN, HIGH)
    delta = jnp.concatenate([delta_in, delta_out], axis=1)
    sums = jnp.sum(delta * delta, axis=0, keepdims=True)
    lanes = sums[:, :128]
    for j in range(1, width // 128):
        lanes = lanes + sums[:, j * 128 : (j + 1) * 128]
    squares = jnp.sum(lanes, axis=1, keepdims=True)
    weight = w_ref[0].astype(jnp.float32)

    mine = lax.broadcasted_iota(jnp.int32, (1, 128), 1) == client
    ends = jnp.concatenate(
        [jnp.where(mine, squares, 0.0), jnp.where(mine, weight, 0.0)], axis=1
    )
    for r in range(rank):
        row_out[r] = jnp.concatenate([delta[r : r + 1], ends], axis=1)

    def ro_copy(k, to_core, from_core):
        return pltpu.make_async_remote_copy(
            src_ref=row_out.at[at_chip(k)],
            dst_ref=row_in.at[client],
            send_sem=ro_send.at[k, to_core],
            recv_sem=ro_recv.at[k, from_core],
            device_id={"client": at_chip(k) * CORES + to_core},
            device_id_type=MESH,
        )

    for k in range(1, chips):
        for to_core in range(CORES):
            ro_copy(k, to_core, core).start()
    ro_copy(0, 1 - core, core).start()
    row_in[client] = row_out[chip]
    for k in range(1, chips):
        for from_core in range(CORES):
            ro_copy(k, from_core, from_core).wait_recv()
    ro_copy(0, 1 - core, 1 - core).wait_recv()
    ends = row_in[0][:, width:]
    for c in range(1, clients):
        ends = ends + row_in[c][:, width:]

    z_start(1, ends[:, :128])
    for piece in pieces[4:]:
        piece.wait()
    noise = jnp.concatenate(
        [nin_ref[pl.ds(chip, 1), :], nout_ref[pl.ds(chip, 1), :]], axis=1
    )
    weights = ends[:, 128:]
    wsum = jnp.sum(weights, axis=1, keepdims=True)
    scales = weights * jnp.minimum(1.0, clip_bound / jnp.sqrt(z_finish(1) + 1e-06))
    row = scales[:, :1] * row_in[0][:, :width]
    for c in range(1, clients):
        row = row + scales[:, c : c + 1] * row_in[c][:, :width]
    row_done[chip] = (row + noise_mult * clip_bound * noise) * out_scale / wsum

    def rd_copy(k):
        return pltpu.make_async_remote_copy(
            src_ref=row_done.at[chip],
            dst_ref=row_done.at[chip],
            send_sem=rd_send.at[k],
            recv_sem=rd_recv.at[k],
            device_id={"client": at_chip(k) * CORES + core},
            device_id_type=MESH,
        )

    for k in range(1, chips):
        rd_copy(k).start()

    def drain_step(it, _):
        for way in range(2):
            for e in range(stops):
                for p in range(4):
                    if long(way, p) or e > 0:
                        rs_copy(it, way, p, 0, e, z).wait_send()
                    if p < 2:
                        rs_copy(it, way, p, 1, e, z).wait_send()
                if way == 0 or e < stops - 1:
                    pt_copy(it, way, 0, e, z).wait_send()
                pt_copy(it, way, 1, e, z).wait_send()

            @pl.when(it < ITERS - 1)
            def _():
                for e in range(stops):
                    for p in range(4):
                        if long(way, p) or e < stops - 1:
                            ag_copy(it, way, p, 0, e, z).wait_send()
                        if p < 2:
                            ag_copy(it, way, p, 1, e, z).wait_send()

        return 0

    lax.fori_loop(0, ITERS, drain_step, 0)

    for k in range(1, chips):
        for to_core in range(CORES):
            ro_copy(k, to_core, core).wait_send()
    ro_copy(0, 1 - core, core).wait_send()
    for k in range(1, chips):
        rd_copy(k).wait()
    for r in range(rank):
        row = row_done[r]
        oin_ref[r : r + 1, :] = row[:, :width_in]
        oout_ref[r : r + 1, :] = row[:, width_in:]


def on_device(
    n,
    clients,
    hidden,
    frozen_residual,
    head,
    global_input_factor,
    global_output_factor,
    counts,
    weights,
    input_privacy_noise,
    output_privacy_noise,
):
    tokens, hidden_units = hidden.shape[1:]
    nout = head.shape[1]
    rank, model_width = global_output_factor.shape
    width_in = input_privacy_noise.shape[1]
    width_out = output_privacy_noise.shape[1]
    half = rank // 2
    stops = n // 4
    chips = clients // CORES
    width = width_in + width_out
    out_scale = math.sqrt(rank * (hidden_units + model_width)) / clip_bound
    f32 = jnp.float32
    dma = pltpu.SemaphoreType.DMA
    hbm = pl.BlockSpec(memory_space=pltpu.HBM)
    vmem = pl.BlockSpec(memory_space=pltpu.VMEM)
    smem = pl.BlockSpec(memory_space=pltpu.SMEM)
    return pl.pallas_call(
        functools.partial(kernel, n, clients, out_scale),
        out_shape=(
            jax.ShapeDtypeStruct((rank, width_in), f32),
            jax.ShapeDtypeStruct((rank, width_out), f32),
        ),
        in_specs=[
            hbm, hbm, hbm, hbm, hbm, smem, smem, hbm, hbm
        ],
        out_specs=(vmem, vmem),
        scratch_shapes=[
            pltpu.VMEM((nout, tokens), jnp.bfloat16),
            pltpu.VMEM((nout, model_width), jnp.bfloat16),
            pltpu.VMEM((rank, hidden_units), jnp.bfloat16),
            pltpu.VMEM((rank, model_width), jnp.bfloat16),
            pltpu.VMEM((rank, width_in), f32),
            pltpu.VMEM((rank, width_out), f32),
            pltpu.VMEM((n, tokens, width_in), jnp.bfloat16),
            pltpu.VMEM((nout, nout), f32),
            pltpu.VMEM((rank, nout), f32),
            pltpu.VMEM((nout, rank), f32),
            pltpu.VMEM((rank, nout), f32),
            pltpu.VMEM((1, tokens), f32),
            pltpu.VMEM((1, tokens), f32),
            pltpu.VMEM((tokens, rank), f32),
            pltpu.VMEM((rank, tokens), jnp.bfloat16),
            pltpu.VMEM((rank, rank), f32),
            pltpu.VMEM((rank, tokens), f32),
            pltpu.VMEM((ITERS, n, 2, half, width_in), f32),
            pltpu.VMEM((ITERS, 2, 2, stops, 2, half, width_in), f32),
            pltpu.VMEM((ITERS - 1, n, 2, half, width_in), f32),
            pltpu.VMEM((2, half, width_in), f32),
            pltpu.VMEM((ITERS, n, half, 128), f32),
            pltpu.VMEM((2, n, 1, 128), f32),
            pltpu.VMEM((rank, 1, width + 256), f32),
            pltpu.VMEM((clients, 1, width + 256), f32),
            pltpu.VMEM((rank, 1, width), f32),
            dma((6,)),
            dma((n,)),
            dma((ITERS, 2, 4, 2, stops)),
            dma((ITERS, 2, 4, 2, stops)),
            dma((ITERS - 1, 2, 4, 2, stops)),
            dma((ITERS - 1, 2, 4, 2, stops)),
            dma((ITERS, 2, 2, stops)),
            dma((ITERS, 2, 2, stops)),
            dma((2, n)),
            dma((2, n)),
            dma((chips, CORES)),
            dma((chips, CORES)),
            dma((chips,)),
            dma((chips,)),
        ],
        compiler_params=pltpu.CompilerParams(
            collective_id=0, has_side_effects=True, vmem_limit_bytes=63 * 1024 * 1024
        ),
    )(
        hidden,
        frozen_residual[0].T,
        head[0],
        global_input_factor,
        global_output_factor,
        counts,
        weights,
        input_privacy_noise,
        output_privacy_noise,
    )


def solution(mesh):
    in_specs = (
        P("client", "dp", None),
        P("client", "dp", None),
        P("client", None, None),
        P(),
        P(),
        P("client", "dp"),
        P("client"),
        P(None, "dp"),
        P(None, "dp"),
    )
    out_specs = (P(None, "dp"), P(None, "dp"))
    body = functools.partial(on_device, mesh.shape["dp"], mesh.shape["client"])
    return jax.shard_map(
        body, mesh=mesh, in_specs=in_specs, out_specs=out_specs, check_vma=False
    )
```
